32 devices in a mesh: groups: 2 (over x), seq: 8 (over z, y), adapter: 2 (over core).
Axes of the slice: x: 2, y: 2, z: 4, core: 2. Of those that a mesh axis runs over, the one named last changes fastest.
Arguments:
- tokens: bfloat16 [1024, 4608], P(('groups', 'seq', 'adapter')), parts along dimension 0, may hold values from -6 to 6
- shared_up_weight: bfloat16 [4608, 36864], P(None, ('seq', 'adapter')), may hold values from -0.09375 to 0.09375
- adapter_down_factor: float32 [8, 4608, 64], P(('groups', 'adapter'), 'seq'), parts along dimension 0, may hold values from -0.09375 to 0.09375
- adapter_up_factor: float32 [8, 64, 36864], P('groups', None, ('seq', 'adapter')), parts along dimension 0, may hold values from -0.375 to 0.375
- adapter_per_block: int32 [8, 1], P('groups'), parts along dimension 0, may hold values from 0 to 3
- rows_per_block: int32 [8], P('groups'), parts along dimension 0, may hold values from 32 to 128, as said below
Outputs:
- hidden: bfloat16 [1024, 36864], P('groups', ('seq', 'adapter')), parts along dimension 0
The draws below stay inside these ranges and needn't reach their ends.
There are 2 independent parts, one for each index of `groups`. The reference program is written for one: setup_inputs(seed, part) draws one part's arguments, and reference() takes and returns one part's arrays. A program takes and returns all parts, laid end to end along the dimension named above; an argument that names none is the same for every part. Nothing has to cross between parts.
Inputs may be any that keep to these rules, and one draw needn't show every extreme that they name: `adapter_per_block`: every one of the 4 adapters serves one or more blocks. `rows_per_block`: the live rows of a block stand at its start and the rest are padding; some block is full.
All inputs are finite; a program needn't handle non-finite values.
Results may differ from the reference program's by a relative error of at most 0.005.
Values may be sent and summed in bfloat16 or wider, within the bound.
No kernel may reach another device: no remote copies, remote signals or barrier semaphores. Data moves between devices by JAX's collectives and lax.ppermute only.
A program may use at most 128 MiB of HBM per device.

```python
import jax
import jax.numpy as jnp
from jax import lax

MODEL_WIDTH = 4608
HIDDEN_UNITS = 36864
ADAPTER_RANK = 64
BLOCK = 128
ADAPTER_COUNT = 4
TOKEN_COUNT = 512
BLOCKS = 4


def draw_rows_per_block(key, part):
    key = jax.random.fold_in(key, 7)
    first_key, second_key = jax.random.split(key)
    blocks = TOKEN_COUNT // BLOCK
    counts = jax.random.randint(first_key, (blocks,), BLOCK // 4, BLOCK + 1)
    full_at = jax.random.randint(second_key, (), 0, blocks)
    return jnp.where(jnp.arange(blocks) == full_at, BLOCK, counts).astype(jnp.int32)


def steps_of(own_key, extent, cuts, low, largest):
    factor_of = 1.0
    for dim, blocks in cuts:
        heights = jax.random.uniform(jax.random.fold_in(jax.random.fold_in(own_key, 6), dim), (blocks,), jnp.float32, low / len(cuts), largest / len(cuts))
        factor_of = factor_of * jnp.repeat(jnp.exp(heights), extent[dim] // blocks).reshape((-1,) + (1,) * (len(extent) - 1 - dim))
    return factor_of


def picks_of(stream_key, rows, amount, top, lift):
    ranking = jax.random.permutation(jax.random.fold_in(stream_key, 1), amount)
    pull = ranking
    for power in range(3):
        pull = pull * pull // amount
    pull = pull * lift // amount
    chance = jax.random.randint(jax.random.fold_in(stream_key, 2), (rows, amount), 0, 4096) + pull
    holders = jax.random.permutation(jax.random.fold_in(stream_key, 3), rows)[jnp.arange(amount) % rows]
    chance = jnp.where(jnp.arange(rows)[:, None] == holders[None, :], 1 << 14, chance)
    priority = chance * amount + jnp.arange(amount)
    return lax.top_k(priority.astype(jnp.int32), top)[1].astype(jnp.int32)


def centred(stream_key, shape, spread, bound, cuts=(), dtype=jnp.bfloat16):
    gain = steps_of(stream_key, shape, cuts, -0.22, 0.18) if cuts else 1.0
    result = jax.random.normal(stream_key, shape, jnp.float32) * spread * gain
    return jnp.minimum(jnp.maximum(result, -bound), bound).astype(dtype)


def setup_inputs(seed: int = 0, part: int = 0) -> dict:
    seeds = jax.random.split(jax.random.key(seed), 7)
    part_splits = jax.random.split(jax.random.fold_in(seeds[6], part), 7)
    return {
        "tokens": centred(part_splits[0], (TOKEN_COUNT, MODEL_WIDTH), 1.0, 6.0, ((0, 16),)),
        "shared_up_weight": centred(seeds[1], (MODEL_WIDTH, HIDDEN_UNITS), MODEL_WIDTH ** -0.5, 0.09375, ((1, 16),)),
        "adapter_down_factor": centred(part_splits[2], (ADAPTER_COUNT, MODEL_WIDTH, ADAPTER_RANK), MODEL_WIDTH ** -0.5, 0.09375, ((0, 2), (1, 8)), jnp.float32),
        "adapter_up_factor": centred(part_splits[3], (ADAPTER_COUNT, ADAPTER_RANK, HIDDEN_UNITS), (4 * ADAPTER_RANK) ** -0.5, 0.375, ((2, 16),), jnp.float32),
        "adapter_per_block": picks_of(part_splits[4], BLOCKS, ADAPTER_COUNT, 1, 4096),
        "rows_per_block": draw_rows_per_block(jax.random.fold_in(jax.random.fold_in(seeds[6], part), 71), part),
    }


exact_precision = lax.Precision.HIGHEST


def reference(tokens, shared_up_weight, adapter_down_factor, adapter_up_factor, adapter_per_block, rows_per_block):
    blocks = TOKEN_COUNT // BLOCK
    base_output = jnp.dot(tokens, shared_up_weight, preferred_element_type=jnp.float32)
    indicator_matrix = (adapter_per_block[:, 0][:, None] == jnp.arange(ADAPTER_COUNT)[None, :]).astype(jnp.float32)
    blocked_rows = tokens.astype(jnp.float32).reshape(blocks, BLOCK, MODEL_WIDTH)
    picked_down_factor = jnp.einsum('vx,xsk->vsk', indicator_matrix, adapter_down_factor, precision=exact_precision)
    rank_reduction = jnp.einsum('lyx,lxz->lyz', blocked_rows, picked_down_factor, precision=exact_precision)
    picked_up_factor = jnp.einsum('gp,piz->giz', indicator_matrix, adapter_up_factor, precision=exact_precision)
    adapter_update = jnp.einsum('zyd,zdc->zyc', rank_reduction, picked_up_factor, precision=exact_precision).reshape(TOKEN_COUNT, HIDDEN_UNITS)
    position = jnp.arange(TOKEN_COUNT) % BLOCK
    active_rows = (position < jnp.repeat(rows_per_block, BLOCK)).astype(jnp.float32)
    return ((base_output + adapter_update) * active_rows[:, None]).astype(jnp.bfloat16)
```

```python
import functools

import jax
import jax.numpy as jnp
from jax import lax
from jax.experimental import pallas as pl
from jax.experimental.pallas import tpu as pltpu
from jax.sharding import PartitionSpec as P

BLOCK = 128
AXES = ("seq", "adapter")
CHUNKS = 2


def ring_position(s, n):
    z, y = s // 2, s % 2
    return z * (1 - y) + (n - 1 - z) * y


def ring_member(pos, n):
    up = pos < n // 2
    return jnp.where(up, 2 * pos, 2 * (n - 1 - pos) + 1)


def ring_perm(n):
    at = {ring_position(s, n): s for s in range(n)}
    perm = []
    for pos in range(n):
        s = at[pos]
        perm.append((2 * s, 2 * at[(pos + 1) % n]))
        perm.append((2 * s + 1, 2 * at[(pos - 1) % n] + 1))
    return perm


def core_perm(n):
    return [(2 * s + c, 2 * s + 1 - c) for s in range(n) for c in range(2)]


def y_perm(n):
    return [(2 * s + c, 2 * (s ^ 1) + c) for s in range(n) for c in range(2)]


def z_perm(n, shift):
    nz = n // 2
    return [
        (2 * (2 * z + y) + c, 2 * (2 * ((z - shift) % nz) + y) + c)
        for z in range(nz)
        for y in range(2)
        for c in range(2)
    ]


def gather_ring(piece, n):
    ring, swap = ring_perm(n), core_perm(n)
    own, other = [], []
    for step in range(n):
        if step:
            piece = lax.ppermute(piece, AXES, ring)
        own.append(piece)
        other.append(lax.ppermute(piece, AXES, swap))
    return own + other


def piece_rows(n, rows):
    s, c = lax.axis_index("seq"), lax.axis_index("adapter")
    pos = ring_position(s, n)
    step = jnp.arange(n)
    first = []
    for core in (c, 1 - c):
        back = jnp.where(core == 0, pos - step, pos + step)
        first.append((2 * ring_member(jnp.mod(back, n), n) + core) * rows)
    return jnp.concatenate(first).astype(jnp.int32)


def shrink_piece(tokens, down, adapters, n):
    z, y, c = lax.axis_index("seq") // 2, lax.axis_index("seq") % 2, lax.axis_index("adapter")
    nz, rows = n // 2, tokens.shape[0]
    held, width, rank = down.shape
    half = rank // 2
    both = lax.ppermute(tokens, AXES, core_perm(n))
    chip_rows = jnp.where(c == 0, jnp.stack([tokens, both]), jnp.stack([both, tokens])).reshape(2 * rows, -1)
    factor = jnp.swapaxes(down, 1, 2).astype(jnp.bfloat16).reshape(held, 2, half, width)
    mine = lax.dynamic_index_in_dim(factor, c, 1, False)
    theirs = lax.ppermute(lax.dynamic_index_in_dim(factor, 1 - c, 1, False), AXES, core_perm(n))
    every = jnp.where(c == 0, jnp.stack([mine, theirs]), jnp.stack([theirs, mine])).reshape(2 * held, half, width)
    per_block = BLOCK // (2 * rows)
    parts = []
    for shift in range(nz):
        seat = jnp.mod(z - shift, nz)
        pick = lax.dynamic_index_in_dim(every, adapters[2 * seat // per_block], 0, False)
        parts.append(lax.ppermute(pick, AXES, z_perm(n, shift)) if shift else pick)
    mine = jnp.stack(parts)
    theirs = lax.ppermute(mine, AXES, y_perm(n))
    factor = jnp.where(y == 0, jnp.stack([mine, theirs], 1), jnp.stack([theirs, mine], 1))
    turned = lax.dynamic_slice_in_dim(
        jnp.concatenate([chip_rows, chip_rows], 1), z * 2 * width, n * width, 1
    ).reshape(2 * rows, nz, 2, width)
    shrink = jnp.einsum("tzyk,zyrk->tr", turned, factor, preferred_element_type=jnp.float32)
    high = shrink.astype(jnp.bfloat16)
    low = (shrink - high.astype(jnp.float32)).astype(jnp.bfloat16)
    return jnp.concatenate([high[:rows], high[rows:], low[:rows], low[rows:]], 1)


def collect(first, pieces, held, sems):
    copies = []
    for i, piece in enumerate(pieces):
        rows = piece.shape[0]
        place = held.at[pl.ds(pl.multiple_of(first[i], rows), rows), :]
        copies.append(pltpu.make_async_copy(piece, place, sems.at[i]))
    for copy in copies:
        copy.start()
    for copy in copies:
        copy.wait()


def first_kernel(count, first, *refs):
    pieces, (w_ref, out_ref, held, sems) = refs[:count], refs[count:]

    @pl.when(pl.program_id(0) == 0)
    def _():
        collect(first, pieces, held, sems)

    out_ref[...] = jnp.dot(held[...], w_ref[...], preferred_element_type=jnp.float32)


def last_kernel(count, first, adapters, live, *refs):
    pieces, (w_ref, base_ref, up_ref, out_ref, held, shrink, sems) = refs[:count], refs[count:]
    depth, rows = w_ref.shape[0], pieces[0].shape[0]
    half = shrink.shape[1] // 4

    @pl.when(pl.program_id(0) == 0)
    def _():
        collect(first, pieces, held, sems)
        for start in range(0, shrink.shape[0], 2 * rows):
            zero = held[start : start + rows, depth:]
            one = held[start + rows : start + 2 * rows, depth:]
            for core in range(2):
                a, b = core * half, (2 + core) * half
                shrink[start + core * rows : start + (core + 1) * rows, :] = jnp.concatenate(
                    [zero[:, a : a + half], one[:, a : a + half], zero[:, b : b + half], one[:, b : b + half]], 1
                )

    total = base_ref[...] + jnp.dot(held[:, :depth], w_ref[...], preferred_element_type=jnp.float32)
    for block in range(shrink.shape[0] // BLOCK):
        at = slice(block * BLOCK, (block + 1) * BLOCK)
        factor = up_ref[adapters[block]].astype(jnp.bfloat16)
        delta = jnp.dot(shrink[at, :], jnp.concatenate([factor, factor], 0), preferred_element_type=jnp.float32)
        on = lax.broadcasted_iota(jnp.int32, delta.shape, 0) < live[block]
        out_ref[at, :] = jnp.where(on, total[at] + delta, 0.0).astype(out_ref.dtype)


def matmul_first(first, pieces, weight, chunk, columns):
    count, (rows, depth) = len(pieces), pieces[0].shape
    total, width = rows * count, weight.shape[1]
    return pl.pallas_call(
        functools.partial(first_kernel, count),
        out_shape=jax.ShapeDtypeStruct((total, width), jnp.float32),
        grid_spec=pltpu.PrefetchScalarGridSpec(
            num_scalar_prefetch=1,
            grid=(width // columns,),
            in_specs=[pl.BlockSpec(memory_space=pl.ANY)] * count
            + [pl.BlockSpec((depth, columns), lambda j, *_: (chunk, j))],
            out_specs=pl.BlockSpec((total, columns), lambda j, *_: (0, j)),
            scratch_shapes=[pltpu.VMEM((total, depth), jnp.bfloat16), pltpu.SemaphoreType.DMA((count,))],
        ),
        compiler_params=pltpu.CompilerParams(vmem_limit_bytes=40 << 20),
        cost_estimate=pl.CostEstimate(
            flops=2 * total * depth * width, bytes_accessed=2 * depth * width + 4 * total * width, transcendentals=0
        ),
    )(first, *pieces, weight)


def matmul_last(first, adapters, live, pieces, weight, chunk, base, up, columns):
    count, (rows, wide) = len(pieces), pieces[0].shape
    total, width = rows * count, weight.shape[1]
    rank = up.shape[1]
    depth = wide - 2 * rank
    return pl.pallas_call(
        functools.partial(last_kernel, count),
        out_shape=jax.ShapeDtypeStruct((total, width), jnp.bfloat16),
        grid_spec=pltpu.PrefetchScalarGridSpec(
            num_scalar_prefetch=3,
            grid=(width // columns,),
            in_specs=[pl.BlockSpec(memory_space=pl.ANY)] * count
            + [
                pl.BlockSpec((depth, columns), lambda j, *_: (chunk, j)),
                pl.BlockSpec((total, columns), lambda j, *_: (0, j)),
                pl.BlockSpec((up.shape[0], rank, columns), lambda j, *_: (0, 0, j)),
            ],
            out_specs=pl.BlockSpec((total, columns), lambda j, *_: (0, j)),
            scratch_shapes=[
                pltpu.VMEM((total, wide), jnp.bfloat16),
                pltpu.VMEM((total, 2 * rank), jnp.bfloat16),
                pltpu.SemaphoreType.DMA((count,)),
            ],
        ),
        compiler_params=pltpu.CompilerParams(vmem_limit_bytes=40 << 20),
        cost_estimate=pl.CostEstimate(
            flops=2 * total * depth * width, bytes_accessed=2 * depth * width + 6 * total * width, transcendentals=0
        ),
    )(first, adapters, live, *pieces, weight, base, up)


def on_device(n, tokens, weight, down, up, adapter_per_block, rows_per_block):
    rows = tokens.shape[0]
    adapters = adapter_per_block[:, 0]
    columns = 256 if weight.shape[1] % 256 == 0 else weight.shape[1]
    depth = tokens.shape[1] // CHUNKS
    first = piece_rows(n, rows)
    early = gather_ring(tokens[:, :depth], n)
    shrink = shrink_piece(tokens, down, adapters, n)
    late = gather_ring(jnp.concatenate([tokens[:, depth:], shrink], 1), n)
    base = matmul_first(first, early, weight, 0, columns)
    return matmul_last(first, adapters, rows_per_block, late, weight, 1, base, up, columns)


def solution(mesh):
    placed = (
        P(("groups", "seq", "adapter"), None),
        P(None, ("seq", "adapter")),
        P(("groups", "adapter"), "seq", None),
        P("groups", None, ("seq", "adapter")),
        P("groups", None),
        P("groups"),
    )
    return jax.shard_map(
        functools.partial(on_device, mesh.shape["seq"]),
        mesh=mesh,
        in_specs=placed,
        out_specs=P("groups", ("seq", "adapter")),
        check_vma=False,
    )
```

```python
import functools

import jax
import jax.numpy as jnp
import numpy as np
from jax import lax
from jax.experimental import pallas as pl
from jax.experimental.pallas import tpu as pltpu
from jax.sharding import PartitionSpec as P

BLOCK = 128
AXES = ("seq", "adapter")
CHUNKS = 2


def ring_order(n):
    return [2 * z for z in range(n // 2)] + [2 * z + 1 for z in reversed(range(n // 2))]


def ring_distances(n):
    steps = [0]
    for hop in range(1, n // 2):
        steps += [-hop, hop]
    return steps + [n // 2]


def ring_perm(n, way):
    order = ring_order(n)
    return [(2 * s + c, 2 * order[(pos + way) % n] + c) for pos, s in enumerate(order) for c in range(2)]


def flip_perm(n, y, c):
    return [(2 * s + k, 2 * (s ^ y) + (k ^ c)) for s in range(n) for k in range(2)]


def z_perm(n, shift):
    nz = n // 2
    return [
        (2 * (2 * z + y) + c, 2 * (2 * ((z - shift) % nz) + y) + c)
        for z in range(nz)
        for y in range(2)
        for c in range(2)
    ]


def device_table(n):
    order, nz = ring_order(n), n // 2
    place = {s: pos for pos, s in enumerate(order)}
    table = np.zeros((2 * n, 3, n), np.int32)
    for s in range(n):
        for c in range(2):
            for i, distance in enumerate(ring_distances(n)):
                chip = order[(place[s] + distance) % n]
                table[2 * s + c, 0, i] = chip
                for core in range(2):
                    turn = (chip // 2 - s // 2) % nz
                    table[2 * s + c, 1 + core, i] = 4 * turn + 2 * ((chip ^ s) & 1) + (core ^ c)
    return table.reshape(2 * n, -1)


def gather_ring(chunks, n):
    ahead, back = ring_perm(n, 1), ring_perm(n, -1)
    swap = flip_perm(n, 0, 1)
    own = [[x] for x in chunks]
    other = [[lax.ppermute(x, AXES, swap)] for x in chunks]
    up, down = list(chunks), list(chunks)
    for hop in range(1, n // 2):
        for k in range(len(chunks)):
            up[k] = lax.ppermute(up[k], AXES, ahead)
            down[k] = lax.ppermute(down[k], AXES, back)
        for k in range(len(chunks)):
            own[k] += [up[k], down[k]]
            other[k] += [lax.ppermute(x, AXES, swap) for x in (up[k], down[k])]
    for k in range(len(chunks)):
        end = lax.ppermute(*((down[k], AXES, back) if k % 2 else (up[k], AXES, ahead)))
        own[k].append(end)
        other[k].append(lax.ppermute(end, AXES, swap))
    return own, other


def pick_kernel(n, blocks_apart, adapters, place, keep, keep_far, give, give_far, *outs):
    nz, held = n // 2, keep.shape[0]
    s, c = place[0], place[1]
    z, y = s >> 1, s & 1
    for shift, out in enumerate(outs):
        seat = z - shift
        seat = jnp.where(seat < 0, seat + nz, seat)
        adapter = adapters[(seat * 2 * blocks_apart) // BLOCK]
        for index in range(held):

            @pl.when(adapter == c * held + index)
            def _():
                out[y] = keep[index]
                out[1 - y] = keep_far[index]

            @pl.when(adapter == (1 - c) * held + index)
            def _():
                out[y] = give[index]
                out[1 - y] = give_far[index]


def split_kernel(place, down_ref, keep, give):
    half = keep.shape[1]
    c = place[1]
    for ref, core in ((keep, c), (give, 1 - c)):
        ref[...] = down_ref[:, pl.ds(pl.multiple_of(core * half, half), half), :].astype(jnp.bfloat16)


def whole(count):
    return [pl.BlockSpec(memory_space=pltpu.VMEM)] * count


def small_call(kernel, scalars, arrays, outs):
    return pl.pallas_call(
        kernel,
        out_shape=[jax.ShapeDtypeStruct(shape, jnp.bfloat16) for shape in outs],
        in_specs=[pl.BlockSpec(memory_space=pltpu.SMEM)] * len(scalars) + whole(len(arrays)),
        out_specs=whole(len(outs)),
    )(*scalars, *arrays)


def spread_shrink(own, other, down, adapters, place, n):
    z, c = lax.axis_index("seq") >> 1, lax.axis_index("adapter")
    nz, rows = n // 2, own[0].shape[0]
    held, width, rank = down.shape
    half = rank // 2
    part = (held, half, width)
    keep, give = small_call(split_kernel, [place], [jnp.swapaxes(down, 1, 2)], [part, part])
    keep_far = lax.ppermute(keep, AXES, flip_perm(n, 1, 0))
    give_near = lax.ppermute(give, AXES, flip_perm(n, 0, 1))
    give_far = lax.ppermute(give, AXES, flip_perm(n, 1, 1))
    picks = small_call(
        functools.partial(pick_kernel, n, 2 * rows),
        [adapters, place],
        [keep, keep_far, give_near, give_far],
        [(2, half, width)] * nz,
    )
    factor = jnp.stack(
        [picks[0]] + [lax.ppermute(picks[shift], AXES, z_perm(n, shift)) for shift in range(1, nz)]
    )
    mine, theirs = jnp.concatenate(own, 1), jnp.concatenate(other, 1)
    chip_rows = jnp.where(c == 0, jnp.stack([mine, theirs]), jnp.stack([theirs, mine])).reshape(2 * rows, -1)
    turned = lax.dynamic_slice_in_dim(
        jnp.concatenate([chip_rows, chip_rows], 1), z * 2 * width, n * width, 1
    ).reshape(2 * rows, nz, 2, width)
    shrink = jnp.einsum("tzyk,zyrk->tr", turned, factor, preferred_element_type=jnp.float32)
    high = shrink.astype(jnp.bfloat16)
    low = (shrink - high.astype(jnp.float32)).astype(jnp.bfloat16)
    piece = jnp.concatenate([high[:rows], high[rows:], low[:rows], low[rows:]], 1)
    near = jnp.concatenate(
        [piece] + [lax.ppermute(piece, AXES, flip_perm(n, y, c)) for y, c in ((0, 1), (1, 0), (1, 1))], 0
    )
    return [near] + [lax.ppermute(near, AXES, z_perm(n, shift)) for shift in range(1, nz)]


def rows_kernel(layout, table, place, adapters, live, *refs):
    n, begin, entries, chunks, aliased = layout
    count = 2 * entries * chunks
    pieces, refs = refs[:count], refs[count:]
    parts, refs = refs[: n // 2], refs[n // 2 :]
    w_ref, up_ref = refs[:2]
    out_ref, held, near, shrink, block, in_sems, out_sems = refs[2 + aliased :]
    rows, depth = pieces[0].shape
    chip, (_, columns) = 2 * rows, w_ref.shape
    half = near.shape[1] // 4
    step = pl.program_id(0)
    c = place[1]

    @pl.when(step == 0)
    def _():
        copies = []
        for i in range(entries):
            for k in range(chunks):
                for far in range(2):
                    at = (i * chunks + k) * 2 + far
                    core = 1 - c if far else c
                    row = pl.multiple_of(i * chip + core * rows, rows)
                    to = held.at[pl.ds(row, rows), pl.ds(k * depth, depth)]
                    copies.append(pltpu.make_async_copy(pieces[at], to, in_sems.at[at]))
        for copy in copies:
            copy.start()
        for j, part in enumerate(parts):
            near[j * 4 * rows : (j + 1) * 4 * rows, :] = part[...]
        for i in range(entries):
            zero, one = (
                near[pl.ds(pl.multiple_of(table[(1 + core) * n + begin + i] * rows, rows), rows), :]
                for core in range(2)
            )
            for core in range(2):
                a, b = core * half, (2 + core) * half
                shrink[i * chip + core * rows : i * chip + (core + 1) * rows, :] = jnp.concatenate(
                    [zero[:, a : a + half], one[:, a : a + half], zero[:, b : b + half], one[:, b : b + half]], 1
                )
        for copy in copies:
            copy.wait()

    def outgoing(j, i):
        to = out_ref.at[pl.ds(pl.multiple_of(table[begin + i] * chip, chip), chip), pl.ds(j * columns, columns)]
        return pltpu.make_async_copy(block.at[j, pl.ds(i * chip, chip), :], to, out_sems.at[j, i])

    tile = jnp.dot(held[...], w_ref[...], preferred_element_type=jnp.float32)
    for i in range(entries):
        first = table[begin + i] * chip
        of_block = first // BLOCK
        factor = up_ref[adapters[of_block]].astype(jnp.bfloat16)
        at = slice(i * chip, (i + 1) * chip)
        delta = jnp.dot(
            shrink[at, :], jnp.concatenate([factor, factor], 0), preferred_element_type=jnp.float32
        )
        row = lax.broadcasted_iota(jnp.int32, delta.shape, 0) + (first - of_block * BLOCK)
        block[step, at, :] = jnp.where(row < live[of_block], tile[at] + delta, 0.0).astype(out_ref.dtype)
    for j in range(block.shape[0]):

        @pl.when(step == j)
        def _():
            for i in range(entries):
                outgoing(j, i).start()

    @pl.when(step == block.shape[0] - 1)
    def _():
        for j in range(block.shape[0]):
            for i in range(entries):
                outgoing(j, i).wait()


def rows_matmul(n, begin, own, other, parts, scalars, weight, up, into):
    chunks, entries = len(own), len(own[0])
    pieces = [x[k][i] for i in range(entries) for k in range(chunks) for x in (own, other)]
    rows, depth = pieces[0].shape
    total, width = 2 * rows * entries, weight.shape[1]
    columns = 768 if width % 768 == 0 else width
    held, rank = up.shape[:2]
    aliased = [] if into is None else [into]
    operands = [*scalars, *pieces, *parts, weight, up, *aliased]
    return pl.pallas_call(
        functools.partial(rows_kernel, (n, begin, entries, chunks, len(aliased))),
        out_shape=jax.ShapeDtypeStruct((2 * n * rows, width), jnp.bfloat16),
        grid_spec=pltpu.PrefetchScalarGridSpec(
            num_scalar_prefetch=len(scalars),
            grid=(width // columns,),
            in_specs=[pl.BlockSpec(memory_space=pl.ANY)] * len(pieces)
            + whole(len(parts))
            + [
                pl.BlockSpec((weight.shape[0], columns), lambda j, *_: (0, j)),
                pl.BlockSpec((held, rank, columns), lambda j, *_: (0, 0, j)),
            ]
            + [pl.BlockSpec(memory_space=pl.ANY)] * len(aliased),
            out_specs=pl.BlockSpec(memory_space=pl.ANY),
            scratch_shapes=[
                pltpu.VMEM((total, chunks * depth), jnp.bfloat16),
                pltpu.VMEM((2 * n * rows, 2 * rank), jnp.bfloat16),
                pltpu.VMEM((total, 2 * rank), jnp.bfloat16),
                pltpu.VMEM((width // columns, total, columns), jnp.bfloat16),
                pltpu.SemaphoreType.DMA((len(pieces),)),
                pltpu.SemaphoreType.DMA((width // columns, entries)),
            ],
        ),
        input_output_aliases={len(operands) - 1: 0} if aliased else {},
        compiler_params=pltpu.CompilerParams(vmem_limit_bytes=44 << 20),
        cost_estimate=pl.CostEstimate(
            flops=2 * total * chunks * depth * width,
            bytes_accessed=2 * chunks * depth * width + 2 * total * width,
            transcendentals=0,
        ),
    )(*operands)


def on_device(n, tokens, weight, down, up, adapter_per_block, rows_per_block):
    depth = tokens.shape[1] // CHUNKS
    adapters = adapter_per_block[:, 0]
    device = lax.axis_index(AXES)
    table = lax.dynamic_index_in_dim(jnp.asarray(device_table(n)), device, 0, False)
    place = jnp.stack([device >> 1, device & 1]).astype(jnp.int32)
    own, other = gather_ring([tokens[:, k * depth : (k + 1) * depth] for k in range(CHUNKS)], n)
    parts = spread_shrink([x[0] for x in own], [x[0] for x in other], down, adapters, place, n)
    scalars = (table, place, adapters, rows_per_block)
    cut = 1 + 2 * (n // 2 - 2)
    out = None
    for begin, end in ((0, cut), (cut, n)):
        out = rows_matmul(
            n, begin, [x[begin:end] for x in own], [x[begin:end] for x in other], parts, scalars, weight, up, out
        )
    return out


def solution(mesh):
    placed = (
        P(("groups", "seq", "adapter"), None),
        P(None, ("seq", "adapter")),
        P(("groups", "adapter"), "seq", None),
        P("groups", None, ("seq", "adapter")),
        P("groups", None),
        P("groups"),
    )
    return jax.shard_map(
        functools.partial(on_device, mesh.shape["seq"]),
        mesh=mesh,
        in_specs=placed,
        out_specs=P("groups", ("seq", "adapter")),
        check_vma=False,
    )
```

```python
import functools

import jax
import jax.numpy as jnp
import numpy as np
from jax import lax
from jax.experimental import pallas as pl
from jax.experimental.pallas import tpu as pltpu
from jax.sharding import PartitionSpec as P

BLOCK = 128
AXES = ("seq", "adapter")
CHUNKS = 2


def ring_order(n):
    return [2 * z for z in range(n // 2)] + [2 * z + 1 for z in reversed(range(n // 2))]


def ring_distances(n):
    steps = [0]
    for hop in range(1, n // 2):
        steps += [-hop, hop]
    return steps + [n // 2]


def ring_perm(n, way):
    order = ring_order(n)
    return [(2 * s + c, 2 * order[(pos + way) % n] + c) for pos, s in enumerate(order) for c in range(2)]


def flip_perm(n, y, c):
    return [(2 * s + k, 2 * (s ^ y) + (k ^ c)) for s in range(n) for k in range(2)]


def z_perm(n, shift):
    nz = n // 2
    return [
        (2 * (2 * z + y) + c, 2 * (2 * ((z - shift) % nz) + y) + c)
        for z in range(nz)
        for y in range(2)
        for c in range(2)
    ]


def device_table(n):
    order, nz = ring_order(n), n // 2
    place = {s: pos for pos, s in enumerate(order)}
    table = np.zeros((2 * n, 3, n), np.int32)
    for s in range(n):
        for c in range(2):
            for i, distance in enumerate(ring_distances(n)):
                chip = order[(place[s] + distance) % n]
                table[2 * s + c, 0, i] = chip
                for core in range(2):
                    turn = (chip // 2 - s // 2) % nz
                    table[2 * s + c, 1 + core, i] = 4 * turn + 2 * ((chip ^ s) & 1) + (core ^ c)
    return table.reshape(2 * n, -1)


def gather_ring(chunks, n):
    ahead, back = ring_perm(n, 1), ring_perm(n, -1)
    swap = flip_perm(n, 0, 1)
    own = [[x] for x in chunks]
    other = [[lax.ppermute(x, AXES, swap)] for x in chunks]
    up, down = list(chunks), list(chunks)
    for hop in range(1, n // 2):
        for k in range(len(chunks)):
            up[k] = lax.ppermute(up[k], AXES, ahead)
            down[k] = lax.ppermute(down[k], AXES, back)
        for k in range(len(chunks)):
            own[k] += [up[k], down[k]]
            other[k] += [lax.ppermute(x, AXES, swap) for x in (up[k], down[k])]
    for k in range(len(chunks)):
        end = lax.ppermute(*((down[k], AXES, back) if k % 2 else (up[k], AXES, ahead)))
        own[k].append(end)
        other[k].append(lax.ppermute(end, AXES, swap))
    return own, other


def pick_kernel(n, blocks_apart, adapters, place, keep, keep_far, give, give_far, *outs):
    nz, held = n // 2, keep.shape[0]
    s, c = place[0], place[1]
    z, y = s >> 1, s & 1
    for shift, out in enumerate(outs):
        seat = z - shift
        seat = jnp.where(seat < 0, seat + nz, seat)
        adapter = adapters[(seat * 2 * blocks_apart) // BLOCK]
        for index in range(held):

            @pl.when(adapter == c * held + index)
            def _():
                out[y] = keep[index]
                out[1 - y] = keep_far[index]

            @pl.when(adapter == (1 - c) * held + index)
            def _():
                out[y] = give[index]
                out[1 - y] = give_far[index]


def split_kernel(place, down_ref, keep, give):
    half = keep.shape[1]
    c = place[1]
    for ref, core in ((keep, c), (give, 1 - c)):
        ref[...] = down_ref[:, pl.ds(pl.multiple_of(core * half, half), half), :].astype(jnp.bfloat16)


def whole(count):
    return [pl.BlockSpec(memory_space=pltpu.VMEM)] * count


def in_vmem(arrays):
    return [pltpu.with_memory_space_constraint(x, pltpu.VMEM) for x in arrays]


def call(kernel, scalars, arrays, after, outs, scratch=(), limit=8, flops=0):
    operands = len(scalars) + len(arrays)

    def body(*refs):
        kernel(*refs[:operands], *refs[operands + len(after) :])

    return pl.pallas_call(
        body,
        out_shape=[pltpu.VMEM(shape, dtype) for shape, dtype in outs],
        in_specs=[pl.BlockSpec(memory_space=pltpu.SMEM)] * len(scalars)
        + whole(len(arrays))
        + [pl.BlockSpec(memory_space=pl.ANY)] * len(after),
        out_specs=whole(len(outs)),
        scratch_shapes=list(scratch),
        compiler_params=pltpu.CompilerParams(vmem_limit_bytes=limit << 20),
        cost_estimate=pl.CostEstimate(flops=flops, bytes_accessed=0, transcendentals=0),
    )(*scalars, *in_vmem(arrays), *after)


def assemble(place, pieces, held, entries):
    rows, depth = pieces[0].shape
    chunks = held.shape[1] // depth
    c = place[1]
    for i in range(entries):
        for k in range(chunks):
            for far in range(2):
                core = 1 - c if far else c
                row = pl.multiple_of(i * 2 * rows + core * rows, rows)
                held[pl.ds(row, rows), k * depth : (k + 1) * depth] = pieces[(i * chunks + k) * 2 + far][...]


def shrink_kernel(nz, count, place, *refs):
    parts, pieces, (out, held, turned, factor) = refs[:nz], refs[nz : nz + count], refs[nz + count :]
    rows, half = out.shape[0], factor.shape[0]
    z = place[0] >> 1
    assemble(place, pieces, held, 1)
    for j, part in enumerate(parts):
        turned[j] = part[...]
    width = turned.shape[3]
    for at in range(nz):
        turn = jnp.where(at < z, at - z + nz, at - z)
        for y in range(2):
            first = (2 * at + y) * width
            factor[:, first : first + width] = turned[turn, y]
    shrink = lax.dot_general(
        held[...], factor[...], (((1,), (1,)), ((), ())), preferred_element_type=jnp.float32
    )
    high = shrink.astype(jnp.bfloat16)
    low = (shrink - high.astype(jnp.float32)).astype(jnp.bfloat16)
    out[...] = jnp.concatenate([high[:rows], high[rows:], low[:rows], low[rows:]], 1)


class Shrink:
    def __init__(self, down, place, n):
        self.n, self.place = n, place
        held, self.width, rank = down.shape
        self.half = rank // 2
        part = ((held, self.half, self.width), jnp.bfloat16)
        keep, give = call(split_kernel, [place], [jnp.swapaxes(down, 1, 2)], [], [part, part])
        self.factors = [keep] + [
            lax.ppermute(x, AXES, flip_perm(n, y, c)) for x, y, c in ((keep, 1, 0), (give, 0, 1), (give, 1, 1))
        ]

    def pick(self, adapters, rows, after):
        nz = self.n // 2
        self.picks = call(
            functools.partial(pick_kernel, self.n, 2 * rows),
            [adapters, self.place],
            self.factors,
            after,
            [((2, self.half, self.width), jnp.bfloat16)] * nz,
        )
        self.parts = [self.picks[0]] + [
            lax.ppermute(self.picks[shift], AXES, z_perm(self.n, shift)) for shift in range(1, nz)
        ]

    def multiply(self, pieces, after):
        n, rows = self.n, pieces[0].shape[0]
        (self.piece,) = call(
            functools.partial(shrink_kernel, n // 2, len(pieces)),
            [self.place],
            [*self.parts, *pieces],
            after,
            [((rows, 4 * self.half), jnp.bfloat16)],
            [
                pltpu.VMEM((2 * rows, n * self.width), jnp.bfloat16),
                pltpu.VMEM((n // 2, 2, self.half, self.width), jnp.bfloat16),
                pltpu.VMEM((self.half, n * self.width), jnp.bfloat16),
            ],
        )
        self.near = jnp.concatenate(
            [self.piece]
            + [lax.ppermute(self.piece, AXES, flip_perm(n, y, c)) for y, c in ((0, 1), (1, 0), (1, 1))],
            0,
        )
        return [self.near] + [lax.ppermute(self.near, AXES, z_perm(n, shift)) for shift in range(1, n // 2)]


def load_kernel(w_ref, up_ref, w_out, up_out, held, sems):
    parts = sems.shape[0] - 1
    depth, rank = w_ref.shape[0] // parts, up_ref.shape[1]
    copies = [
        pltpu.make_async_copy(
            w_ref.at[pl.ds(k * depth, depth), :], w_out.at[pl.ds(k * depth, depth), :], sems.at[k]
        )
        for k in range(parts)
    ]
    copies = [pltpu.make_async_copy(up_ref, held, sems.at[parts])] + copies
    for copy in copies:
        copy.start()
    copies[0].wait()
    for adapter in range(up_ref.shape[0]):
        factor = held[adapter].astype(jnp.bfloat16)
        up_out[adapter, :rank, :] = factor
        up_out[adapter, rank:, :] = factor
    for copy in copies[1:]:
        copy.wait()


def load(weight, up):
    adapters, rank, width = up.shape
    return pl.pallas_call(
        load_kernel,
        out_shape=[
            pltpu.VMEM(weight.shape, weight.dtype),
            pltpu.VMEM((adapters, 2 * rank, width), jnp.bfloat16),
        ],
        in_specs=[pl.BlockSpec(memory_space=pltpu.HBM)] * 2,
        out_specs=whole(2),
        scratch_shapes=[pltpu.VMEM(up.shape, up.dtype), pltpu.SemaphoreType.DMA((9,))],
        compiler_params=pltpu.CompilerParams(vmem_limit_bytes=8 << 20),
        cost_estimate=pl.CostEstimate(
            flops=0, bytes_accessed=2 * weight.size + 4 * up.size, transcendentals=0
        ),
    )(*(pltpu.with_memory_space_constraint(x, pltpu.HBM) for x in (weight, up)))


def tile_width(width):
    return 768 if width % 768 == 0 else width


def base_kernel(entries, count, place, *refs):
    pieces, w_ref, (base, held) = refs[:count], refs[count], refs[count + 1 :]
    assemble(place, pieces, held, entries)
    width = w_ref.shape[1]
    columns = tile_width(width)
    for j in range(0, width, columns):
        at = slice(j, j + columns)
        base[:, at] = jnp.dot(held[...], w_ref[:, at], preferred_element_type=jnp.float32)


def base_rows(pieces, entries, weight, place, after):
    rows, depth = pieces[0].shape
    total = 2 * rows * entries
    shape = (total, weight.shape[1])
    (base,) = call(
        functools.partial(base_kernel, entries, len(pieces)),
        [place],
        [*pieces, weight],
        after,
        [(shape, jnp.float32)],
        [pltpu.VMEM((total, weight.shape[0]), jnp.bfloat16)],
        limit=8,
        flops=2 * total * weight.size,
    )
    return base


def collect_shrink(n, begin, entries, table, parts, near, shrink):
    rows = near.shape[0] // (2 * n)
    half = near.shape[1] // 4
    for j, part in enumerate(parts):
        near[j * 4 * rows : (j + 1) * 4 * rows, :] = part[...]
    for i in range(entries):
        zero, one = (
            near[pl.ds(pl.multiple_of(table[(1 + core) * n + begin + i] * rows, rows), rows), :]
            for core in range(2)
        )
        for core in range(2):
            a, b = core * half, (2 + core) * half
            first = (2 * i + core) * rows
            shrink[first : first + rows, :] = jnp.concatenate(
                [zero[:, a : a + half], one[:, a : a + half], zero[:, b : b + half], one[:, b : b + half]], 1
            )


def finish_chip(first, adapters, live, base, shrink, up_ref, at):
    of_block = first // BLOCK
    delta = jnp.dot(shrink, up_ref[adapters[of_block], :, at], preferred_element_type=jnp.float32)
    row = lax.broadcasted_iota(jnp.int32, delta.shape, 0) + (first - of_block * BLOCK)
    return jnp.where(row < live[of_block], base + delta, 0.0).astype(jnp.bfloat16)


def finish_kernel(n, counts, table, place, adapters, live, *refs):
    base_count, part_count = counts
    bases, refs = refs[:base_count], refs[base_count:]
    parts, refs = refs[:part_count], refs[part_count:]
    up_ref, out_ref, near, shrink, block, sems = refs
    chip = 2 * near.shape[0] // (2 * n)
    entries = shrink.shape[0] // chip
    collect_shrink(n, 0, entries, table, parts, near, shrink)
    width = up_ref.shape[2]
    columns = tile_width(width)
    copies = []
    for j in range(width // columns):
        at = slice(j * columns, (j + 1) * columns)
        i = 0
        for base in bases:
            for k in range(base.shape[0] // chip):
                first = table[i] * chip
                rows = slice(i * chip, (i + 1) * chip)
                block[j, rows, :] = finish_chip(
                    first, adapters, live, base[k * chip : (k + 1) * chip, at], shrink[rows, :], up_ref, at
                )
                copies.append(
                    pltpu.make_async_copy(
                        block.at[j, pl.ds(i * chip, chip), :],
                        out_ref.at[pl.ds(pl.multiple_of(first, chip), chip), pl.ds(j * columns, columns)],
                        sems.at[j, i],
                    )
                )
                copies[-1].start()
                i += 1
    for copy in copies:
        copy.wait()


def last_kernel(n, counts, table, place, adapters, live, *refs):
    piece_count, part_count = counts
    pieces, refs = refs[:piece_count], refs[piece_count:]
    parts, refs = refs[:part_count], refs[part_count:]
    w_ref, up_ref, _, out_ref, held, near, shrink, block, sems = refs
    chip = held.shape[0]
    assemble(place, pieces, held, 1)
    collect_shrink(n, n - 1, 1, table, parts, near, shrink)
    width = up_ref.shape[2]
    columns = tile_width(width)
    first = table[n - 1] * chip
    copies = []
    for j in range(width // columns):
        at = slice(j * columns, (j + 1) * columns)
        base = jnp.dot(held[...], w_ref[:, at], preferred_element_type=jnp.float32)
        block[j] = finish_chip(first, adapters, live, base, shrink[...], up_ref, at)
        copies.append(
            pltpu.make_async_copy(
                block.at[j],
                out_ref.at[pl.ds(pl.multiple_of(first, chip), chip), pl.ds(j * columns, columns)],
                sems.at[j],
            )
        )
        copies[-1].start()
    for copy in copies:
        copy.wait()


def finish(kernel, n, counts, scalars, arrays, into, total, rows, up, held, flops):
    _, wide, width = up.shape
    columns = tile_width(width)
    tiles = width // columns
    sems = (tiles,) if held else (tiles, n - 1)
    return pl.pallas_call(
        functools.partial(kernel, n, counts),
        out_shape=jax.ShapeDtypeStruct((total, width), jnp.bfloat16),
        in_specs=[pl.BlockSpec(memory_space=pltpu.SMEM)] * len(scalars)
        + whole(len(arrays))
        + [pl.BlockSpec(memory_space=pl.ANY)] * len(into),
        out_specs=pl.BlockSpec(memory_space=pl.ANY),
        scratch_shapes=held
        + [
            pltpu.VMEM((total, wide), jnp.bfloat16),
            pltpu.VMEM((rows, wide), jnp.bfloat16),
            pltpu.VMEM((tiles, rows, columns), jnp.bfloat16),
            pltpu.SemaphoreType.DMA(sems),
        ],
        input_output_aliases={len(scalars) + len(arrays): 0} if into else {},
        compiler_params=pltpu.CompilerParams(vmem_limit_bytes=12 << 20),
        cost_estimate=pl.CostEstimate(flops=flops, bytes_accessed=2 * rows * width, transcendentals=0),
    )(*scalars, *in_vmem(arrays), *into)


def on_device(n, tokens, weight, down, up, adapter_per_block, rows_per_block):
    rows = tokens.shape[0]
    chip, total = 2 * rows, 2 * n * rows
    depth = tokens.shape[1] // CHUNKS
    adapters = adapter_per_block[:, 0]
    device = lax.axis_index(AXES)
    table = lax.dynamic_index_in_dim(jnp.asarray(device_table(n)), device, 0, False)
    place = jnp.stack([device >> 1, device & 1]).astype(jnp.int32)
    own, other = gather_ring([tokens[:, k * depth : (k + 1) * depth] for k in range(CHUNKS)], n)
    shrink = Shrink(down, place, n)
    weight, up = load(weight, up)

    def pieces(begin, end):
        return [x[k][i] for i in range(begin, end) for k in range(CHUNKS) for x in (own, other)]

    def arrived(hop):
        return [x[i] for x in own for i in range(2 * hop - 1, min(2 * hop + 1, n))]

    shrink.pick(adapters, rows, [*arrived(1), weight])
    bases = [base_rows(pieces(0, 1), 1, weight, place, [shrink.picks[0]])]
    parts = shrink.multiply(pieces(0, 1), [*arrived(2), *bases])
    for hop in range(1, n // 2):
        after = {1: [shrink.piece], 2: [shrink.near, *arrived(3)]}.get(hop, [])
        after.append(bases[-1])
        bases.append(base_rows(pieces(2 * hop - 1, 2 * hop + 1), 2, weight, place, after))
    scalars = (table, place, adapters, rows_per_block)
    out = finish(
        finish_kernel, n, (len(bases), len(parts)), scalars, [*bases, *parts, up],
        [], total, total - chip, up, [], 0,
    )
    last = pieces(n - 1, n)
    return finish(
        last_kernel, n, (len(last), len(parts)), scalars, [*last, *parts, weight, up],
        [out], total, chip, up, [pltpu.VMEM((chip, weight.shape[0]), jnp.bfloat16)], 2 * chip * weight.size,
    )


def solution(mesh):
    placed = (
        P(("groups", "seq", "adapter"), None),
        P(None, ("seq", "adapter")),
        P(("groups", "adapter"), "seq", None),
        P("groups", None, ("seq", "adapter")),
        P("groups", None),
        P("groups"),
    )
    return jax.shard_map(
        functools.partial(on_device, mesh.shape["seq"]),
        mesh=mesh,
        in_specs=placed,
        out_specs=P("groups", ("seq", "adapter")),
        check_vma=False,
    )
```

```python
import functools

import jax
import jax.numpy as jnp
from jax import lax
from jax.experimental import pallas as pl
from jax.experimental.pallas import tpu as pltpu
from jax.sharding import PartitionSpec as P

BLOCK = 128
AXES = ("seq", "adapter")
CHUNKS = 2


def ring_perm(n, way):
    order = [2 * z for z in range(n // 2)] + [2 * z + 1 for z in reversed(range(n // 2))]
    return [(2 * s + c, 2 * order[(pos + way) % n] + c) for pos, s in enumerate(order) for c in range(2)]


def swap_cores(x, n):
    return lax.ppermute(x, AXES, [(2 * s + c, 2 * s + 1 - c) for s in range(n) for c in range(2)])


def chip_at(distance, n):
    s = lax.axis_index("seq")
    z = s >> 1
    pos = jnp.where(s & 1 == 0, z, n - 1 - z) + distance
    pos = jnp.where(pos >= n, pos - n, pos)
    pos = jnp.where(pos < 0, pos + n, pos)
    return jnp.where(pos < n // 2, 2 * pos, 2 * (n - 1 - pos) + 1)


def hop_distances(hop, n):
    if hop == 0:
        return [0]
    return [-hop, hop] if hop < n // 2 else [hop]


class Ring:
    def __init__(self, chunks, n):
        self.n, self.up, self.down = n, list(chunks), list(chunks)

    def hop(self, hop, after=()):
        n = self.n
        if hop < n // 2:
            self.up = [lax.ppermute(x, AXES, ring_perm(n, 1)) for x in self.up]
            self.down = [lax.ppermute(x, AXES, ring_perm(n, -1)) for x in self.down]
            pieces = self.up + self.down
        else:
            pieces = [
                lax.ppermute((self.down if k % 2 else self.up)[k], AXES, ring_perm(n, -1 if k % 2 else 1))
                for k in range(CHUNKS)
            ]
        rows, depth = pieces[0].shape
        (joined,) = call(
            join_kernel, [], pieces, list(after), [((rows * len(pieces), depth), pieces[0].dtype)]
        )
        return joined


def join_kernel(*refs):
    *pieces, out = refs
    rows = pieces[0].shape[0]
    for i, piece in enumerate(pieces):
        out[i * rows : (i + 1) * rows, :] = piece[...]


def whole(count):
    return [pl.BlockSpec(memory_space=pltpu.VMEM)] * count


def in_vmem(arrays):
    return [pltpu.with_memory_space_constraint(x, pltpu.VMEM) for x in arrays]


def call(kernel, scalars, arrays, after, outs, scratch=(), limit=8, flops=0):
    operands = len(scalars) + len(arrays)

    def body(*refs):
        kernel(*refs[:operands], *refs[operands + len(after) :])

    return pl.pallas_call(
        body,
        out_shape=[pltpu.VMEM(shape, dtype) for shape, dtype in outs],
        in_specs=[pl.BlockSpec(memory_space=pltpu.SMEM)] * len(scalars)
        + whole(len(arrays))
        + [pl.BlockSpec(memory_space=pl.ANY)] * len(after),
        out_specs=whole(len(outs)),
        scratch_shapes=list(scratch),
        compiler_params=pltpu.CompilerParams(vmem_limit_bytes=limit << 20),
        cost_estimate=pl.CostEstimate(flops=flops, bytes_accessed=0, transcendentals=0),
    )(*scalars, *in_vmem(arrays), *after)


def split_kernel(down_ref, keep, give):
    half = keep.shape[1]
    c = lax.axis_index("adapter")
    for ref, core in ((keep, c), (give, 1 - c)):
        ref[...] = down_ref[:, pl.ds(pl.multiple_of(core * half, half), half), :].astype(jnp.bfloat16)


def pick_kernel(chip_rows, adapters, keep, give, out):
    held = keep.shape[0]
    c = lax.axis_index("adapter")
    for s in range(out.shape[0]):
        adapter = adapters[s * chip_rows // BLOCK]
        for index in range(held):

            @pl.when(adapter == c * held + index)
            def _():
                out[s] = keep[index]

            @pl.when(adapter == (1 - c) * held + index)
            def _():
                out[s] = give[index]


def shrink_kernel(own, other, parts, out, held, factor):
    rows, width = own.shape[0], parts.shape[2]
    c = lax.axis_index("adapter")
    for ref, core in ((own, c), (other, 1 - c)):
        held[pl.ds(pl.multiple_of(core * rows, rows), rows), :] = ref[...]
    for s in range(parts.shape[0]):
        factor[:, s * width : (s + 1) * width] = parts[s]
    shrink = lax.dot_general(
        held[...], factor[...], (((1,), (1,)), ((), ())), preferred_element_type=jnp.float32
    )
    high = shrink.astype(jnp.bfloat16)
    low = (shrink - high.astype(jnp.float32)).astype(jnp.bfloat16)
    piece = jnp.concatenate([high[:rows], high[rows:], low[:rows], low[rows:]], 1)
    for device in range(out.shape[0]):
        out[device] = piece


def load_kernel(w_ref, up_ref, w_out, up_out, held, sems):
    parts = sems.shape[0] - 1
    depth, rank = w_ref.shape[0] // parts, up_ref.shape[1]
    copies = [pltpu.make_async_copy(up_ref, held, sems.at[parts])] + [
        pltpu.make_async_copy(
            w_ref.at[pl.ds(k * depth, depth), :], w_out.at[pl.ds(k * depth, depth), :], sems.at[k]
        )
        for k in range(parts)
    ]
    for copy in copies:
        copy.start()
    copies[0].wait()
    for adapter in range(up_ref.shape[0]):
        factor = held[adapter].astype(jnp.bfloat16)
        up_out[adapter, :rank, :] = factor
        up_out[adapter, rank:, :] = factor
    for copy in copies[1:]:
        copy.wait()


def load(weight, up):
    adapters, rank, width = up.shape
    return pl.pallas_call(
        load_kernel,
        out_shape=[
            pltpu.VMEM(weight.shape, weight.dtype),
            pltpu.VMEM((adapters, 2 * rank, width), jnp.bfloat16),
        ],
        in_specs=[pl.BlockSpec(memory_space=pltpu.HBM)] * 2,
        out_specs=whole(2),
        scratch_shapes=[pltpu.VMEM(up.shape, up.dtype), pltpu.SemaphoreType.DMA((9,))],
        compiler_params=pltpu.CompilerParams(vmem_limit_bytes=8 << 20),
        cost_estimate=pl.CostEstimate(
            flops=0, bytes_accessed=2 * weight.size + 4 * up.size, transcendentals=0
        ),
    )(*(pltpu.with_memory_space_constraint(x, pltpu.HBM) for x in (weight, up)))


def assemble(pairs, rows, held):
    width = held.shape[1]
    c = lax.axis_index("adapter")
    first = 0
    for pair in pairs:
        depth = pair[0].shape[1]
        chunks = width // depth
        for chip in range(pair[0].shape[0] // (rows * chunks)):
            for k in range(chunks):
                at = (chip * chunks + k) * rows
                for ref, core in zip(pair, (c, 1 - c)):
                    row = pl.multiple_of(first + core * rows, rows)
                    held[pl.ds(row, rows), k * depth : (k + 1) * depth] = ref[at : at + rows, :]
            first += 2 * rows


def tile_width(width):
    return 768 if width % 768 == 0 else width


def base_kernel(rows, *refs):
    *pairs, w_ref, base, held = refs
    assemble(list(zip(pairs[::2], pairs[1::2])), rows, held)
    width = w_ref.shape[1]
    columns = tile_width(width)
    for j in range(0, width, columns):
        at = slice(j, j + columns)
        base[:, at] = jnp.dot(held[...], w_ref[:, at], preferred_element_type=jnp.float32)


def base_rows(pairs, chips, rows, weight, after):
    total = 2 * rows * chips
    (base,) = call(
        functools.partial(base_kernel, rows),
        [],
        [x for pair in pairs for x in pair] + [weight],
        after,
        [((total, weight.shape[1]), jnp.float32)],
        [pltpu.VMEM((total, weight.shape[0]), jnp.bfloat16)],
        flops=2 * total * weight.size,
    )
    return base


def finish_tile(distances, n, adapters, live, spread, up_ref, out_ref, block, sems, j, base_of):
    rows = spread.shape[1]
    half = spread.shape[2] // 4
    chip_rows, columns = 2 * rows, block.shape[2]
    at = slice(j * columns, (j + 1) * columns)
    copies = []
    for i, distance in enumerate(distances):
        chip = chip_at(distance, n)
        zero, one = spread[2 * chip], spread[2 * chip + 1]
        shrink = jnp.concatenate(
            [
                jnp.concatenate([x[:, a : a + half] for a in (k * half, (2 + k) * half) for x in (zero, one)], 1)
                for k in range(2)
            ],
            0,
        )
        first = chip * chip_rows
        of_block = first // BLOCK
        delta = jnp.dot(shrink, up_ref[adapters[of_block], :, at], preferred_element_type=jnp.float32)
        row = lax.broadcasted_iota(jnp.int32, delta.shape, 0) + (first - of_block * BLOCK)
        place = slice(i * chip_rows, (i + 1) * chip_rows)
        total = jnp.where(row < live[of_block], base_of(i) + delta, 0.0)
        block[j, place, :] = total.astype(out_ref.dtype)
        copies.append(
            pltpu.make_async_copy(
                block.at[j, pl.ds(i * chip_rows, chip_rows), :],
                out_ref.at[pl.ds(pl.multiple_of(first, chip_rows), chip_rows), pl.ds(j * columns, columns)],
                sems.at[j, i],
            )
        )
        copies[-1].start()
    return copies


def finish_kernel(distances, n, adapters, live, *refs):
    *bases, spread, up_ref, out_ref, block, sems = refs
    chip_rows = 2 * spread.shape[1]
    place = [(base, k * chip_rows) for base in bases for k in range(base.shape[0] // chip_rows)]
    copies = []
    for j in range(block.shape[0]):
        columns = slice(j * block.shape[2], (j + 1) * block.shape[2])

        def base_of(i):
            base, row = place[i]
            return base[row : row + chip_rows, columns]

        copies += finish_tile(distances, n, adapters, live, spread, up_ref, out_ref, block, sems, j, base_of)
    for copy in copies:
        copy.wait()


def last_kernel(distances, n, adapters, live, *refs):
    *pairs, spread, w_ref, up_ref, _, out_ref, block, sems, held = refs
    rows = spread.shape[1]
    assemble(list(zip(pairs[::2], pairs[1::2])), rows, held)
    copies = []
    for j in range(block.shape[0]):
        columns = slice(j * block.shape[2], (j + 1) * block.shape[2])
        base = jnp.dot(held[...], w_ref[:, columns], preferred_element_type=jnp.float32)

        def base_of(i):
            return base[2 * i * rows : 2 * (i + 1) * rows]

        copies += finish_tile(distances, n, adapters, live, spread, up_ref, out_ref, block, sems, j, base_of)
    for copy in copies:
        copy.wait()


def finish(kernel, distances, n, scalars, arrays, others, into, rows, width, scratch=(), flops=0):
    columns = tile_width(width)
    total = 2 * rows * len(distances)
    operands = len(scalars) + len(arrays)

    def body(*refs):
        refs = refs[:operands] + refs[operands + len(others) :]
        kernel(distances, n, *refs)

    return pl.pallas_call(
        body,
        out_shape=jax.ShapeDtypeStruct((2 * n * rows, width), jnp.bfloat16),
        in_specs=[pl.BlockSpec(memory_space=pltpu.SMEM)] * len(scalars)
        + whole(len(arrays))
        + [pl.BlockSpec(memory_space=pl.ANY)] * (len(others) + len(into)),
        out_specs=pl.BlockSpec(memory_space=pl.ANY),
        scratch_shapes=[
            pltpu.VMEM((width // columns, total, columns), jnp.bfloat16),
            pltpu.SemaphoreType.DMA((width // columns, len(distances))),
            *scratch,
        ],
        input_output_aliases={operands + len(others): 0} if into else {},
        compiler_params=pltpu.CompilerParams(vmem_limit_bytes=12 << 20),
        cost_estimate=pl.CostEstimate(flops=flops, bytes_accessed=2 * total * width, transcendentals=0),
    )(*scalars, *in_vmem(arrays), *others, *into)


def on_device(n, tokens, weight, down, up, adapter_per_block, rows_per_block):
    rows, features = tokens.shape
    depth = features // CHUNKS
    held, width, rank = down.shape
    half, last = rank // 2, n // 2
    adapters = adapter_per_block[:, 0]
    ring = Ring([tokens[:, k * depth : (k + 1) * depth] for k in range(CHUNKS)], n)
    part = ((held, half, width), jnp.bfloat16)
    keep, give = call(split_kernel, [], [jnp.swapaxes(down, 1, 2)], [], [part, part])
    give = swap_cores(give, n)
    weight, up = load(weight, up)
    arrived = [tokens, ring.hop(1, [weight])]
    pairs = [(x, swap_cores(x, n)) for x in arrived]

    (picks,) = call(
        functools.partial(pick_kernel, 2 * rows),
        [adapters],
        [keep, give],
        [arrived[1]],
        [((n, half, width), jnp.bfloat16)],
    )
    parts = lax.all_to_all(picks, "seq", 0, 0, tiled=True)
    arrived.append(ring.hop(2, [picks]))
    bases = [base_rows(pairs, 3, rows, weight, [picks])]
    (spread,) = call(
        shrink_kernel,
        [],
        [*pairs[0], parts],
        [arrived[2], *bases],
        [((2 * n, rows, 2 * rank), jnp.bfloat16)],
        [pltpu.VMEM((2 * rows, features), jnp.bfloat16), pltpu.VMEM((half, features), jnp.bfloat16)],
    )
    done = spread
    spread = lax.all_to_all(spread, AXES, 0, 0, tiled=True)
    for hop in range(3, last + 1):
        pairs.append((arrived[hop - 1], swap_cores(arrived[hop - 1], n)))
        arrived.append(ring.hop(hop, [done, *bases[-1:]]))
        if hop < last:
            bases.append(base_rows(pairs[-1:], 2, rows, weight, [arrived[hop], bases[-1]]))
        done = spread
    pairs.append((arrived[last], swap_cores(arrived[last], n)))
    early = [d for hop in range(last - 1) for d in hop_distances(hop, n)]
    late = hop_distances(last - 1, n) + hop_distances(last, n)
    scalars = [adapters, rows_per_block]
    out = finish(
        finish_kernel, early, n, scalars, [*bases, spread, up], [arrived[last]], [], rows, weight.shape[1]
    )
    return finish(
        last_kernel,
        late,
        n,
        scalars,
        [*pairs[last - 1], *pairs[last], spread, weight, up],
        [],
        [out],
        rows,
        weight.shape[1],
        [pltpu.VMEM((2 * rows * len(late), features), jnp.bfloat16)],
        4 * rows * len(late) * weight.size,
    )


def solution(mesh):
    placed = (
        P(("groups", "seq", "adapter"), None),
        P(None, ("seq", "adapter")),
        P(("groups", "adapter"), "seq", None),
        P("groups", None, ("seq", "adapter")),
        P("groups", None),
        P("groups"),
    )
    return jax.shard_map(
        functools.partial(on_device, mesh.shape["seq"]),
        mesh=mesh,
        in_specs=placed,
        out_specs=P("groups", ("seq", "adapter")),
        check_vma=False,
    )
```

```python
import functools

import jax
import jax.numpy as jnp
from jax import lax
from jax.experimental import pallas as pl
from jax.experimental.pallas import tpu as pltpu
from jax.sharding import PartitionSpec as P

BLOCK = 128
AXES = ("seq", "adapter")
CHUNKS = 2


def ring_perm(n, way):
    order = [2 * z for z in range(n // 2)] + [2 * z + 1 for z in reversed(range(n // 2))]
    return [(2 * s + c, 2 * order[(pos + way) % n] + c) for pos, s in enumerate(order) for c in range(2)]


def swap_cores(x, n):
    return lax.ppermute(x, AXES, [(2 * s + c, 2 * s + 1 - c) for s in range(n) for c in range(2)])


def chip_at(distance, n):
    s = lax.axis_index("seq")
    z = s >> 1
    pos = jnp.where(s & 1 == 0, z, n - 1 - z) + distance
    pos = jnp.where(pos >= n, pos - n, pos)
    pos = jnp.where(pos < 0, pos + n, pos)
    return jnp.where(pos < n // 2, 2 * pos, 2 * (n - 1 - pos) + 1)


def y_perm(n):
    return [(2 * s + c, 2 * (s ^ 1) + c) for s in range(n) for c in range(2)]


def z_perm(n, shift):
    nz = n // 2
    return [
        (2 * (2 * z + y) + c, 2 * (2 * ((z - shift) % nz) + y) + c)
        for z in range(nz)
        for y in range(2)
        for c in range(2)
    ]


def hop_distances(hop, n):
    if hop == 0:
        return [0]
    return [-hop, hop] if hop < n // 2 else [hop]


class Ring:
    def __init__(self, chunks, n):
        self.n, self.up, self.down = n, list(chunks), list(chunks)

    def hop(self, hop):
        n = self.n
        if hop < n // 2:
            self.up = [lax.ppermute(x, AXES, ring_perm(n, 1)) for x in self.up]
            self.down = [lax.ppermute(x, AXES, ring_perm(n, -1)) for x in self.down]
            return self.up + self.down
        return [
            lax.ppermute((self.down if k % 2 else self.up)[k], AXES, ring_perm(n, -1 if k % 2 else 1))
            for k in range(CHUNKS)
        ]


def join_kernel(*refs):
    *pieces, out = refs
    rows = pieces[0].shape[0]
    for i, piece in enumerate(pieces):
        out[i * rows : (i + 1) * rows, :] = piece[...]


def join(pieces, after):
    rows, depth = pieces[0].shape
    (joined,) = call(join_kernel, [], pieces, after, [((rows * len(pieces), depth), pieces[0].dtype)])
    return joined


def whole(count):
    return [pl.BlockSpec(memory_space=pltpu.VMEM)] * count


def in_vmem(arrays):
    return [pltpu.with_memory_space_constraint(x, pltpu.VMEM) for x in arrays]


def call(kernel, scalars, arrays, after, outs, scratch=(), limit=8, flops=0):
    operands = len(scalars) + len(arrays)

    def body(*refs):
        kernel(*refs[:operands], *refs[operands + len(after) :])

    return pl.pallas_call(
        body,
        out_shape=[pltpu.VMEM(shape, dtype) for shape, dtype in outs],
        in_specs=[pl.BlockSpec(memory_space=pltpu.SMEM)] * len(scalars)
        + whole(len(arrays))
        + [pl.BlockSpec(memory_space=pl.ANY)] * len(after),
        out_specs=whole(len(outs)),
        scratch_shapes=list(scratch),
        compiler_params=pltpu.CompilerParams(vmem_limit_bytes=limit << 20),
        cost_estimate=pl.CostEstimate(flops=flops, bytes_accessed=0, transcendentals=0),
    )(*scalars, *in_vmem(arrays), *after)


class Window:
    def __init__(self, n, width, depth):
        self.width, self.depth = width, depth
        self.size = -(-(width + max(s * width % 128 for s in range(n))) // 128) * 128
        for s in range(n):
            start = s * width // 128 * 128
            assert start // depth == (start + self.size - 1) // depth

    def start(self, chip):
        return (chip * self.width) >> 7 << 7

    def shift(self, chip):
        return chip * self.width - self.start(chip)


def prepare_kernel(n, window, distances, tokens, down, factor, *sends):
    s = lax.axis_index("seq")
    zeros = jnp.zeros((down.shape[1], window.size - window.width), jnp.float32)
    for index in range(down.shape[0]):
        wide = jnp.concatenate([down[index], zeros], 1)
        factor[index] = pltpu.roll(wide, window.shift(s), 1).astype(jnp.bfloat16)
    for distance, send in zip(distances, sends):
        start = pl.multiple_of(window.start(chip_at(distance, n)), 128)
        send[...] = tokens[:, pl.ds(start, window.size)]


def pack(parts, out):
    chips, rows, rank = parts.shape
    for t in range(chips):
        i, k = t % (chips // 2), t // (chips // 2)
        out[i * rows : (i + 1) * rows, k * rank : (k + 1) * rank] = parts[t].astype(out.dtype)


def partial_kernel(n, window, groups, opposite, adapters, *refs):
    *pieces, factor, other, received, total, rounded, parts = refs
    s, c = lax.axis_index("seq"), lax.axis_index("adapter")
    rows, held = received.shape[0], factor.shape[0]
    start = window.start(s)
    chunk = jnp.where(start >= window.depth, 1, 0)
    inside = pl.multiple_of(start - chunk * window.depth, 128)
    found = []
    for piece, distances in zip(pieces, groups):
        for i, distance in enumerate(distances):
            row = pl.multiple_of((i * CHUNKS + chunk) * rows, rows)
            found.append((distance, piece[pl.ds(row, rows), pl.ds(inside, window.size)]))
    for distance, x in [*found, (opposite, received[...])]:
        chip = chip_at(distance, n)
        adapter = adapters[chip * 2 * rows // BLOCK]
        index = lax.rem(adapter, held)
        mine = (adapter >= c * held) & (adapter < (c + 1) * held)
        weights = jnp.where(mine, factor[index], other[index])
        parts[chip] = lax.dot_general(x, weights, (((1,), (1,)), ((), ())), preferred_element_type=jnp.float32)
    pack(parts, total)
    rounded[...] = total[...].astype(jnp.bfloat16)


def add_kernel(total, *refs):
    *received, out, rounded = refs
    value = total[...]
    for x in received:
        value += x[...].astype(jnp.float32)
    out[...] = value
    rounded[...] = value.astype(jnp.bfloat16)


def load_kernel(chunk, w_ref, *refs):
    *up_refs, sems = refs
    w_out = up_refs.pop(1 if len(up_refs) > 1 else 0)
    parts = sems.shape[0] - 1
    depth = w_out.shape[0] // parts
    first = chunk * w_out.shape[0]
    copies = [
        pltpu.make_async_copy(
            w_ref.at[pl.ds(first + k * depth, depth), :], w_out.at[pl.ds(k * depth, depth), :], sems.at[k]
        )
        for k in range(parts)
    ]
    if up_refs:
        up_ref, up_out, held = up_refs
        up_copy = pltpu.make_async_copy(up_ref, held, sems.at[parts])
        up_copy.start()
    for copy in copies:
        copy.start()
    if up_refs:
        up_copy.wait()
        up_out[...] = held[...].astype(jnp.bfloat16)
    for copy in copies:
        copy.wait()


def load(weight, chunk, up=None):
    depth, width = weight.shape[0] // CHUNKS, weight.shape[1]
    ups = [] if up is None else [up]
    return pl.pallas_call(
        functools.partial(load_kernel, chunk),
        out_shape=[pltpu.VMEM((depth, width), weight.dtype)] + [pltpu.VMEM(x.shape, jnp.bfloat16) for x in ups],
        in_specs=[pl.BlockSpec(memory_space=pltpu.HBM)] * (1 + len(ups)),
        out_specs=whole(1 + len(ups)),
        scratch_shapes=[pltpu.VMEM(x.shape, x.dtype) for x in ups] + [pltpu.SemaphoreType.DMA((5,))],
        compiler_params=pltpu.CompilerParams(vmem_limit_bytes=8 << 20),
        cost_estimate=pl.CostEstimate(flops=0, bytes_accessed=2 * depth * width, transcendentals=0),
    )(*(pltpu.with_memory_space_constraint(x, pltpu.HBM) for x in [weight, *ups]))


def assemble(pairs, rows, held):
    width = held.shape[1]
    c = lax.axis_index("adapter")
    first = 0
    for pair in pairs:
        depth = pair[0].shape[1]
        chunks = width // depth
        for chip in range(pair[0].shape[0] // (rows * chunks)):
            for k in range(chunks):
                at = (chip * chunks + k) * rows
                for ref, core in zip(pair, (c, 1 - c)):
                    row = pl.multiple_of(first + core * rows, rows)
                    held[pl.ds(row, rows), k * depth : (k + 1) * depth] = ref[at : at + rows, :]
            first += 2 * rows


def tile_width(width):
    return 768 if width % 768 == 0 else width


def multiply(held, weights, at):
    depth = weights[0].shape[0]
    return sum(
        jnp.dot(held[:, k * depth : (k + 1) * depth], w[:, at], preferred_element_type=jnp.float32)
        for k, w in enumerate(weights)
    )


def base_kernel(rows, count, *refs):
    pairs, weights, (base, held) = refs[:count], refs[count : count + CHUNKS], refs[count + CHUNKS :]
    assemble(list(zip(pairs[::2], pairs[1::2])), rows, held)
    width = base.shape[1]
    columns = tile_width(width)
    for j in range(0, width, columns):
        at = slice(j, j + columns)
        base[:, at] = multiply(held, weights, at)


def base_rows(pairs, chips, rows, weights, after):
    total, depth, width = 2 * rows * chips, CHUNKS * weights[0].shape[0], weights[0].shape[1]
    arrays = [x for pair in pairs for x in pair]
    (base,) = call(
        functools.partial(base_kernel, rows, len(arrays)),
        [],
        arrays + weights,
        after,
        [((total, width), jnp.float32)],
        [pltpu.VMEM((total, depth), jnp.bfloat16)],
        limit=8 + (2 * total * depth >> 20),
        flops=2 * total * depth * width,
    )
    return base


def finish_kernel(n, rows, groups, adapters, live, *refs):
    *bases, own, other, up_ref, out_ref, shrink, block, sems = refs
    c = lax.axis_index("adapter")
    chip_rows, rank = 2 * rows, up_ref.shape[1]
    tiles, _, columns = block.shape
    for t in range(n):
        i, k = t % (n // 2), t // (n // 2)
        for ref, core in ((own, c), (other, 1 - c)):
            part = ref[i * rows : (i + 1) * rows, k * rank : (k + 1) * rank]
            shrink[t, pl.ds(pl.multiple_of(core * rows, rows), rows), :] = part.astype(jnp.bfloat16)
    places = [
        (distance, base, i * chip_rows)
        for base, distances in zip(bases, groups)
        for i, distance in enumerate(distances)
    ]
    copies = []
    for j in range(tiles):
        at = slice(j * columns, (j + 1) * columns)
        for i, (distance, base, row) in enumerate(places):
            chip = chip_at(distance, n)
            first = chip * chip_rows
            of_block = first // BLOCK
            delta = jnp.dot(shrink[chip], up_ref[adapters[of_block], :, at], preferred_element_type=jnp.float32)
            index = lax.broadcasted_iota(jnp.int32, delta.shape, 0) + (first - of_block * BLOCK)
            total = jnp.where(index < live[of_block], base[row : row + chip_rows, at] + delta, 0.0)
            place = pl.ds(i * chip_rows, chip_rows)
            block[j, place, :] = total.astype(out_ref.dtype)
            copies.append(
                pltpu.make_async_copy(
                    block.at[j, place, :],
                    out_ref.at[pl.ds(pl.multiple_of(first, chip_rows), chip_rows), pl.ds(j * columns, columns)],
                    sems.at[j, i],
                )
            )
            copies[-1].start()
    for copy in copies:
        copy.wait()


def finish(n, rows, groups, scalars, bases, own, other, up):
    rank, width = up.shape[1:]
    total, columns = 2 * n * rows, tile_width(width)
    arrays = [*bases, own, other, up]
    return pl.pallas_call(
        functools.partial(finish_kernel, n, rows, groups),
        out_shape=jax.ShapeDtypeStruct((total, width), jnp.bfloat16),
        in_specs=[pl.BlockSpec(memory_space=pltpu.SMEM)] * len(scalars) + whole(len(arrays)),
        out_specs=pl.BlockSpec(memory_space=pl.ANY),
        scratch_shapes=[
            pltpu.VMEM((n, 2 * rows, rank), jnp.bfloat16),
            pltpu.VMEM((width // columns, total, columns), jnp.bfloat16),
            pltpu.SemaphoreType.DMA((width // columns, n)),
        ],
        compiler_params=pltpu.CompilerParams(vmem_limit_bytes=8 << 20),
        cost_estimate=pl.CostEstimate(
            flops=2 * total * rank * width, bytes_accessed=2 * total * width, transcendentals=0
        ),
    )(*scalars, *in_vmem(arrays))


def on_device(n, tokens, weight, down, up, adapter_per_block, rows_per_block):
    rows, features = tokens.shape
    depth = features // CHUNKS
    held, width, rank = down.shape
    last = n // 2
    adapters = adapter_per_block[:, 0]
    window = Window(n, width, depth)
    early = [d for hop in range(last - 1) for d in hop_distances(hop, n)]
    late = hop_distances(last - 1, n)

    chunks = [tokens[:, k * depth : (k + 1) * depth] for k in range(CHUNKS)]
    ring = Ring(chunks, n)
    factor, send = call(
        functools.partial(prepare_kernel, n, window, [last]),
        [],
        [tokens, jnp.swapaxes(down, 1, 2)],
        [],
        [((held, rank, window.size), jnp.bfloat16), ((rows, window.size), jnp.bfloat16)],
    )
    received = lax.ppermute(send, AXES, ring_perm(n, last))
    other_factor = swap_cores(factor, n)
    weights, (last_weight, up) = [load(weight, k)[0] for k in range(CHUNKS - 1)], load(weight, CHUNKS - 1, up)
    weights.append(last_weight)

    pieces = chunks + [x for hop in range(1, last - 1) for x in ring.hop(hop)]
    near = join(pieces, [*weights, received, other_factor])
    far = join(ring.hop(last - 1), [])
    half = (n // 2 * rows, 2 * rank)
    sums = [(half, jnp.float32), (half, jnp.bfloat16)]
    total, rounded = call(
        functools.partial(partial_kernel, n, window, [early, late], last),
        [adapters],
        [near, far, factor, other_factor, received],
        [],
        sums,
        [pltpu.VMEM((n, rows, rank), jnp.float32)],
    )
    bases = [base_rows([(near, swap_cores(near, n))], len(early), rows, weights, [rounded])]
    total, rounded = call(add_kernel, [], [total, lax.ppermute(rounded, AXES, y_perm(n))], [], sums)
    final = join(ring.hop(last), [*bases, rounded])
    total, rounded = call(
        add_kernel,
        [],
        [total] + [lax.ppermute(rounded, AXES, z_perm(n, shift)) for shift in range(1, n // 2)],
        [final],
        sums,
    )
    pairs = [(x, swap_cores(x, n)) for x in (far, final)]
    bases.append(base_rows(pairs, len(late) + 1, rows, weights, [rounded]))
    return finish(
        n,
        rows,
        [early, late + [last]],
        [adapters, rows_per_block],
        bases,
        total,
        swap_cores(rounded, n),
        up,
    )


def solution(mesh):
    placed = (
        P(("groups", "seq", "adapter"), None),
        P(None, ("seq", "adapter")),
        P(("groups", "adapter"), "seq", None),
        P("groups", None, ("seq", "adapter")),
        P("groups", None),
        P("groups"),
    )
    return jax.shard_map(
        functools.partial(on_device, mesh.shape["seq"]),
        mesh=mesh,
        in_specs=placed,
        out_specs=P("groups", ("seq", "adapter")),
        check_vma=False,
    )
```

```python
import functools

import jax
import jax.numpy as jnp
from jax import lax
from jax.experimental import pallas as pl
from jax.experimental.pallas import tpu as pltpu
from jax.sharding import PartitionSpec as P

BLOCK = 128
AXES = ("seq", "adapter")
CHUNKS = 2


def ring_perm(n, way, other_way=None):
    order = [2 * z for z in range(n // 2)] + [2 * z + 1 for z in reversed(range(n // 2))]
    ways = (way, way if other_way is None else other_way)
    return [(2 * s + c, 2 * order[(pos + ways[c]) % n] + c) for pos, s in enumerate(order) for c in range(2)]


def swap_cores(x, n):
    return lax.ppermute(x, AXES, [(2 * s + c, 2 * s + 1 - c) for s in range(n) for c in range(2)])


def chip_at(distance, n):
    s = lax.axis_index("seq")
    z = s >> 1
    pos = jnp.where(s & 1 == 0, z, n - 1 - z) + distance
    pos = jnp.where(pos >= n, pos - n, pos)
    pos = jnp.where(pos < 0, pos + n, pos)
    return jnp.where(pos < n // 2, 2 * pos, 2 * (n - 1 - pos) + 1)


def y_perm(n):
    return [(2 * s + c, 2 * (s ^ 1) + c) for s in range(n) for c in range(2)]


def z_perm(n, shift):
    nz = n // 2
    return [
        (2 * (2 * z + y) + c, 2 * (2 * ((z - shift) % nz) + y) + c)
        for z in range(nz)
        for y in range(2)
        for c in range(2)
    ]


def hop_distances(hop, n):
    if hop == 0:
        return [0]
    return [-hop, hop] if hop < n // 2 else [hop]


def ring_hop(up, down, n):
    return [lax.ppermute(x, AXES, ring_perm(n, 1)) for x in up], [lax.ppermute(x, AXES, ring_perm(n, -1)) for x in down]


def join_kernel(turned, *refs):
    *pieces, out = refs[:-1] if turned else refs
    first = 0
    for piece in pieces:
        out[first : first + piece.shape[0], :] = piece[...]
        first += piece.shape[0]
    if turned:
        c = lax.axis_index("adapter")
        rows = pieces[-1].shape[0]
        for core, begin in enumerate((len(pieces) - 2 * CHUNKS, len(pieces) - CHUNKS)):

            @pl.when(c == core)
            def _():
                for i, piece in enumerate(pieces[begin : begin + CHUNKS]):
                    refs[-1][i * rows : (i + 1) * rows, :] = piece[...]


def join(pieces, after, turned=False):
    (rows, depth), dtype = pieces[-1].shape, pieces[-1].dtype
    outs = [((sum(x.shape[0] for x in pieces), depth), dtype)] + [((CHUNKS * rows, depth), dtype)] * turned
    return call(functools.partial(join_kernel, turned), [], pieces, after, outs)


def whole(count):
    return [pl.BlockSpec(memory_space=pltpu.VMEM)] * count


def in_vmem(arrays):
    return [pltpu.with_memory_space_constraint(x, pltpu.VMEM) for x in arrays]


def call(kernel, scalars, arrays, after, outs, scratch=(), limit=8, flops=0):
    operands = len(scalars) + len(arrays)

    def body(*refs):
        kernel(*refs[:operands], *refs[operands + len(after) :])

    return pl.pallas_call(
        body,
        out_shape=[pltpu.VMEM(shape, dtype) for shape, dtype in outs],
        in_specs=[pl.BlockSpec(memory_space=pltpu.SMEM)] * len(scalars)
        + whole(len(arrays))
        + [pl.BlockSpec(memory_space=pl.ANY)] * len(after),
        out_specs=whole(len(outs)),
        scratch_shapes=list(scratch),
        compiler_params=pltpu.CompilerParams(vmem_limit_bytes=limit << 20),
        cost_estimate=pl.CostEstimate(flops=flops, bytes_accessed=0, transcendentals=0),
    )(*scalars, *in_vmem(arrays), *after)


class Window:
    def __init__(self, n, width, depth):
        self.width, self.depth = width, depth
        self.size = -(-(width + max(s * width % 128 for s in range(n))) // 128) * 128
        for s in range(n):
            start = s * width // 128 * 128
            assert start // depth == (start + self.size - 1) // depth

    def start(self, chip):
        return (chip * self.width) >> 7 << 7

    def shift(self, chip):
        return chip * self.width - self.start(chip)


def prepare_kernel(n, window, distances, tokens, down, factor, *sends):
    s = lax.axis_index("seq")
    zeros = jnp.zeros((down.shape[1], window.size - window.width), jnp.float32)
    for index in range(down.shape[0]):
        wide = jnp.concatenate([down[index], zeros], 1)
        factor[index] = pltpu.roll(wide, window.shift(s), 1).astype(jnp.bfloat16)
    for distance, send in zip(distances, sends):
        start = pl.multiple_of(window.start(chip_at(distance, n)), 128)
        send[...] = tokens[:, pl.ds(start, window.size)]


def near_kernel(tokens, behind, ahead, factor, out, *chunks):
    held, rank, size = factor.shape
    rows, depth = chunks[0].shape
    for i, ref in enumerate((tokens, behind, ahead)):
        for k in range(CHUNKS):
            piece = ref[:, k * depth : (k + 1) * depth]
            at = (i * CHUNKS + k) * rows
            out[at : at + rows, :] = piece
            if i:
                chunks[(i - 1) * CHUNKS + k][...] = piece
    first = 3 * CHUNKS * rows
    out[first:, :] = jnp.zeros((rank, depth), out.dtype)
    for index in range(held):
        out[first:, index * size : (index + 1) * size] = factor[index]


def pack(parts, out):
    chips, rows, rank = parts.shape
    for t in range(chips):
        i, k = t % (chips // 2), t // (chips // 2)
        out[i * rows : (i + 1) * rows, k * rank : (k + 1) * rank] = parts[t].astype(out.dtype)


def partial_kernel(n, window, groups, far, adapters, *refs):
    *pieces, factor, other, total, rounded, parts = refs
    pieces, received = pieces[: len(groups)], pieces[len(groups) :]
    s, c = lax.axis_index("seq"), lax.axis_index("adapter")
    rows, size = received[0].shape
    held, rank, _ = factor.shape
    start = window.start(s)
    chunk = jnp.where(start >= window.depth, 1, 0)
    inside = pl.multiple_of(start - chunk * window.depth, 128)
    found = []
    for piece, distances in zip(pieces, groups):
        for i, distance in enumerate(distances):
            row = pl.multiple_of((i * CHUNKS + chunk) * rows, rows)
            found.append((distance, piece[pl.ds(row, rows), pl.ds(inside, size)]))
    found += [(distance, x[...]) for distance, x in zip(far, received)]
    below = other.shape[0] - rank
    for distance, x in found:
        chip = chip_at(distance, n)
        adapter = adapters[chip * 2 * rows // BLOCK]
        index = lax.rem(adapter, held)
        mine = (adapter >= c * held) & (adapter < (c + 1) * held)
        theirs = other[below:, pl.ds(pl.multiple_of(index * size, 128), size)]
        weights = jnp.where(mine, factor[index], theirs)
        parts[chip] = lax.dot_general(x, weights, (((1,), (1,)), ((), ())), preferred_element_type=jnp.float32)
    pack(parts, total)
    rounded[...] = total[...].astype(jnp.bfloat16)


def add_kernel(total, *refs):
    *received, out, rounded = refs
    value = total[...]
    for x in received:
        value += x[...].astype(jnp.float32)
    out[...] = value
    rounded[...] = value.astype(jnp.bfloat16)


def load_kernel(chunk, w_ref, *refs):
    *up_refs, sems = refs
    w_out = up_refs.pop(1 if len(up_refs) > 1 else 0)
    parts = sems.shape[0] - 1
    depth = w_out.shape[0] // parts
    first = chunk * w_out.shape[0]
    copies = [
        pltpu.make_async_copy(
            w_ref.at[pl.ds(first + k * depth, depth), :], w_out.at[pl.ds(k * depth, depth), :], sems.at[k]
        )
        for k in range(parts)
    ]
    if up_refs:
        up_ref, up_out, held = up_refs
        up_copy = pltpu.make_async_copy(up_ref, held, sems.at[parts])
        up_copy.start()
    for copy in copies:
        copy.start()
    if up_refs:
        up_copy.wait()
        up_out[...] = held[...].astype(jnp.bfloat16)
    for copy in copies:
        copy.wait()


def load(weight, chunk, up=None):
    depth, width = weight.shape[0] // CHUNKS, weight.shape[1]
    ups = [] if up is None else [up]
    return pl.pallas_call(
        functools.partial(load_kernel, chunk),
        out_shape=[pltpu.VMEM((depth, width), weight.dtype)] + [pltpu.VMEM(x.shape, jnp.bfloat16) for x in ups],
        in_specs=[pl.BlockSpec(memory_space=pltpu.HBM)] * (1 + len(ups)),
        out_specs=whole(1 + len(ups)),
        scratch_shapes=[pltpu.VMEM(x.shape, x.dtype) for x in ups] + [pltpu.SemaphoreType.DMA((5,))],
        compiler_params=pltpu.CompilerParams(vmem_limit_bytes=8 << 20),
        cost_estimate=pl.CostEstimate(flops=0, bytes_accessed=2 * depth * width, transcendentals=0),
    )(*(pltpu.with_memory_space_constraint(x, pltpu.HBM) for x in [weight, *ups]))


def assemble(pairs, counts, rows, held):
    c = lax.axis_index("adapter")
    first = 0
    for pair, (begin, end) in zip(pairs, counts):
        depth = pair[0].shape[1]
        for chip in range(begin, end):
            for k in range(CHUNKS):
                at = (chip * CHUNKS + k) * rows
                for ref, core in zip(pair, (c, 1 - c)):
                    row = pl.multiple_of(first + core * rows, rows)
                    held[pl.ds(row, rows), k * depth : (k + 1) * depth] = ref[at : at + rows, :]
            first += 2 * rows


def tile_width(width):
    return 768 if width % 768 == 0 else width


def multiply(held, weights, at):
    depth = weights[0].shape[0]
    return sum(
        jnp.dot(held[:, k * depth : (k + 1) * depth], w[:, at], preferred_element_type=jnp.float32)
        for k, w in enumerate(weights)
    )


def base_kernel(rows, counts, *refs):
    count = 2 * len(counts)
    pairs, weights, (base, held) = refs[:count], refs[count : count + CHUNKS], refs[count + CHUNKS :]
    assemble(list(zip(pairs[::2], pairs[1::2])), counts, rows, held)
    width = base.shape[1]
    columns = tile_width(width)
    for j in range(0, width, columns):
        at = slice(j, j + columns)
        base[:, at] = multiply(held, weights, at)


def base_rows(pairs, counts, rows, weights, after):
    chips = sum(end - begin for begin, end in counts)
    total, depth, width = 2 * rows * chips, CHUNKS * weights[0].shape[0], weights[0].shape[1]
    arrays = [x for pair in pairs for x in pair]
    (base,) = call(
        functools.partial(base_kernel, rows, counts),
        [],
        arrays + weights,
        after,
        [((total, width), jnp.float32)],
        [pltpu.VMEM((total, depth), jnp.bfloat16)],
        limit=8 + (2 * total * depth >> 20),
        flops=2 * total * depth * width,
    )
    return base


def finish_kernel(n, rows, groups, adapters, live, *refs):
    *bases, own, other, up_ref, out_ref, shrink, block, sems = refs
    c = lax.axis_index("adapter")
    chip_rows, rank = 2 * rows, up_ref.shape[1]
    tiles, _, columns = block.shape
    for t in range(n):
        i, k = t % (n // 2), t // (n // 2)
        for ref, core in ((own, c), (other, 1 - c)):
            part = ref[i * rows : (i + 1) * rows, k * rank : (k + 1) * rank]
            shrink[t, pl.ds(pl.multiple_of(core * rows, rows), rows), :] = part.astype(jnp.bfloat16)
    places = [
        (distance, base, i * chip_rows)
        for base, distances in zip(bases, groups)
        for i, distance in enumerate(distances)
    ]
    copies = []
    for j in range(tiles):
        at = slice(j * columns, (j + 1) * columns)
        for i, (distance, base, row) in enumerate(places):
            chip = chip_at(distance, n)
            first = chip * chip_rows
            of_block = first // BLOCK
            delta = jnp.dot(shrink[chip], up_ref[adapters[of_block], :, at], preferred_element_type=jnp.float32)
            index = lax.broadcasted_iota(jnp.int32, delta.shape, 0) + (first - of_block * BLOCK)
            total = jnp.where(index < live[of_block], base[row : row + chip_rows, at] + delta, 0.0)
            place = pl.ds(i * chip_rows, chip_rows)
            block[j, place, :] = total.astype(out_ref.dtype)
            copies.append(
                pltpu.make_async_copy(
                    block.at[j, place, :],
                    out_ref.at[pl.ds(pl.multiple_of(first, chip_rows), chip_rows), pl.ds(j * columns, columns)],
                    sems.at[j, i],
                )
            )
            copies[-1].start()
    for copy in copies:
        copy.wait()


def finish(n, rows, groups, scalars, bases, own, other, up):
    rank, width = up.shape[1:]
    total, columns = 2 * n * rows, tile_width(width)
    arrays = [*bases, own, other, up]
    return pl.pallas_call(
        functools.partial(finish_kernel, n, rows, groups),
        out_shape=jax.ShapeDtypeStruct((total, width), jnp.bfloat16),
        in_specs=[pl.BlockSpec(memory_space=pltpu.SMEM)] * len(scalars) + whole(len(arrays)),
        out_specs=pl.BlockSpec(memory_space=pl.ANY),
        scratch_shapes=[
            pltpu.VMEM((n, 2 * rows, rank), jnp.bfloat16),
            pltpu.VMEM((width // columns, total, columns), jnp.bfloat16),
            pltpu.SemaphoreType.DMA((width // columns, n)),
        ],
        compiler_params=pltpu.CompilerParams(vmem_limit_bytes=8 << 20),
        cost_estimate=pl.CostEstimate(
            flops=2 * total * rank * width, bytes_accessed=2 * total * width, transcendentals=0
        ),
    )(*scalars, *in_vmem(arrays))


def on_device(n, tokens, weight, down, up, adapter_per_block, rows_per_block):
    rows, features = tokens.shape
    depth = features // CHUNKS
    held, width, rank = down.shape
    last = n // 2
    adapters = adapter_per_block[:, 0]
    window = Window(n, width, depth)
    near, mid, far = ([d for hop in hops for d in hop_distances(hop, n)] for hops in ((0, 1), range(2, last - 1), [last - 1]))
    half = (n // 2 * rows, 2 * rank)
    sums = [(half, jnp.float32), (half, jnp.bfloat16)]

    (behind,), (ahead,) = ring_hop([tokens], [tokens], n)
    ends = far + [last]
    columns = ((rows, window.size), jnp.bfloat16)
    factor, *sends = call(
        functools.partial(prepare_kernel, n, window, ends),
        [],
        [tokens, jnp.swapaxes(down, 1, 2)],
        [],
        [((held, rank, window.size), jnp.bfloat16)] + [columns] * len(ends),
    )
    received = [lax.ppermute(x, AXES, ring_perm(n, d)) for d, x in zip(ends, sends)]
    come_from = [-d for d in far] + [last]
    weights = [load(weight, k)[0] for k in range(CHUNKS - 1)]
    piece = ((rows, depth), jnp.bfloat16)
    near_rows, *chunks = call(
        near_kernel,
        [],
        [tokens, behind, ahead, factor],
        [*weights, *received],
        [((3 * CHUNKS * rows + rank, depth), jnp.bfloat16)] + [piece] * (2 * CHUNKS),
    )

    up_way, down_way = chunks[:CHUNKS], chunks[CHUNKS:]
    near_pair = (near_rows, swap_cores(near_rows, n))
    last_weight, up = load(weight, CHUNKS - 1, up)
    weights.append(last_weight)
    arrived = []
    for _ in range(2, last - 1):
        up_way, down_way = ring_hop(up_way, down_way, n)
        arrived += up_way + down_way
    (mid_rows,) = join(arrived, [last_weight])

    total, rounded = call(
        functools.partial(partial_kernel, n, window, [near, mid], come_from),
        [adapters],
        [near_rows, mid_rows, *received, factor, near_pair[1]],
        [],
        sums,
        [pltpu.VMEM((n, rows, rank), jnp.float32)],
    )
    total, rounded = call(add_kernel, [], [total, lax.ppermute(rounded, AXES, y_perm(n))], [], sums)
    bases = [base_rows([near_pair], [(0, len(near))], rows, weights, [mid_rows])]
    up_way, down_way = ring_hop(up_way, down_way, n)
    far_rows, turned = join([mid_rows, *up_way, *down_way], [*bases, rounded], True)

    far_pair = (far_rows, swap_cores(far_rows, n))
    total, rounded = call(
        add_kernel,
        [],
        [total] + [lax.ppermute(rounded, AXES, z_perm(n, shift)) for shift in range(1, n // 2)],
        [],
        sums,
    )
    (last_rows,) = join([lax.ppermute(turned, AXES, ring_perm(n, 1, -1))], [rounded])

    cut = len(mid)
    bases.append(base_rows([far_pair], [(0, cut)], rows, weights, [last_rows]))
    pairs = [far_pair, (last_rows, swap_cores(last_rows, n))]
    bases.append(base_rows(pairs, [(cut, cut + len(far)), (0, 1)], rows, weights, [bases[-1]]))
    return finish(
        n,
        rows,
        [near, mid, far + [last]],
        [adapters, rows_per_block],
        bases,
        total,
        swap_cores(rounded, n),
        up,
    )


def solution(mesh):
    placed = (
        P(("groups", "seq", "adapter"), None),
        P(None, ("seq", "adapter")),
        P(("groups", "adapter"), "seq", None),
        P("groups", None, ("seq", "adapter")),
        P("groups", None),
        P("groups"),
    )
    return jax.shard_map(
        functools.partial(on_device, mesh.shape["seq"]),
        mesh=mesh,
        in_specs=placed,
        out_specs=P("groups", ("seq", "adapter")),
        check_vma=False,
    )
```

```python
import functools

import jax
import jax.numpy as jnp
from jax import lax
from jax.experimental import pallas as pl
from jax.experimental.pallas import tpu as pltpu
from jax.sharding import PartitionSpec as P

BLOCK = 128
AXES = ("seq", "adapter")
CHUNKS = 2


def ring_perm(n, way, other_way=None):
    order = [2 * z for z in range(n // 2)] + [2 * z + 1 for z in reversed(range(n // 2))]
    ways = (way, way if other_way is None else other_way)
    return [(2 * s + c, 2 * order[(pos + ways[c]) % n] + c) for pos, s in enumerate(order) for c in range(2)]


def swap_cores(x, n):
    return lax.ppermute(x, AXES, [(2 * s + c, 2 * s + 1 - c) for s in range(n) for c in range(2)])


def chip_at(distance, n):
    s = lax.axis_index("seq")
    z = s >> 1
    pos = jnp.where(s & 1 == 0, z, n - 1 - z) + distance
    pos = jnp.where(pos >= n, pos - n, pos)
    pos = jnp.where(pos < 0, pos + n, pos)
    return jnp.where(pos < n // 2, 2 * pos, 2 * (n - 1 - pos) + 1)


def y_perm(n):
    return [(2 * s + c, 2 * (s ^ 1) + c) for s in range(n) for c in range(2)]


def z_perm(n, shift):
    nz = n // 2
    return [
        (2 * (2 * z + y) + c, 2 * (2 * ((z - shift) % nz) + y) + c)
        for z in range(nz)
        for y in range(2)
        for c in range(2)
    ]


def hop_distances(hop, n):
    if hop == 0:
        return [0]
    return [-hop, hop] if hop < n // 2 else [hop]


def ring_hop(up, down, n):
    return [lax.ppermute(x, AXES, ring_perm(n, 1)) for x in up], [lax.ppermute(x, AXES, ring_perm(n, -1)) for x in down]


def join_kernel(ways, *refs):
    count = len(refs) - 1 - (2 * CHUNKS if ways == 2 else ways)
    pieces, out, on = refs[:count], refs[count], refs[count + 1 :]
    first = 0
    for piece in pieces:
        out[first : first + piece.shape[0], :] = piece[...]
        first += piece.shape[0]
    arrived = pieces[len(pieces) - 2 * CHUNKS :]
    if ways == 2:
        for piece, ref in zip(arrived, on):
            ref[...] = piece[...]
    if ways == 1:
        c = lax.axis_index("adapter")
        rows = arrived[0].shape[0]
        for core in range(2):

            @pl.when(c == core)
            def _():
                for i, piece in enumerate(arrived[core * CHUNKS : (core + 1) * CHUNKS]):
                    on[0][i * rows : (i + 1) * rows, :] = piece[...]


def join(pieces, after, ways=0):
    (rows, depth), dtype = pieces[-1].shape, pieces[-1].dtype
    on = {0: [], 1: [CHUNKS * rows], 2: [rows] * 2 * CHUNKS}[ways]
    outs = [((count, depth), dtype) for count in [sum(x.shape[0] for x in pieces), *on]]
    return call(functools.partial(join_kernel, ways), pieces, after, outs)


def whole(count):
    return [pl.BlockSpec(memory_space=pltpu.VMEM)] * count


def in_vmem(arrays):
    return [pltpu.with_memory_space_constraint(x, pltpu.VMEM) for x in arrays]


def call(kernel, arrays, after, outs, scratch=(), limit=8, flops=0, outside=()):
    operands = len(arrays) + len(outside)

    def body(*refs):
        kernel(*refs[:operands], *refs[operands + len(after) :])

    return pl.pallas_call(
        body,
        out_shape=[pltpu.VMEM(shape, dtype) for shape, dtype in outs],
        in_specs=whole(len(arrays)) + [pl.BlockSpec(memory_space=pl.ANY)] * (len(outside) + len(after)),
        out_specs=whole(len(outs)),
        scratch_shapes=list(scratch),
        compiler_params=pltpu.CompilerParams(vmem_limit_bytes=limit << 20),
        cost_estimate=pl.CostEstimate(flops=flops, bytes_accessed=0, transcendentals=0),
    )(*in_vmem(arrays), *outside, *after)


class Window:
    def __init__(self, n, width, depth):
        self.width, self.depth = width, depth
        self.size = -(-(width + max(s * width % 128 for s in range(n))) // 128) * 128
        for s in range(n):
            start = s * width // 128 * 128
            assert start // depth == (start + self.size - 1) // depth

    def start(self, chip):
        return (chip * self.width) >> 7 << 7

    def shift(self, chip):
        return chip * self.width - self.start(chip)


def near_kernel(tokens, behind, ahead, factor, out, *chunks):
    held, rank, size = factor.shape
    rows, depth = chunks[0].shape
    for i, ref in enumerate((tokens, behind, ahead)):
        for k in range(CHUNKS):
            piece = ref[:, k * depth : (k + 1) * depth]
            at = (i * CHUNKS + k) * rows
            out[at : at + rows, :] = piece
            if i:
                chunks[(i - 1) * CHUNKS + k][...] = piece
    first = 3 * CHUNKS * rows
    out[first:, :] = jnp.zeros((rank, depth), out.dtype)
    for index in range(held):
        out[first:, index * size : (index + 1) * size] = factor[index]


def pack(parts, out):
    chips, rows, rank = parts.shape
    for t in range(chips):
        i, k = t % (chips // 2), t // (chips // 2)
        out[i * rows : (i + 1) * rows, k * rank : (k + 1) * rank] = parts[t].astype(out.dtype)


def partial_kernel(n, window, groups, far, *refs):
    *pieces, factor, other, adapters_ref, total, rounded, adapters, x, products, parts, sem = refs
    lookup = pltpu.make_async_copy(adapters_ref, adapters, sem)
    lookup.start()
    pieces, received = pieces[: len(groups)], pieces[len(groups) :]
    s, c = lax.axis_index("seq"), lax.axis_index("adapter")
    rows, size = received[0].shape
    held, rank, _ = factor.shape
    start = window.start(s)
    chunk = jnp.where(start >= window.depth, 1, 0)
    inside = pl.multiple_of(start - chunk * window.depth, 128)
    order = []
    for piece, distances in zip(pieces, groups):
        for i, distance in enumerate(distances):
            row = pl.multiple_of((i * CHUNKS + chunk) * rows, rows)
            x[len(order) * rows : (len(order) + 1) * rows, :] = piece[pl.ds(row, rows), pl.ds(inside, size)]
            order.append(distance)
    for piece, distance in zip(received, far):
        x[len(order) * rows : (len(order) + 1) * rows, :] = piece[...]
        order.append(distance)
    below = other.shape[0] - rank
    for index in range(held):
        theirs = other[below:, index * size : (index + 1) * size]
        for core, weights in ((c, factor[index]), (1 - c, theirs)):
            products[core * held + index] = lax.dot_general(
                x[...], weights, (((1,), (1,)), ((), ())), preferred_element_type=jnp.float32
            )
    lookup.wait()
    for i, distance in enumerate(order):
        chip = chip_at(distance, n)
        parts[chip] = products[adapters[chip * 2 * rows // BLOCK], i * rows : (i + 1) * rows, :]
    pack(parts, total)
    rounded[...] = total[...].astype(jnp.bfloat16)


def add_kernel(total, *refs):
    *received, out, rounded = refs
    value = total[...]
    for x in received:
        value += x[...].astype(jnp.float32)
    out[...] = value
    rounded[...] = value.astype(jnp.bfloat16)


def weight_copies(first, w_ref, w_out, sems):
    parts = sems.shape[0]
    depth = w_out.shape[0] // parts
    return [
        pltpu.make_async_copy(
            w_ref.at[pl.ds(first + k * depth, depth), :], w_out.at[pl.ds(k * depth, depth), :], sems.at[k]
        )
        for k in range(parts)
    ]


def first_load_kernel(n, window, distances, w_ref, tokens_ref, down_ref, w_out, factor, *refs):
    *sends, tokens, down, sems, small_sems = refs
    copies = weight_copies(0, w_ref, w_out, sems)
    small = [
        pltpu.make_async_copy(source, to, small_sems.at[k])
        for k, (source, to) in enumerate(((tokens_ref, tokens), (down_ref, down)))
    ]
    for copy in small + copies:
        copy.start()
    for copy in small:
        copy.wait()
    zeros = jnp.zeros((down.shape[1], window.size - window.width), jnp.float32)
    for index in range(down.shape[0]):
        wide = jnp.concatenate([down[index], zeros], 1)
        factor[index] = pltpu.roll(wide, window.shift(lax.axis_index("seq")), 1).astype(jnp.bfloat16)
    for distance, send in zip(distances, sends):
        start = pl.multiple_of(window.start(chip_at(distance, n)), 128)
        send[...] = tokens[:, pl.ds(start, window.size)]
    for copy in copies:
        copy.wait()


def second_load_kernel(first, w_ref, up_ref, w_out, up_out, held, sems, up_sem):
    copies = weight_copies(first, w_ref, w_out, sems)
    up_copy = pltpu.make_async_copy(up_ref, held, up_sem)
    up_copy.start()
    for copy in copies:
        copy.start()
    up_copy.wait()
    up_out[...] = held[...].astype(jnp.bfloat16)
    for copy in copies:
        copy.wait()


def load(kernel, arrays, after, outs, scratch):
    operands = len(arrays)

    def body(*refs):
        kernel(*refs[:operands], *refs[operands + len(after) :])

    return pl.pallas_call(
        body,
        out_shape=[pltpu.VMEM(shape, jnp.bfloat16) for shape in outs],
        in_specs=[pl.BlockSpec(memory_space=pltpu.HBM)] * operands
        + [pl.BlockSpec(memory_space=pl.ANY)] * len(after),
        out_specs=whole(len(outs)),
        scratch_shapes=scratch,
        compiler_params=pltpu.CompilerParams(vmem_limit_bytes=8 << 20),
        cost_estimate=pl.CostEstimate(
            flops=0, bytes_accessed=2 * outs[0][0] * outs[0][1], transcendentals=0
        ),
    )(*(pltpu.with_memory_space_constraint(x, pltpu.HBM) for x in arrays), *after)


def assemble(pairs, counts, rows, held):
    c = lax.axis_index("adapter")
    first = 0
    for pair, (begin, end) in zip(pairs, counts):
        depth = pair[0].shape[1]
        for chip in range(begin, end):
            for k in range(CHUNKS):
                at = (chip * CHUNKS + k) * rows
                for ref, core in zip(pair, (c, 1 - c)):
                    row = pl.multiple_of(first + core * rows, rows)
                    held[pl.ds(row, rows), k * depth : (k + 1) * depth] = ref[at : at + rows, :]
            first += 2 * rows


def tile_width(width):
    return 768 if width % 768 == 0 else width


def multiply(held, weights, at):
    total, first = 0.0, 0
    for w in weights:
        columns = held[:, first : first + w.shape[0]]
        total += jnp.dot(columns, w[:, at], preferred_element_type=jnp.float32)
        first += w.shape[0]
    return total


def base_kernel(rows, counts, *refs):
    count = 2 * len(counts)
    pairs, weights, (base, held) = refs[:count], refs[count:-2], refs[-2:]
    assemble(list(zip(pairs[::2], pairs[1::2])), counts, rows, held)
    width = base.shape[1]
    columns = tile_width(width)
    for j in range(0, width, columns):
        at = slice(j, j + columns)
        base[:, at] = multiply(held, weights, at)


def base_rows(pairs, counts, rows, weights, after):
    chips = sum(end - begin for begin, end in counts)
    total, depth, width = 2 * rows * chips, sum(w.shape[0] for w in weights), weights[0].shape[1]
    arrays = [x for pair in pairs for x in pair]
    (base,) = call(
        functools.partial(base_kernel, rows, counts),
        arrays + weights,
        after,
        [((total, width), jnp.float32)],
        [pltpu.VMEM((total, depth), jnp.bfloat16)],
        limit=8 + (2 * total * depth >> 20),
        flops=2 * total * depth * width,
    )
    return base


def finish_kernel(n, rows, groups, skipped, adapters, live, *refs):
    *bases, own, other, up_ref = refs[: len(groups) + 3]
    out_ref, *token, shrink, block, sems = refs[len(groups) + 3 + skipped :]
    for ref in token:
        ref[...] = jnp.zeros_like(ref)
    c = lax.axis_index("adapter")
    chip_rows, rank = 2 * rows, up_ref.shape[1]
    tiles, _, columns = block.shape
    for t in range(n):
        i, k = t % (n // 2), t // (n // 2)
        for ref, core in ((own, c), (other, 1 - c)):
            part = ref[i * rows : (i + 1) * rows, k * rank : (k + 1) * rank]
            shrink[t, pl.ds(pl.multiple_of(core * rows, rows), rows), :] = part.astype(jnp.bfloat16)
    places = [
        (distance, base, i * chip_rows)
        for base, distances in zip(bases, groups)
        for i, distance in enumerate(distances)
    ]
    copies = []
    for j in range(tiles):
        at = slice(j * columns, (j + 1) * columns)
        for i, (distance, base, row) in enumerate(places):
            chip = chip_at(distance, n)
            first = chip * chip_rows
            of_block = first // BLOCK
            delta = jnp.dot(shrink[chip], up_ref[adapters[of_block], :, at], preferred_element_type=jnp.float32)
            index = lax.broadcasted_iota(jnp.int32, delta.shape, 0) + (first - of_block * BLOCK)
            total = jnp.where(index < live[of_block], base[row : row + chip_rows, at] + delta, 0.0)
            place = pl.ds(i * chip_rows, chip_rows)
            block[j, place, :] = total.astype(out_ref.dtype)
            copies.append(
                pltpu.make_async_copy(
                    block.at[j, place, :],
                    out_ref.at[pl.ds(pl.multiple_of(first, chip_rows), chip_rows), pl.ds(j * columns, columns)],
                    sems.at[j, i],
                )
            )
            copies[-1].start()
    for copy in copies:
        copy.wait()


def finish(n, rows, groups, scalars, bases, own, other, up, into):
    rank, width = up.shape[1:]
    count = sum(len(group) for group in groups)
    total, columns = 2 * rows * count, tile_width(width)
    arrays = [*bases, own, other, up]
    token = [] if into else [pltpu.VMEM((8, 128), jnp.float32)]
    return pl.pallas_call(
        functools.partial(finish_kernel, n, rows, groups, len(into)),
        out_shape=[jax.ShapeDtypeStruct((2 * n * rows, width), jnp.bfloat16)] + token,
        in_specs=[pl.BlockSpec(memory_space=pltpu.SMEM)] * len(scalars)
        + whole(len(arrays))
        + [pl.BlockSpec(memory_space=pl.ANY)] * len(into),
        out_specs=[pl.BlockSpec(memory_space=pl.ANY)] + whole(len(token)),
        scratch_shapes=[
            pltpu.VMEM((n, 2 * rows, rank), jnp.bfloat16),
            pltpu.VMEM((width // columns, total, columns), jnp.bfloat16),
            pltpu.SemaphoreType.DMA((width // columns, count)),
        ],
        input_output_aliases={len(scalars) + len(arrays): 0} if into else {},
        compiler_params=pltpu.CompilerParams(vmem_limit_bytes=8 << 20),
        cost_estimate=pl.CostEstimate(
            flops=2 * total * rank * width, bytes_accessed=2 * total * width, transcendentals=0
        ),
    )(*scalars, *in_vmem(arrays), *into)


def on_device(n, tokens, weight, down, up, adapter_per_block, rows_per_block):
    rows, features = tokens.shape
    depth = features // CHUNKS
    held, width, rank = down.shape
    last = n // 2
    adapters = adapter_per_block[:, 0]
    window = Window(n, width, depth)
    near, mid, far = ([d for hop in hops for d in hop_distances(hop, n)] for hops in ((0, 1), range(2, last - 1), [last - 1]))
    half = (n // 2 * rows, 2 * rank)
    sums = [(half, jnp.float32), (half, jnp.bfloat16)]

    (behind,), (ahead,) = ring_hop([tokens], [tokens], n)
    ends = far + [last]
    cut = features * 3 // 5 // 256 * 256
    weights, factor, *sends = load(
        functools.partial(first_load_kernel, n, window, ends),
        [weight, tokens, jnp.swapaxes(down, 1, 2)],
        [],
        [(cut, weight.shape[1]), (held, rank, window.size)] + [(rows, window.size)] * len(ends),
        [
            pltpu.VMEM(tokens.shape, tokens.dtype),
            pltpu.VMEM((held, rank, width), down.dtype),
            pltpu.SemaphoreType.DMA((4,)),
            pltpu.SemaphoreType.DMA((2,)),
        ],
    )
    received = [lax.ppermute(x, AXES, ring_perm(n, d)) for d, x in zip(ends, sends)]
    come_from = [-d for d in far] + [last]
    piece = ((rows, depth), jnp.bfloat16)
    near_rows, *chunks = call(
        near_kernel,
        [tokens, behind, ahead, factor],
        received,
        [((3 * CHUNKS * rows + rank, depth), jnp.bfloat16)] + [piece] * (2 * CHUNKS),
    )

    up_way, down_way = chunks[:CHUNKS], chunks[CHUNKS:]
    near_pair = (near_rows, swap_cores(near_rows, n))
    other_weights, up = load(
        functools.partial(second_load_kernel, cut),
        [weight, up],
        [near_rows],
        [(features - cut, weight.shape[1]), up.shape],
        [pltpu.VMEM(up.shape, up.dtype), pltpu.SemaphoreType.DMA((4,)), pltpu.SemaphoreType.DMA],
    )
    weights = [weights, other_weights]
    arrived = []
    for _ in range(2, last - 1):
        up_way, down_way = ring_hop(up_way, down_way, n)
        arrived += up_way + down_way
    mid_rows, *chunks = join(arrived, [other_weights], 2)
    up_way, down_way = chunks[:CHUNKS], chunks[CHUNKS:]

    total, rounded = call(
        functools.partial(partial_kernel, n, window, [near, mid], come_from),
        [near_rows, mid_rows, *received, factor, near_pair[1]],
        [],
        sums,
        [
            pltpu.SMEM(adapters.shape, jnp.int32),
            pltpu.VMEM((n * rows, window.size), jnp.bfloat16),
            pltpu.VMEM((2 * held, n * rows, rank), jnp.float32),
            pltpu.VMEM((n, rows, rank), jnp.float32),
            pltpu.SemaphoreType.DMA,
        ],
        outside=[adapters],
    )
    total, rounded = call(add_kernel, [total, lax.ppermute(rounded, AXES, y_perm(n))], [], sums)
    up_way, down_way = ring_hop(up_way, down_way, n)
    far_rows, turned = join([mid_rows, *up_way, *down_way], [rounded], 1)

    far_pair = (far_rows, swap_cores(far_rows, n))
    bases = [base_rows([near_pair], [(0, len(near))], rows, weights, [far_rows])]
    total, rounded = call(
        add_kernel,
        [total] + [lax.ppermute(rounded, AXES, z_perm(n, shift)) for shift in range(1, n // 2)],
        [],
        sums,
    )
    (last_rows,) = join([lax.ppermute(turned, AXES, ring_perm(n, 1, -1))], [rounded, *bases])

    count = len(mid)
    bases.append(base_rows([far_pair], [(0, count)], rows, weights, [last_rows]))
    scalars = [adapters, rows_per_block]
    sums = [total, swap_cores(rounded, n)]
    out, token = finish(n, rows, [near, mid], scalars, bases, *sums, up, [])
    pairs = [far_pair, (last_rows, swap_cores(last_rows, n))]
    bases = [base_rows(pairs, [(count, count + len(far)), (0, 1)], rows, weights, [token])]
    return finish(n, rows, [far + [last]], scalars, bases, *sums, up, [out])[0]


def solution(mesh):
    placed = (
        P(("groups", "seq", "adapter"), None),
        P(None, ("seq", "adapter")),
        P(("groups", "adapter"), "seq", None),
        P("groups", None, ("seq", "adapter")),
        P("groups", None),
        P("groups"),
    )
    return jax.shard_map(
        functools.partial(on_device, mesh.shape["seq"]),
        mesh=mesh,
        in_specs=placed,
        out_specs=P("groups", ("seq", "adapter")),
        check_vma=False,
    )
```

```python
import functools

import jax
import jax.numpy as jnp
from jax import lax
from jax.experimental import pallas as pl
from jax.experimental.pallas import tpu as pltpu
from jax.sharding import PartitionSpec as P

BLOCK = 128
AXES = ("seq", "adapter")
CHUNKS = 2


def ring_perm(n, way, other_way=None):
    order = [2 * z for z in range(n // 2)] + [2 * z + 1 for z in reversed(range(n // 2))]
    ways = (way, way if other_way is None else other_way)
    return [(2 * s + c, 2 * order[(pos + ways[c]) % n] + c) for pos, s in enumerate(order) for c in range(2)]


def swap_cores(x, n):
    return lax.ppermute(x, AXES, [(2 * s + c, 2 * s + 1 - c) for s in range(n) for c in range(2)])


def chip_at(distance, n):
    s = lax.axis_index("seq")
    z = s >> 1
    pos = jnp.where(s & 1 == 0, z, n - 1 - z) + distance
    pos = jnp.where(pos >= n, pos - n, pos)
    pos = jnp.where(pos < 0, pos + n, pos)
    return jnp.where(pos < n // 2, 2 * pos, 2 * (n - 1 - pos) + 1)


def y_perm(n):
    return [(2 * s + c, 2 * (s ^ 1) + c) for s in range(n) for c in range(2)]


def z_perm(n, shift):
    nz = n // 2
    return [
        (2 * (2 * z + y) + c, 2 * (2 * ((z - shift) % nz) + y) + c)
        for z in range(nz)
        for y in range(2)
        for c in range(2)
    ]


def hop_distances(hop, n):
    if hop == 0:
        return [0]
    return [-hop, hop] if hop < n // 2 else [hop]


def ring_hop(up, down, n):
    return [lax.ppermute(x, AXES, ring_perm(n, 1)) for x in up], [lax.ppermute(x, AXES, ring_perm(n, -1)) for x in down]


def join_kernel(ways, *refs):
    count = len(refs) - 1 - (2 * CHUNKS if ways == 2 else ways)
    pieces, out, on = refs[:count], refs[count], refs[count + 1 :]
    first = 0
    for piece in pieces:
        out[first : first + piece.shape[0], :] = piece[...]
        first += piece.shape[0]
    arrived = pieces[len(pieces) - 2 * CHUNKS :]
    if ways == 2:
        for piece, ref in zip(arrived, on):
            ref[...] = piece[...]
    if ways == 1:
        c = lax.axis_index("adapter")
        rows = arrived[0].shape[0]
        for core in range(2):

            @pl.when(c == core)
            def _():
                for i, piece in enumerate(arrived[core * CHUNKS : (core + 1) * CHUNKS]):
                    on[0][i * rows : (i + 1) * rows, :] = piece[...]


def join(pieces, after, ways=0):
    (rows, depth), dtype = pieces[-1].shape, pieces[-1].dtype
    on = {0: [], 1: [CHUNKS * rows], 2: [rows] * 2 * CHUNKS}[ways]
    outs = [((count, depth), dtype) for count in [sum(x.shape[0] for x in pieces), *on]]
    return call(functools.partial(join_kernel, ways), pieces, after, outs)


def whole(count):
    return [pl.BlockSpec(memory_space=pltpu.VMEM)] * count


def in_vmem(arrays):
    return [pltpu.with_memory_space_constraint(x, pltpu.VMEM) for x in arrays]


def call(kernel, arrays, after, outs, scratch=(), limit=8, flops=0, outside=()):
    operands = len(arrays) + len(outside)

    def body(*refs):
        kernel(*refs[:operands], *refs[operands + len(after) :])

    return pl.pallas_call(
        body,
        out_shape=[pltpu.VMEM(shape, dtype) for shape, dtype in outs],
        in_specs=whole(len(arrays)) + [pl.BlockSpec(memory_space=pl.ANY)] * (len(outside) + len(after)),
        out_specs=whole(len(outs)),
        scratch_shapes=list(scratch),
        compiler_params=pltpu.CompilerParams(vmem_limit_bytes=limit << 20),
        cost_estimate=pl.CostEstimate(flops=flops, bytes_accessed=0, transcendentals=0),
    )(*in_vmem(arrays), *outside, *after)


class Window:
    def __init__(self, n, width, depth):
        self.width, self.depth = width, depth
        self.size = -(-(width + max(s * width % 128 for s in range(n))) // 128) * 128
        for s in range(n):
            start = s * width // 128 * 128
            assert start // depth == (start + self.size - 1) // depth

    def start(self, chip):
        return (chip * self.width) >> 7 << 7

    def shift(self, chip):
        return chip * self.width - self.start(chip)


def near_kernel(tokens, behind, ahead, factor, out, *chunks):
    held, rank, size = factor.shape
    rows, depth = chunks[0].shape
    for i, ref in enumerate((tokens, behind, ahead)):
        for k in range(CHUNKS):
            piece = ref[:, k * depth : (k + 1) * depth]
            at = (i * CHUNKS + k) * rows
            out[at : at + rows, :] = piece
            if i:
                chunks[(i - 1) * CHUNKS + k][...] = piece
    first = 3 * CHUNKS * rows
    out[first:, :] = jnp.zeros((rank, depth), out.dtype)
    for index in range(held):
        out[first:, index * size : (index + 1) * size] = factor[index]


def pack(parts, out):
    chips, rows, rank = parts.shape
    for t in range(chips):
        i, k = t % (chips // 2), t // (chips // 2)
        out[i * rows : (i + 1) * rows, k * rank : (k + 1) * rank] = parts[t].astype(out.dtype)


def partial_kernel(n, window, groups, far, *refs):
    *pieces, factor, other, adapters_ref, total, rounded, adapters, x, products, parts, sem = refs
    lookup = pltpu.make_async_copy(adapters_ref, adapters, sem)
    lookup.start()
    pieces, received = pieces[: len(groups)], pieces[len(groups) :]
    s, c = lax.axis_index("seq"), lax.axis_index("adapter")
    rows, size = received[0].shape
    held, rank, _ = factor.shape
    start = window.start(s)
    chunk = jnp.where(start >= window.depth, 1, 0)
    inside = pl.multiple_of(start - chunk * window.depth, 128)
    order = []
    for piece, distances in zip(pieces, groups):
        for i, distance in enumerate(distances):
            row = pl.multiple_of((i * CHUNKS + chunk) * rows, rows)
            x[len(order) * rows : (len(order) + 1) * rows, :] = piece[pl.ds(row, rows), pl.ds(inside, size)]
            order.append(distance)
    for piece, distance in zip(received, far):
        x[len(order) * rows : (len(order) + 1) * rows, :] = piece[...]
        order.append(distance)
    below = other.shape[0] - rank
    for index in range(held):
        theirs = other[below:, index * size : (index + 1) * size]
        for core, weights in ((c, factor[index]), (1 - c, theirs)):
            products[core * held + index] = lax.dot_general(
                x[...], weights, (((1,), (1,)), ((), ())), preferred_element_type=jnp.float32
            )
    lookup.wait()
    for i, distance in enumerate(order):
        chip = chip_at(distance, n)
        parts[chip] = products[adapters[chip * 2 * rows // BLOCK], i * rows : (i + 1) * rows, :]
    pack(parts, total)
    rounded[...] = total[...].astype(jnp.bfloat16)


def add_kernel(total, *refs):
    *received, out, rounded = refs
    value = total[...]
    for x in received:
        value += x[...].astype(jnp.float32)
    out[...] = value
    rounded[...] = value.astype(jnp.bfloat16)


def weight_copies(first, w_ref, w_out, sems):
    parts = sems.shape[0]
    depth = w_out.shape[0] // parts
    return [
        pltpu.make_async_copy(
            w_ref.at[pl.ds(first + k * depth, depth), :], w_out.at[pl.ds(k * depth, depth), :], sems.at[k]
        )
        for k in range(parts)
    ]


def prepare_kernel(n, window, distances, tokens_ref, down_ref, factor, *refs):
    *sends, tokens, down, sems = refs
    copies = [
        pltpu.make_async_copy(source, to, sems.at[k])
        for k, (source, to) in enumerate(((tokens_ref, tokens), (down_ref, down)))
    ]
    for copy in copies:
        copy.start()
    copies[0].wait()
    for distance, send in zip(distances, sends):
        start = pl.multiple_of(window.start(chip_at(distance, n)), 128)
        send[...] = tokens[:, pl.ds(start, window.size)]
    copies[1].wait()
    zeros = jnp.zeros((down.shape[1], window.size - window.width), jnp.float32)
    for index in range(down.shape[0]):
        wide = jnp.concatenate([down[index], zeros], 1)
        factor[index] = pltpu.roll(wide, window.shift(lax.axis_index("seq")), 1).astype(jnp.bfloat16)


def first_load_kernel(w_ref, w_out, sems):
    copies = weight_copies(0, w_ref, w_out, sems)
    for copy in copies:
        copy.start()
    for copy in copies:
        copy.wait()


def second_load_kernel(chips, rows, w_ref, up_ref, first_w, near, w_out, up_out, base, up, held, sems, up_sem):
    first, parts = first_w.shape[0], sems.shape[0]
    copies = weight_copies(first, w_ref, w_out, sems)
    up_copy = pltpu.make_async_copy(up_ref, up, up_sem)
    up_copy.start()
    for copy in copies:
        copy.start()
    assemble_core(near, chips, rows, held)
    base[...] = jnp.dot(held[:, :first], first_w[...], preferred_element_type=jnp.float32)
    up_copy.wait()
    up_out[...] = up[...].astype(jnp.bfloat16)
    deep = w_out.shape[0] // parts
    for k, copy in enumerate(copies):
        copy.wait()
        columns = held[:, first + k * deep : first + (k + 1) * deep]
        weight = w_out[k * deep : (k + 1) * deep, :]
        base[...] += jnp.dot(columns, weight, preferred_element_type=jnp.float32)


def assemble_core(ref, chips, rows, held):
    depth = ref.shape[1]
    for i in range(chips):
        for k in range(CHUNKS):
            at = (i * CHUNKS + k) * rows
            held[i * rows : (i + 1) * rows, k * depth : (k + 1) * depth] = ref[at : at + rows, :]


def core_kernel(rows, ref, *refs):
    *weights, base, held = refs
    assemble_core(ref, base.shape[0] // rows, rows, held)
    columns = tile_width(base.shape[1])
    for j in range(0, base.shape[1], columns):
        at = slice(j, j + columns)
        base[:, at] = multiply(held, weights, at)


def both_kernel(rows, ref, mine, *refs):
    *weights, base, held = refs
    chips = mine.shape[0] // rows
    c = lax.axis_index("adapter")
    assemble_core(ref, chips, rows, held)
    columns = tile_width(base.shape[1])
    for j in range(0, base.shape[1], columns):
        at = slice(j, j + columns)
        tile = multiply(held, weights, at)
        for i in range(chips):
            here = slice(i * rows, (i + 1) * rows)
            for core, value in ((c, mine[here, at]), (1 - c, tile[here])):
                base[pl.ds(pl.multiple_of((2 * i + core) * rows, rows), rows), at] = value


def core_rows(ref, chips, rows, weights, after, mine=None):
    total, depth, width = rows * chips, sum(w.shape[0] for w in weights), weights[0].shape[1]
    (base,) = call(
        functools.partial(core_kernel if mine is None else both_kernel, rows),
        [ref] + ([] if mine is None else [mine]) + weights,
        after,
        [((total if mine is None else 2 * total, width), jnp.float32)],
        [pltpu.VMEM((total, depth), jnp.bfloat16)],
        limit=8 + (2 * total * depth >> 20),
        flops=2 * total * depth * width,
    )
    return base


def load(kernel, arrays, after, outs, scratch, inside=(), flops=0):
    operands = len(arrays) + len(inside)

    def body(*refs):
        kernel(*refs[:operands], *refs[operands + len(after) :])

    return pl.pallas_call(
        body,
        out_shape=[pltpu.VMEM(shape, dtype) for shape, dtype in outs],
        in_specs=[pl.BlockSpec(memory_space=pltpu.HBM)] * len(arrays)
        + whole(len(inside))
        + [pl.BlockSpec(memory_space=pl.ANY)] * len(after),
        out_specs=whole(len(outs)),
        scratch_shapes=scratch,
        compiler_params=pltpu.CompilerParams(vmem_limit_bytes=8 << 20),
        cost_estimate=pl.CostEstimate(
            flops=flops, bytes_accessed=2 * outs[0][0][0] * outs[0][0][1], transcendentals=0
        ),
    )(*(pltpu.with_memory_space_constraint(x, pltpu.HBM) for x in arrays), *in_vmem(inside), *after)


def assemble(pairs, counts, rows, held):
    c = lax.axis_index("adapter")
    first = 0
    for pair, chips in zip(pairs, counts):
        depth = pair[0].shape[1]
        for chip in range(chips):
            for k in range(CHUNKS):
                at = (chip * CHUNKS + k) * rows
                for ref, core in zip(pair, (c, 1 - c)):
                    row = pl.multiple_of(first + core * rows, rows)
                    held[pl.ds(row, rows), k * depth : (k + 1) * depth] = ref[at : at + rows, :]
            first += 2 * rows


def tile_width(width):
    return 768 if width % 768 == 0 else width


def multiply(held, weights, at):
    total, first = 0.0, 0
    for w in weights:
        columns = held[:, first : first + w.shape[0]]
        total += jnp.dot(columns, w[:, at], preferred_element_type=jnp.float32)
        first += w.shape[0]
    return total


def base_kernel(rows, counts, *refs):
    count = 2 * len(counts)
    pairs, weights, (base, held) = refs[:count], refs[count:-2], refs[-2:]
    assemble(list(zip(pairs[::2], pairs[1::2])), counts, rows, held)
    width = base.shape[1]
    columns = tile_width(width)
    for j in range(0, width, columns):
        at = slice(j, j + columns)
        base[:, at] = multiply(held, weights, at)


def base_rows(pairs, counts, rows, weights, after):
    chips = sum(counts)
    total, depth, width = 2 * rows * chips, sum(w.shape[0] for w in weights), weights[0].shape[1]
    arrays = [x for pair in pairs for x in pair]
    (base,) = call(
        functools.partial(base_kernel, rows, counts),
        arrays + weights,
        after,
        [((total, width), jnp.float32)],
        [pltpu.VMEM((total, depth), jnp.bfloat16)],
        limit=8 + (2 * total * depth >> 20),
        flops=2 * total * depth * width,
    )
    return base


def finish_kernel(n, rows, groups, adapters, live, *refs):
    *bases, own, other, up_ref = refs[: len(groups) + 3]
    out_ref, shrink, block, sems = refs[len(groups) + 3 :]
    c = lax.axis_index("adapter")
    chip_rows, rank = 2 * rows, up_ref.shape[1]
    tiles, _, columns = block.shape
    for t in range(n):
        i, k = t % (n // 2), t // (n // 2)
        for ref, core in ((own, c), (other, 1 - c)):
            part = ref[i * rows : (i + 1) * rows, k * rank : (k + 1) * rank]
            shrink[t, pl.ds(pl.multiple_of(core * rows, rows), rows), :] = part.astype(jnp.bfloat16)
    places = [
        (distance, base, i * chip_rows)
        for base, distances in zip(bases, groups)
        for i, distance in enumerate(distances)
    ]
    copies = []
    for j in range(tiles):
        at = slice(j * columns, (j + 1) * columns)
        for i, (distance, base, row) in enumerate(places):
            chip = chip_at(distance, n)
            first = chip * chip_rows
            of_block = first // BLOCK
            delta = jnp.dot(shrink[chip], up_ref[adapters[of_block], :, at], preferred_element_type=jnp.float32)
            index = lax.broadcasted_iota(jnp.int32, delta.shape, 0) + (first - of_block * BLOCK)
            total = jnp.where(index < live[of_block], base[row : row + chip_rows, at] + delta, 0.0)
            place = pl.ds(i * chip_rows, chip_rows)
            block[j, place, :] = total.astype(out_ref.dtype)
            copies.append(
                pltpu.make_async_copy(
                    block.at[j, place, :],
                    out_ref.at[pl.ds(pl.multiple_of(first, chip_rows), chip_rows), pl.ds(j * columns, columns)],
                    sems.at[j, i],
                )
            )
            copies[-1].start()
    for copy in copies:
        copy.wait()


def finish(n, rows, groups, scalars, bases, own, other, up):
    rank, width = up.shape[1:]
    total, columns = 2 * n * rows, tile_width(width)
    arrays = [*bases, own, other, up]
    return pl.pallas_call(
        functools.partial(finish_kernel, n, rows, groups),
        out_shape=jax.ShapeDtypeStruct((total, width), jnp.bfloat16),
        in_specs=[pl.BlockSpec(memory_space=pltpu.SMEM)] * len(scalars) + whole(len(arrays)),
        out_specs=pl.BlockSpec(memory_space=pl.ANY),
        scratch_shapes=[
            pltpu.VMEM((n, 2 * rows, rank), jnp.bfloat16),
            pltpu.VMEM((width // columns, total, columns), jnp.bfloat16),
            pltpu.SemaphoreType.DMA((width // columns, n)),
        ],
        compiler_params=pltpu.CompilerParams(vmem_limit_bytes=8 << 20),
        cost_estimate=pl.CostEstimate(
            flops=2 * total * rank * width, bytes_accessed=2 * total * width, transcendentals=0
        ),
    )(*scalars, *in_vmem(arrays))


def on_device(n, tokens, weight, down, up, adapter_per_block, rows_per_block):
    rows, features = tokens.shape
    depth = features // CHUNKS
    held, width, rank = down.shape
    last = n // 2
    adapters = adapter_per_block[:, 0]
    window = Window(n, width, depth)
    near, mid, far = ([d for hop in hops for d in hop_distances(hop, n)] for hops in ((0, 1), range(2, last - 1), [last - 1]))
    half = (n // 2 * rows, 2 * rank)
    sums = [(half, jnp.float32), (half, jnp.bfloat16)]

    (behind,), (ahead,) = ring_hop([tokens], [tokens], n)
    ends = far + [last]
    bf16 = jnp.bfloat16
    factor, *sends = load(
        functools.partial(prepare_kernel, n, window, ends),
        [tokens, jnp.swapaxes(down, 1, 2)],
        [],
        [((held, rank, window.size), bf16)] + [((rows, window.size), bf16)] * len(ends),
        [
            pltpu.VMEM(tokens.shape, tokens.dtype),
            pltpu.VMEM((held, rank, width), down.dtype),
            pltpu.SemaphoreType.DMA((2,)),
        ],
    )
    received = [lax.ppermute(x, AXES, ring_perm(n, d)) for d, x in zip(ends, sends)]
    come_from = [-d for d in far] + [last]
    cut, hidden = features * 3 // 5 // 256 * 256, weight.shape[1]
    (first_weight,) = load(
        first_load_kernel, [weight], [], [((cut, hidden), bf16)], [pltpu.SemaphoreType.DMA((4,))]
    )
    piece = ((rows, depth), bf16)
    near_rows, *chunks = call(
        near_kernel,
        [tokens, behind, ahead, factor],
        [first_weight, *received],
        [((len(near) * CHUNKS * rows + rank, depth), bf16)] + [piece] * (2 * CHUNKS),
    )

    up_way, down_way = chunks[:CHUNKS], chunks[CHUNKS:]
    near_swapped = swap_cores(near_rows, n)
    own = len(near) * rows
    other_weight, up, mine = load(
        functools.partial(second_load_kernel, len(near), rows),
        [weight, up],
        [],
        [((features - cut, hidden), bf16), (up.shape, bf16), ((own, hidden), jnp.float32)],
        [
            pltpu.VMEM(up.shape, up.dtype),
            pltpu.VMEM((own, features), bf16),
            pltpu.SemaphoreType.DMA((4,)),
            pltpu.SemaphoreType.DMA,
        ],
        [first_weight, near_rows],
        2 * own * features * hidden,
    )
    weights = [first_weight, other_weight]
    arrived = []
    for _ in range(2, last - 1):
        up_way, down_way = ring_hop(up_way, down_way, n)
        arrived += up_way + down_way
    mid_rows, *chunks = join(arrived, [other_weight], 2)
    up_way, down_way = chunks[:CHUNKS], chunks[CHUNKS:]

    total, rounded = call(
        functools.partial(partial_kernel, n, window, [near, mid], come_from),
        [near_rows, mid_rows, *received, factor, near_swapped],
        [],
        sums,
        [
            pltpu.SMEM(adapters.shape, jnp.int32),
            pltpu.VMEM((n * rows, window.size), bf16),
            pltpu.VMEM((2 * held, n * rows, rank), jnp.float32),
            pltpu.VMEM((n, rows, rank), jnp.float32),
            pltpu.SemaphoreType.DMA,
        ],
        outside=[adapters],
    )
    bases = [core_rows(near_swapped, len(near), rows, weights, [rounded], mine)]
    total, rounded = call(add_kernel, [total, lax.ppermute(rounded, AXES, y_perm(n))], [], sums)
    up_way, down_way = ring_hop(up_way, down_way, n)
    late_rows, turned = join([mid_rows, *up_way, *down_way], [rounded, *bases], 1)

    late = mid + far
    late_swapped = swap_cores(late_rows, n)
    mine = core_rows(late_rows, len(late), rows, weights, [])
    total, rounded = call(
        add_kernel,
        [total] + [lax.ppermute(rounded, AXES, z_perm(n, shift)) for shift in range(1, n // 2)],
        [],
        sums,
    )
    (last_rows,) = join([lax.ppermute(turned, AXES, ring_perm(n, 1, -1))], [rounded, mine])

    bases.append(core_rows(late_swapped, len(late), rows, weights, [last_rows], mine))
    last_pair = (last_rows, swap_cores(last_rows, n))
    bases.append(base_rows([last_pair], [1], rows, weights, bases[-1:]))
    return finish(
        n,
        rows,
        [near, late, [last]],
        [adapters, rows_per_block],
        bases,
        total,
        swap_cores(rounded, n),
        up,
    )


def solution(mesh):
    placed = (
        P(("groups", "seq", "adapter"), None),
        P(None, ("seq", "adapter")),
        P(("groups", "adapter"), "seq", None),
        P("groups", None, ("seq", "adapter")),
        P("groups", None),
        P("groups"),
    )
    return jax.shard_map(
        functools.partial(on_device, mesh.shape["seq"]),
        mesh=mesh,
        in_specs=placed,
        out_specs=P("groups", ("seq", "adapter")),
        check_vma=False,
    )
```

```python
import functools

import jax
import jax.numpy as jnp
from jax import lax
from jax.experimental import pallas as pl
from jax.experimental.pallas import tpu as pltpu
from jax.sharding import PartitionSpec as P

BLOCK = 128
AXES = ("seq", "adapter")
CHUNKS = 2


def ring_perm(n, way, other_way=None):
    order = [2 * z for z in range(n // 2)] + [2 * z + 1 for z in reversed(range(n // 2))]
    ways = (way, way if other_way is None else other_way)
    return [(2 * s + c, 2 * order[(pos + ways[c]) % n] + c) for pos, s in enumerate(order) for c in range(2)]


def swap_cores(x, n):
    return lax.ppermute(x, AXES, [(2 * s + c, 2 * s + 1 - c) for s in range(n) for c in range(2)])


def chip_at(distance, n):
    s = lax.axis_index("seq")
    z = s >> 1
    pos = jnp.where(s & 1 == 0, z, n - 1 - z) + distance
    pos = jnp.where(pos >= n, pos - n, pos)
    pos = jnp.where(pos < 0, pos + n, pos)
    return jnp.where(pos < n // 2, 2 * pos, 2 * (n - 1 - pos) + 1)


def y_perm(n):
    return [(2 * s + c, 2 * (s ^ 1) + c) for s in range(n) for c in range(2)]


def z_perm(n, shift):
    nz = n // 2
    return [
        (2 * (2 * z + y) + c, 2 * (2 * ((z - shift) % nz) + y) + c)
        for z in range(nz)
        for y in range(2)
        for c in range(2)
    ]


def hop_distances(hop, n):
    if hop == 0:
        return [0]
    return [-hop, hop] if hop < n // 2 else [hop]


def ring_hop(up, down, n):
    return [lax.ppermute(x, AXES, ring_perm(n, 1)) for x in up], [lax.ppermute(x, AXES, ring_perm(n, -1)) for x in down]


def join_kernel(ways, *refs):
    count = len(refs) - 1 - (2 * CHUNKS if ways == 2 else ways)
    pieces, out, on = refs[:count], refs[count], refs[count + 1 :]
    first = 0
    for piece in pieces:
        out[first : first + piece.shape[0], :] = piece[...]
        first += piece.shape[0]
    arrived = pieces[len(pieces) - 2 * CHUNKS :]
    if ways == 2:
        for piece, ref in zip(arrived, on):
            ref[...] = piece[...]
    if ways == 1:
        c = lax.axis_index("adapter")
        rows = arrived[0].shape[0]
        for core in range(2):

            @pl.when(c == core)
            def _():
                for i, piece in enumerate(arrived[core * CHUNKS : (core + 1) * CHUNKS]):
                    on[0][i * rows : (i + 1) * rows, :] = piece[...]


def join(pieces, after, ways=0):
    (rows, depth), dtype = pieces[-1].shape, pieces[-1].dtype
    on = {0: [], 1: [CHUNKS * rows], 2: [rows] * 2 * CHUNKS}[ways]
    outs = [((count, depth), dtype) for count in [sum(x.shape[0] for x in pieces), *on]]
    return call(functools.partial(join_kernel, ways), pieces, after, outs)


def whole(count):
    return [pl.BlockSpec(memory_space=pltpu.VMEM)] * count


def in_vmem(arrays):
    return [pltpu.with_memory_space_constraint(x, pltpu.VMEM) for x in arrays]


def call(kernel, arrays, after, outs, scratch=(), limit=8, flops=0, outside=()):
    operands = len(arrays) + len(outside)

    def body(*refs):
        kernel(*refs[:operands], *refs[operands + len(after) :])

    return pl.pallas_call(
        body,
        out_shape=[pltpu.VMEM(shape, dtype) for shape, dtype in outs],
        in_specs=whole(len(arrays)) + [pl.BlockSpec(memory_space=pl.ANY)] * (len(outside) + len(after)),
        out_specs=whole(len(outs)),
        scratch_shapes=list(scratch),
        compiler_params=pltpu.CompilerParams(vmem_limit_bytes=limit << 20),
        cost_estimate=pl.CostEstimate(flops=flops, bytes_accessed=0, transcendentals=0),
    )(*in_vmem(arrays), *outside, *after)


class Window:
    def __init__(self, n, width, depth):
        self.width, self.depth = width, depth
        self.size = -(-(width + max(s * width % 128 for s in range(n))) // 128) * 128
        for s in range(n):
            start = s * width // 128 * 128
            assert start // depth == (start + self.size - 1) // depth

    def start(self, chip):
        return (chip * self.width) >> 7 << 7

    def shift(self, chip):
        return chip * self.width - self.start(chip)


def near_kernel(tokens, behind, ahead, factor, out, *chunks):
    held, rank, size = factor.shape
    rows, depth = chunks[0].shape
    for i, ref in enumerate((tokens, behind, ahead)):
        for k in range(CHUNKS):
            piece = ref[:, k * depth : (k + 1) * depth]
            at = (i * CHUNKS + k) * rows
            out[at : at + rows, :] = piece
            if i:
                chunks[(i - 1) * CHUNKS + k][...] = piece
    first = 3 * CHUNKS * rows
    out[first:, :] = jnp.zeros((rank, depth), out.dtype)
    for index in range(held):
        out[first:, index * size : (index + 1) * size] = factor[index]


def pack(parts, out):
    chips, rows, rank = parts.shape
    for t in range(chips):
        i, k = t % (chips // 2), t // (chips // 2)
        out[i * rows : (i + 1) * rows, k * rank : (k + 1) * rank] = parts[t].astype(out.dtype)


def partial_kernel(n, window, groups, far, *refs):
    *pieces, factor, other, adapters_ref, total, rounded, adapters, x, products, parts, sem = refs
    lookup = pltpu.make_async_copy(adapters_ref, adapters, sem)
    lookup.start()
    pieces, received = pieces[: len(groups)], pieces[len(groups) :]
    s, c = lax.axis_index("seq"), lax.axis_index("adapter")
    rows, size = received[0].shape
    held, rank, _ = factor.shape
    start = window.start(s)
    chunk = jnp.where(start >= window.depth, 1, 0)
    inside = pl.multiple_of(start - chunk * window.depth, 128)
    order = []
    for piece, distances in zip(pieces, groups):
        for i, distance in enumerate(distances):
            row = pl.multiple_of((i * CHUNKS + chunk) * rows, rows)
            x[len(order) * rows : (len(order) + 1) * rows, :] = piece[pl.ds(row, rows), pl.ds(inside, size)]
            order.append(distance)
    for piece, distance in zip(received, far):
        x[len(order) * rows : (len(order) + 1) * rows, :] = piece[...]
        order.append(distance)
    below = other.shape[0] - rank
    for index in range(held):
        theirs = other[below:, index * size : (index + 1) * size]
        for core, weights in ((c, factor[index]), (1 - c, theirs)):
            products[core * held + index] = lax.dot_general(
                x[...], weights, (((1,), (1,)), ((), ())), preferred_element_type=jnp.float32
            )
    lookup.wait()
    for i, distance in enumerate(order):
        chip = chip_at(distance, n)
        parts[chip] = products[adapters[chip * 2 * rows // BLOCK], i * rows : (i + 1) * rows, :]
    pack(parts, total)
    rounded[...] = total[...].astype(jnp.bfloat16)


def add_kernel(total, *refs):
    *received, out, rounded = refs
    value = total[...]
    for x in received:
        value += x[...].astype(jnp.float32)
    out[...] = value
    rounded[...] = value.astype(jnp.bfloat16)


def weight_copies(first, w_ref, w_out, sems):
    parts = sems.shape[0]
    depth = w_out.shape[0] // parts
    return [
        pltpu.make_async_copy(
            w_ref.at[pl.ds(first + k * depth, depth), :], w_out.at[pl.ds(k * depth, depth), :], sems.at[k]
        )
        for k in range(parts)
    ]


def prepare_kernel(n, window, distances, tokens_ref, down_ref, factor, *refs):
    *sends, tokens, down, sems = refs
    copies = [
        pltpu.make_async_copy(source, to, sems.at[k])
        for k, (source, to) in enumerate(((tokens_ref, tokens), (down_ref, down)))
    ]
    for copy in copies:
        copy.start()
    copies[0].wait()
    for distance, send in zip(distances, sends):
        start = pl.multiple_of(window.start(chip_at(distance, n)), 128)
        send[...] = tokens[:, pl.ds(start, window.size)]
    copies[1].wait()
    zeros = jnp.zeros((down.shape[1], window.size - window.width), jnp.float32)
    for index in range(down.shape[0]):
        wide = jnp.concatenate([down[index], zeros], 1)
        factor[index] = pltpu.roll(wide, window.shift(lax.axis_index("seq")), 1).astype(jnp.bfloat16)


def first_load_kernel(w_ref, w_out, sems):
    copies = weight_copies(0, w_ref, w_out, sems)
    for copy in copies:
        copy.start()
    for copy in copies:
        copy.wait()


def second_load_kernel(chips, rows, w_ref, up_ref, first_w, near, w_out, up_out, base, up, held, sems, up_sem):
    first, parts = first_w.shape[0], sems.shape[0]
    copies = weight_copies(first, w_ref, w_out, sems)
    up_copy = pltpu.make_async_copy(up_ref, up, up_sem)
    up_copy.start()
    for copy in copies:
        copy.start()
    assemble_core(near, chips, rows, held)
    base[...] = jnp.dot(held[:, :first], first_w[...], preferred_element_type=jnp.float32)
    up_copy.wait()
    up_out[...] = up[...].astype(jnp.bfloat16)
    deep = w_out.shape[0] // parts
    for k, copy in enumerate(copies):
        copy.wait()
        columns = held[:, first + k * deep : first + (k + 1) * deep]
        weight = w_out[k * deep : (k + 1) * deep, :]
        base[...] += jnp.dot(columns, weight, preferred_element_type=jnp.float32)


def full_rows(rows):
    return max(rows, 128)


def assemble_core(ref, chips, rows, held):
    depth = ref.shape[1]
    for i in range(chips):
        for k in range(CHUNKS):
            at = (i * CHUNKS + k) * rows
            held[i * rows : (i + 1) * rows, k * depth : (k + 1) * depth] = ref[at : at + rows, :]


def core_kernel(rows, ref, *refs):
    *weights, base, held = refs
    assemble_core(ref, base.shape[0] // rows, rows, held)
    columns = tile_width(base.shape[1])
    for j in range(0, base.shape[1], columns):
        at = slice(j, j + columns)
        base[:, at] = multiply(held, weights, at)[: base.shape[0]]


def both_kernel(rows, ref, mine, *refs):
    *weights, base, held = refs
    chips = base.shape[0] // (2 * rows)
    c = lax.axis_index("adapter")
    assemble_core(ref, chips, rows, held)
    columns = tile_width(base.shape[1])
    for j in range(0, base.shape[1], columns):
        at = slice(j, j + columns)
        tile = multiply(held, weights, at)
        for i in range(chips):
            here = slice(i * rows, (i + 1) * rows)
            for core, value in ((c, mine[here, at]), (1 - c, tile[here])):
                base[pl.ds(pl.multiple_of((2 * i + core) * rows, rows), rows), at] = value


def core_rows(ref, chips, rows, weights, after, mine=None):
    total, depth, width = rows * chips, sum(w.shape[0] for w in weights), weights[0].shape[1]
    (base,) = call(
        functools.partial(core_kernel if mine is None else both_kernel, rows),
        [ref] + ([] if mine is None else [mine]) + weights,
        after,
        [((total if mine is None else 2 * total, width), jnp.float32)],
        [pltpu.VMEM((full_rows(total), depth), jnp.bfloat16)],
        limit=8 + (2 * total * depth >> 20),
        flops=2 * total * depth * width,
    )
    return base


def load(kernel, arrays, after, outs, scratch, inside=(), flops=0):
    operands = len(arrays) + len(inside)

    def body(*refs):
        kernel(*refs[:operands], *refs[operands + len(after) :])

    return pl.pallas_call(
        body,
        out_shape=[pltpu.VMEM(shape, dtype) for shape, dtype in outs],
        in_specs=[pl.BlockSpec(memory_space=pltpu.HBM)] * len(arrays)
        + whole(len(inside))
        + [pl.BlockSpec(memory_space=pl.ANY)] * len(after),
        out_specs=whole(len(outs)),
        scratch_shapes=scratch,
        compiler_params=pltpu.CompilerParams(vmem_limit_bytes=8 << 20),
        cost_estimate=pl.CostEstimate(
            flops=flops, bytes_accessed=2 * outs[0][0][0] * outs[0][0][1], transcendentals=0
        ),
    )(*(pltpu.with_memory_space_constraint(x, pltpu.HBM) for x in arrays), *in_vmem(inside), *after)


def assemble(pairs, counts, rows, held):
    c = lax.axis_index("adapter")
    first = 0
    for pair, chips in zip(pairs, counts):
        depth = pair[0].shape[1]
        for chip in range(chips):
            for k in range(CHUNKS):
                at = (chip * CHUNKS + k) * rows
                for ref, core in zip(pair, (c, 1 - c)):
                    row = pl.multiple_of(first + core * rows, rows)
                    held[pl.ds(row, rows), k * depth : (k + 1) * depth] = ref[at : at + rows, :]
            first += 2 * rows


def tile_width(width):
    return 768 if width % 768 == 0 else width


def multiply(held, weights, at):
    total, first = 0.0, 0
    for w in weights:
        columns = held[:, first : first + w.shape[0]]
        total += jnp.dot(columns, w[:, at], preferred_element_type=jnp.float32)
        first += w.shape[0]
    return total


def base_kernel(rows, counts, *refs):
    count = 2 * len(counts)
    pairs, weights, (base, held) = refs[:count], refs[count:-2], refs[-2:]
    assemble(list(zip(pairs[::2], pairs[1::2])), counts, rows, held)
    width = base.shape[1]
    columns = tile_width(width)
    for j in range(0, width, columns):
        at = slice(j, j + columns)
        base[:, at] = multiply(held, weights, at)[: base.shape[0]]


def base_rows(pairs, counts, rows, weights, after):
    chips = sum(counts)
    total, depth, width = 2 * rows * chips, sum(w.shape[0] for w in weights), weights[0].shape[1]
    arrays = [x for pair in pairs for x in pair]
    (base,) = call(
        functools.partial(base_kernel, rows, counts),
        arrays + weights,
        after,
        [((total, width), jnp.float32)],
        [pltpu.VMEM((full_rows(total), depth), jnp.bfloat16)],
        limit=8 + (2 * total * depth >> 20),
        flops=2 * total * depth * width,
    )
    return base


def finish_kernel(n, rows, groups, adapters, live, *refs):
    *bases, own, other, up_ref = refs[: len(groups) + 3]
    out_ref, shrink, block, sems = refs[len(groups) + 3 :]
    c = lax.axis_index("adapter")
    chip_rows, rank = 2 * rows, up_ref.shape[1]
    tiles, _, columns = block.shape
    for t in range(n):
        i, k = t % (n // 2), t // (n // 2)
        for ref, core in ((own, c), (other, 1 - c)):
            part = ref[i * rows : (i + 1) * rows, k * rank : (k + 1) * rank]
            shrink[t, pl.ds(pl.multiple_of(core * rows, rows), rows), :] = part.astype(jnp.bfloat16)
    places = [
        (distance, base, i * chip_rows)
        for base, distances in zip(bases, groups)
        for i, distance in enumerate(distances)
    ]
    copies = []
    for j in range(tiles):
        at = slice(j * columns, (j + 1) * columns)
        for i, (distance, base, row) in enumerate(places):
            chip = chip_at(distance, n)
            first = chip * chip_rows
            of_block = first // BLOCK
            delta = jnp.dot(shrink[chip], up_ref[adapters[of_block], :, at], preferred_element_type=jnp.float32)
            index = lax.broadcasted_iota(jnp.int32, delta.shape, 0) + (first - of_block * BLOCK)
            total = jnp.where(index < live[of_block], base[row : row + chip_rows, at] + delta, 0.0)
            place = pl.ds(i * chip_rows, chip_rows)
            block[j, place, :] = total.astype(out_ref.dtype)
            copies.append(
                pltpu.make_async_copy(
                    block.at[j, place, :],
                    out_ref.at[pl.ds(pl.multiple_of(first, chip_rows), chip_rows), pl.ds(j * columns, columns)],
                    sems.at[j, i],
                )
            )
            copies[-1].start()
    for copy in copies:
        copy.wait()


def finish(n, rows, groups, scalars, bases, own, other, up):
    rank, width = up.shape[1:]
    total, columns = 2 * n * rows, tile_width(width)
    arrays = [*bases, own, other, up]
    return pl.pallas_call(
        functools.partial(finish_kernel, n, rows, groups),
        out_shape=jax.ShapeDtypeStruct((total, width), jnp.bfloat16),
        in_specs=[pl.BlockSpec(memory_space=pltpu.SMEM)] * len(scalars) + whole(len(arrays)),
        out_specs=pl.BlockSpec(memory_space=pl.ANY),
        scratch_shapes=[
            pltpu.VMEM((n, 2 * rows, rank), jnp.bfloat16),
            pltpu.VMEM((width // columns, total, columns), jnp.bfloat16),
            pltpu.SemaphoreType.DMA((width // columns, n)),
        ],
        compiler_params=pltpu.CompilerParams(vmem_limit_bytes=8 << 20),
        cost_estimate=pl.CostEstimate(
            flops=2 * total * rank * width, bytes_accessed=2 * total * width, transcendentals=0
        ),
    )(*scalars, *in_vmem(arrays))


def on_device(n, tokens, weight, down, up, adapter_per_block, rows_per_block):
    rows, features = tokens.shape
    depth = features // CHUNKS
    held, width, rank = down.shape
    last = n // 2
    adapters = adapter_per_block[:, 0]
    window = Window(n, width, depth)
    near, mid, far = ([d for hop in hops for d in hop_distances(hop, n)] for hops in ((0, 1), range(2, last - 1), [last - 1]))
    half = (n // 2 * rows, 2 * rank)
    sums = [(half, jnp.float32), (half, jnp.bfloat16)]

    (behind,), (ahead,) = ring_hop([tokens], [tokens], n)
    ends = far + [last]
    bf16 = jnp.bfloat16
    factor, *sends = load(
        functools.partial(prepare_kernel, n, window, ends),
        [tokens, jnp.swapaxes(down, 1, 2)],
        [],
        [((held, rank, window.size), bf16)] + [((rows, window.size), bf16)] * len(ends),
        [
            pltpu.VMEM(tokens.shape, tokens.dtype),
            pltpu.VMEM((held, rank, width), down.dtype),
            pltpu.SemaphoreType.DMA((2,)),
        ],
    )
    received = [lax.ppermute(x, AXES, ring_perm(n, d)) for d, x in zip(ends, sends)]
    come_from = [-d for d in far] + [last]
    cut, hidden = features * 3 // 5 // 256 * 256, weight.shape[1]
    (first_weight,) = load(
        first_load_kernel, [weight], [], [((cut, hidden), bf16)], [pltpu.SemaphoreType.DMA((4,))]
    )
    piece = ((rows, depth), bf16)
    near_rows, *chunks = call(
        near_kernel,
        [tokens, behind, ahead, factor],
        [first_weight, *received],
        [((len(near) * CHUNKS * rows + rank, depth), bf16)] + [piece] * (2 * CHUNKS),
    )

    up_way, down_way = chunks[:CHUNKS], chunks[CHUNKS:]
    near_swapped = swap_cores(near_rows, n)
    own = len(near) * rows
    other_weight, up, mine = load(
        functools.partial(second_load_kernel, len(near), rows),
        [weight, up],
        [],
        [((features - cut, hidden), bf16), (up.shape, bf16), ((full_rows(own), hidden), jnp.float32)],
        [
            pltpu.VMEM(up.shape, up.dtype),
            pltpu.VMEM((full_rows(own), features), bf16),
            pltpu.SemaphoreType.DMA((4,)),
            pltpu.SemaphoreType.DMA,
        ],
        [first_weight, near_rows],
        2 * own * features * hidden,
    )
    weights = [first_weight, other_weight]
    arrived = []
    for _ in range(2, last - 1):
        up_way, down_way = ring_hop(up_way, down_way, n)
        arrived += up_way + down_way
    mid_rows, *chunks = join(arrived, [other_weight], 2)
    up_way, down_way = chunks[:CHUNKS], chunks[CHUNKS:]

    total, rounded = call(
        functools.partial(partial_kernel, n, window, [near, mid], come_from),
        [near_rows, mid_rows, *received, factor, near_swapped],
        [],
        sums,
        [
            pltpu.SMEM(adapters.shape, jnp.int32),
            pltpu.VMEM((n * rows, window.size), bf16),
            pltpu.VMEM((2 * held, n * rows, rank), jnp.float32),
            pltpu.VMEM((n, rows, rank), jnp.float32),
            pltpu.SemaphoreType.DMA,
        ],
        outside=[adapters],
    )
    bases = [core_rows(near_swapped, len(near), rows, weights, [rounded], mine)]
    total, rounded = call(add_kernel, [total, lax.ppermute(rounded, AXES, y_perm(n))], [], sums)
    up_way, down_way = ring_hop(up_way, down_way, n)
    late_rows, turned = join([mid_rows, *up_way, *down_way], [rounded, *bases], 1)

    late = mid + far
    late_swapped = swap_cores(late_rows, n)
    mine = core_rows(late_rows, len(late), rows, weights, [])
    total, rounded = call(
        add_kernel,
        [total] + [lax.ppermute(rounded, AXES, z_perm(n, shift)) for shift in range(1, n // 2)],
        [],
        sums,
    )
    (last_rows,) = join([lax.ppermute(turned, AXES, ring_perm(n, 1, -1))], [rounded, mine])

    bases.append(core_rows(late_swapped, len(late), rows, weights, [last_rows], mine))
    last_pair = (last_rows, swap_cores(last_rows, n))
    bases.append(base_rows([last_pair], [1], rows, weights, bases[-1:]))
    return finish(
        n,
        rows,
        [near, late, [last]],
        [adapters, rows_per_block],
        bases,
        total,
        swap_cores(rounded, n),
        up,
    )


def solution(mesh):
    placed = (
        P(("groups", "seq", "adapter"), None),
        P(None, ("seq", "adapter")),
        P(("groups", "adapter"), "seq", None),
        P("groups", None, ("seq", "adapter")),
        P("groups", None),
        P("groups"),
    )
    return jax.shard_map(
        functools.partial(on_device, mesh.shape["seq"]),
        mesh=mesh,
        in_specs=placed,
        out_specs=P("groups", ("seq", "adapter")),
        check_vma=False,
    )
```

```python
import functools

import jax
import jax.numpy as jnp
from jax import lax
from jax.experimental import pallas as pl
from jax.experimental.pallas import tpu as pltpu
from jax.sharding import PartitionSpec as P

BLOCK = 128
AXES = ("seq", "adapter")
CHUNKS = 2


def ring_perm(n, way, other_way=None):
    order = [2 * z for z in range(n // 2)] + [2 * z + 1 for z in reversed(range(n // 2))]
    ways = (way, way if other_way is None else other_way)
    return [(2 * s + c, 2 * order[(pos + ways[c]) % n] + c) for pos, s in enumerate(order) for c in range(2)]


def swap_cores(x, n):
    return lax.ppermute(x, AXES, [(2 * s + c, 2 * s + 1 - c) for s in range(n) for c in range(2)])


def chip_at(distance, n):
    s = lax.axis_index("seq")
    z = s >> 1
    pos = jnp.where(s & 1 == 0, z, n - 1 - z) + distance
    pos = jnp.where(pos >= n, pos - n, pos)
    pos = jnp.where(pos < 0, pos + n, pos)
    return jnp.where(pos < n // 2, 2 * pos, 2 * (n - 1 - pos) + 1)


def y_perm(n):
    return [(2 * s + c, 2 * (s ^ 1) + c) for s in range(n) for c in range(2)]


def z_perm(n, shift):
    nz = n // 2
    return [
        (2 * (2 * z + y) + c, 2 * (2 * ((z - shift) % nz) + y) + c)
        for z in range(nz)
        for y in range(2)
        for c in range(2)
    ]


def hop_distances(hop, n):
    if hop == 0:
        return [0]
    return [-hop, hop] if hop < n // 2 else [hop]


def ring_hop(up, down, n):
    return [lax.ppermute(x, AXES, ring_perm(n, 1)) for x in up], [lax.ppermute(x, AXES, ring_perm(n, -1)) for x in down]


def join_kernel(ways, *refs):
    count = len(refs) - 1 - ways
    pieces, out, on = refs[:count], refs[count], refs[count + 1 :]
    first = 0
    for piece in pieces:
        out[first : first + piece.shape[0], :] = piece[...]
        first += piece.shape[0]
    arrived = pieces[len(pieces) - 2 * CHUNKS :]
    if ways == 1:
        c = lax.axis_index("adapter")
        rows = arrived[0].shape[0]
        for core in range(2):

            @pl.when(c == core)
            def _():
                for i, piece in enumerate(arrived[core * CHUNKS : (core + 1) * CHUNKS]):
                    on[0][i * rows : (i + 1) * rows, :] = piece[...]


def join(pieces, after, ways=0):
    (rows, depth), dtype = pieces[-1].shape, pieces[-1].dtype
    on = [CHUNKS * rows] * ways
    outs = [((count, depth), dtype) for count in [sum(x.shape[0] for x in pieces), *on]]
    return call(functools.partial(join_kernel, ways), pieces, after, outs)


def whole(count):
    return [pl.BlockSpec(memory_space=pltpu.VMEM)] * count


def in_vmem(arrays):
    return [pltpu.with_memory_space_constraint(x, pltpu.VMEM) for x in arrays]


def call(kernel, arrays, after, outs, scratch=(), limit=8, flops=0, outside=()):
    operands = len(arrays) + len(outside)

    def body(*refs):
        kernel(*refs[:operands], *refs[operands + len(after) :])

    return pl.pallas_call(
        body,
        out_shape=[pltpu.VMEM(shape, dtype) for shape, dtype in outs],
        in_specs=whole(len(arrays)) + [pl.BlockSpec(memory_space=pl.ANY)] * (len(outside) + len(after)),
        out_specs=whole(len(outs)),
        scratch_shapes=list(scratch),
        compiler_params=pltpu.CompilerParams(vmem_limit_bytes=limit << 20),
        cost_estimate=pl.CostEstimate(flops=flops, bytes_accessed=0, transcendentals=0),
    )(*in_vmem(arrays), *outside, *after)


class Window:
    def __init__(self, n, width, depth):
        self.width, self.depth = width, depth
        self.size = -(-(width + max(s * width % 128 for s in range(n))) // 128) * 128
        for s in range(n):
            start = s * width // 128 * 128
            assert start // depth == (start + self.size - 1) // depth

    def start(self, chip):
        return (chip * self.width) >> 7 << 7

    def shift(self, chip):
        return chip * self.width - self.start(chip)


def near_kernel(tokens, behind, ahead, factor, out, *chunks):
    held, rank, size = factor.shape
    rows, depth = chunks[0].shape
    for i, ref in enumerate((tokens, behind, ahead)):
        for k in range(CHUNKS):
            piece = ref[:, k * depth : (k + 1) * depth]
            at = (i * CHUNKS + k) * rows
            out[at : at + rows, :] = piece
            if i:
                chunks[(i - 1) * CHUNKS + k][...] = piece
    first = 3 * CHUNKS * rows
    out[first:, :] = jnp.zeros((rank, depth), out.dtype)
    for index in range(held):
        out[first:, index * size : (index + 1) * size] = factor[index]


def pack(parts, out):
    chips, rows, rank = parts.shape
    for t in range(chips):
        i, k = t % (chips // 2), t // (chips // 2)
        out[i * rows : (i + 1) * rows, k * rank : (k + 1) * rank] = parts[t].astype(out.dtype)


def partial_kernel(n, window, groups, far, *refs):
    *pieces, factor, other, adapters_ref, total, rounded, adapters, x, products, parts, sem = refs
    lookup = pltpu.make_async_copy(adapters_ref, adapters, sem)
    lookup.start()
    pieces, received = pieces[: len(groups)], pieces[len(groups) :]
    s, c = lax.axis_index("seq"), lax.axis_index("adapter")
    rows, size = received[0].shape
    held, rank, _ = factor.shape
    start = window.start(s)
    chunk = jnp.where(start >= window.depth, 1, 0)
    inside = pl.multiple_of(start - chunk * window.depth, 128)
    order = []
    for piece, distances in zip(pieces, groups):
        for i, distance in enumerate(distances):
            row = pl.multiple_of((i * CHUNKS + chunk) * rows, rows)
            x[len(order) * rows : (len(order) + 1) * rows, :] = piece[pl.ds(row, rows), pl.ds(inside, size)]
            order.append(distance)
    for piece, distance in zip(received, far):
        x[len(order) * rows : (len(order) + 1) * rows, :] = piece[...]
        order.append(distance)
    below = other.shape[0] - rank
    for index in range(held):
        theirs = other[below:, index * size : (index + 1) * size]
        for core, weights in ((c, factor[index]), (1 - c, theirs)):
            products[core * held + index] = lax.dot_general(
                x[...], weights, (((1,), (1,)), ((), ())), preferred_element_type=jnp.float32
            )
    lookup.wait()
    for i, distance in enumerate(order):
        chip = chip_at(distance, n)
        parts[chip] = products[adapters[chip * 2 * rows // BLOCK], i * rows : (i + 1) * rows, :]
    pack(parts, total)
    rounded[...] = total[...].astype(jnp.bfloat16)


def add_kernel(total, *refs):
    *received, out, rounded = refs
    value = total[...]
    for x in received:
        value += x[...].astype(jnp.float32)
    out[...] = value
    rounded[...] = value.astype(jnp.bfloat16)


def prepare_kernel(n, window, distances, tokens_ref, down_ref, factor, *refs):
    *sends, tokens, down, sems = refs
    copies = [
        pltpu.make_async_copy(source, to, sems.at[k])
        for k, (source, to) in enumerate(((tokens_ref, tokens), (down_ref, down)))
    ]
    for copy in copies:
        copy.start()
    copies[0].wait()
    for distance, send in zip(distances, sends):
        start = pl.multiple_of(window.start(chip_at(distance, n)), 128)
        send[...] = tokens[:, pl.ds(start, window.size)]
    copies[1].wait()
    zeros = jnp.zeros((down.shape[1], window.size - window.width), jnp.float32)
    for index in range(down.shape[0]):
        wide = jnp.concatenate([down[index], zeros], 1)
        factor[index] = pltpu.roll(wide, window.shift(lax.axis_index("seq")), 1).astype(jnp.bfloat16)


def full_rows(rows):
    return max(rows, 128)


def assemble_core(ref, chips, rows, held):
    depth = ref.shape[1]
    for i in range(chips):
        for k in range(CHUNKS):
            at = (i * CHUNKS + k) * rows
            held[i * rows : (i + 1) * rows, k * depth : (k + 1) * depth] = ref[at : at + rows, :]


def core_kernel(rows, ref, *refs):
    *weights, base, held = refs
    assemble_core(ref, base.shape[0] // rows, rows, held)
    columns = tile_width(base.shape[1])
    for j in range(0, base.shape[1], columns):
        at = slice(j, j + columns)
        base[:, at] = multiply(held, weights, at)[: base.shape[0]]


def both_kernel(rows, ref, mine, *refs):
    *weights, base, held = refs
    chips = base.shape[0] // (2 * rows)
    c = lax.axis_index("adapter")
    assemble_core(ref, chips, rows, held)
    columns = tile_width(base.shape[1])
    for j in range(0, base.shape[1], columns):
        at = slice(j, j + columns)
        tile = multiply(held, weights, at)
        for i in range(chips):
            here = slice(i * rows, (i + 1) * rows)
            for core, value in ((c, mine[here, at]), (1 - c, tile[here])):
                base[pl.ds(pl.multiple_of((2 * i + core) * rows, rows), rows), at] = value


def core_rows(ref, chips, rows, weights, after, mine=None):
    total, depth, width = rows * chips, sum(w.shape[0] for w in weights), weights[0].shape[1]
    (base,) = call(
        functools.partial(core_kernel if mine is None else both_kernel, rows),
        [ref] + ([] if mine is None else [mine]) + weights,
        after,
        [((total if mine is None else 2 * total, width), jnp.float32)],
        [pltpu.VMEM((full_rows(total), depth), jnp.bfloat16)],
        limit=8 + (2 * total * depth >> 20),
        flops=2 * total * depth * width,
    )
    return base


def cast_kernel(source, out):
    out[...] = source[...].astype(out.dtype)


def in_hbm(arrays):
    return [pltpu.with_memory_space_constraint(x, pltpu.HBM) for x in arrays]


def prepare(kernel, arrays, later, outs, scratch):
    operands = len(arrays)

    def body(*refs):
        kernel(*refs[:operands], *refs[operands + len(later) :])

    return pl.pallas_call(
        body,
        out_shape=[pltpu.VMEM(shape, dtype) for shape, dtype in outs],
        in_specs=[pl.BlockSpec(memory_space=pltpu.HBM)] * (operands + len(later)),
        out_specs=whole(len(outs)),
        scratch_shapes=scratch,
        compiler_params=pltpu.CompilerParams(vmem_limit_bytes=8 << 20),
        cost_estimate=pl.CostEstimate(flops=0, bytes_accessed=0, transcendentals=0),
    )(*in_hbm(arrays), *in_hbm(later))


def assemble(pairs, counts, rows, held):
    c = lax.axis_index("adapter")
    first = 0
    for pair, chips in zip(pairs, counts):
        depth = pair[0].shape[1]
        for chip in range(chips):
            for k in range(CHUNKS):
                at = (chip * CHUNKS + k) * rows
                for ref, core in zip(pair, (c, 1 - c)):
                    row = pl.multiple_of(first + core * rows, rows)
                    held[pl.ds(row, rows), k * depth : (k + 1) * depth] = ref[at : at + rows, :]
            first += 2 * rows


def tile_width(width):
    return 768 if width % 768 == 0 else width


def multiply(held, weights, at):
    total, first = 0.0, 0
    for w in weights:
        columns = held[:, first : first + w.shape[0]]
        total += jnp.dot(columns, w[:, at], preferred_element_type=jnp.float32)
        first += w.shape[0]
    return total


def base_kernel(rows, counts, *refs):
    count = 2 * len(counts)
    pairs, weights, (base, held) = refs[:count], refs[count:-2], refs[-2:]
    assemble(list(zip(pairs[::2], pairs[1::2])), counts, rows, held)
    width = base.shape[1]
    columns = tile_width(width)
    for j in range(0, width, columns):
        at = slice(j, j + columns)
        base[:, at] = multiply(held, weights, at)[: base.shape[0]]


def base_rows(pairs, counts, rows, weights, after):
    chips = sum(counts)
    total, depth, width = 2 * rows * chips, sum(w.shape[0] for w in weights), weights[0].shape[1]
    arrays = [x for pair in pairs for x in pair]
    (base,) = call(
        functools.partial(base_kernel, rows, counts),
        arrays + weights,
        after,
        [((total, width), jnp.float32)],
        [pltpu.VMEM((full_rows(total), depth), jnp.bfloat16)],
        limit=8 + (2 * total * depth >> 20),
        flops=2 * total * depth * width,
    )
    return base


def finish_kernel(n, rows, groups, adapters, live, *refs):
    *bases, own, other, up_ref = refs[: len(groups) + 3]
    out_ref, shrink, block, sems = refs[len(groups) + 3 :]
    c = lax.axis_index("adapter")
    chip_rows, rank = 2 * rows, up_ref.shape[1]
    tiles, _, columns = block.shape
    for t in range(n):
        i, k = t % (n // 2), t // (n // 2)
        for ref, core in ((own, c), (other, 1 - c)):
            part = ref[i * rows : (i + 1) * rows, k * rank : (k + 1) * rank]
            shrink[t, pl.ds(pl.multiple_of(core * rows, rows), rows), :] = part.astype(jnp.bfloat16)
    places = [
        (distance, base, i * chip_rows)
        for base, distances in zip(bases, groups)
        for i, distance in enumerate(distances)
    ]
    copies = []
    for j in range(tiles):
        at = slice(j * columns, (j + 1) * columns)
        for i, (distance, base, row) in enumerate(places):
            chip = chip_at(distance, n)
            first = chip * chip_rows
            of_block = first // BLOCK
            delta = jnp.dot(shrink[chip], up_ref[adapters[of_block], :, at], preferred_element_type=jnp.float32)
            index = lax.broadcasted_iota(jnp.int32, delta.shape, 0) + (first - of_block * BLOCK)
            total = jnp.where(index < live[of_block], base[row : row + chip_rows, at] + delta, 0.0)
            place = pl.ds(i * chip_rows, chip_rows)
            block[j, place, :] = total.astype(out_ref.dtype)
            copies.append(
                pltpu.make_async_copy(
                    block.at[j, place, :],
                    out_ref.at[pl.ds(pl.multiple_of(first, chip_rows), chip_rows), pl.ds(j * columns, columns)],
                    sems.at[j, i],
                )
            )
            copies[-1].start()
    for copy in copies:
        copy.wait()


def finish(n, rows, groups, scalars, bases, own, other, up):
    rank, width = up.shape[1:]
    total, columns = 2 * n * rows, tile_width(width)
    arrays = [*bases, own, other, up]
    return pl.pallas_call(
        functools.partial(finish_kernel, n, rows, groups),
        out_shape=jax.ShapeDtypeStruct((total, width), jnp.bfloat16),
        in_specs=[pl.BlockSpec(memory_space=pltpu.SMEM)] * len(scalars) + whole(len(arrays)),
        out_specs=pl.BlockSpec(memory_space=pl.ANY),
        scratch_shapes=[
            pltpu.VMEM((n, 2 * rows, rank), jnp.bfloat16),
            pltpu.VMEM((width // columns, total, columns), jnp.bfloat16),
            pltpu.SemaphoreType.DMA((width // columns, n)),
        ],
        compiler_params=pltpu.CompilerParams(vmem_limit_bytes=8 << 20),
        cost_estimate=pl.CostEstimate(
            flops=2 * total * rank * width, bytes_accessed=2 * total * width, transcendentals=0
        ),
    )(*scalars, *in_vmem(arrays))


def on_device(n, tokens, weight, down, up, adapter_per_block, rows_per_block):
    rows, features = tokens.shape
    depth = features // CHUNKS
    held, width, rank = down.shape
    last = n // 2
    adapters = adapter_per_block[:, 0]
    window = Window(n, width, depth)
    near, mid, far = ([d for hop in hops for d in hop_distances(hop, n)] for hops in ((0, 1), range(2, last - 1), [last - 1]))
    half = (n // 2 * rows, 2 * rank)
    sums = [(half, jnp.float32), (half, jnp.bfloat16)]

    (behind,), (ahead,) = ring_hop([tokens], [tokens], n)
    ends = far + [last]
    bf16 = jnp.bfloat16
    factor, *sends = prepare(
        functools.partial(prepare_kernel, n, window, ends),
        [tokens, jnp.swapaxes(down, 1, 2)],
        [weight, up],
        [((held, rank, window.size), bf16)] + [((rows, window.size), bf16)] * len(ends),
        [
            pltpu.VMEM(tokens.shape, tokens.dtype),
            pltpu.VMEM((held, rank, width), down.dtype),
            pltpu.SemaphoreType.DMA((2,)),
        ],
    )
    received = [lax.ppermute(x, AXES, ring_perm(n, d)) for d, x in zip(ends, sends)]
    come_from = [-d for d in far] + [last]
    piece = ((rows, depth), bf16)
    near_rows, *chunks = call(
        near_kernel,
        [tokens, behind, ahead, factor],
        received,
        [((len(near) * CHUNKS * rows + rank, depth), bf16)] + [piece] * (2 * CHUNKS),
    )

    up_way, down_way = chunks[:CHUNKS], chunks[CHUNKS:]
    weights = [weight]
    near_swapped = swap_cores(near_rows, n)
    mine = core_rows(near_rows, len(near), rows, weights, [])
    (up,) = call(cast_kernel, [up], [mine], [(up.shape, bf16)])
    arrived = []
    for _ in range(2, last - 1):
        up_way, down_way = ring_hop(up_way, down_way, n)
        arrived += up_way + down_way
    (mid_rows,) = join(arrived, [mine, up])

    total, rounded = call(
        functools.partial(partial_kernel, n, window, [near, mid], come_from),
        [near_rows, mid_rows, *received, factor, near_swapped],
        [],
        sums,
        [
            pltpu.SMEM(adapters.shape, jnp.int32),
            pltpu.VMEM((n * rows, window.size), bf16),
            pltpu.VMEM((2 * held, n * rows, rank), jnp.float32),
            pltpu.VMEM((n, rows, rank), jnp.float32),
            pltpu.SemaphoreType.DMA,
        ],
        outside=[adapters],
    )
    bases = [core_rows(near_swapped, len(near), rows, weights, [rounded], mine)]
    total, rounded = call(add_kernel, [total, lax.ppermute(rounded, AXES, y_perm(n))], [], sums)
    up_way, down_way = ring_hop(up_way, down_way, n)
    late_rows, turned = join([mid_rows, *up_way, *down_way], [rounded, *bases], 1)

    late = mid + far
    late_swapped = swap_cores(late_rows, n)
    mine = core_rows(late_rows, len(late), rows, weights, [])
    total, rounded = call(
        add_kernel,
        [total] + [lax.ppermute(rounded, AXES, z_perm(n, shift)) for shift in range(1, n // 2)],
        [],
        sums,
    )
    (last_rows,) = join([lax.ppermute(turned, AXES, ring_perm(n, 1, -1))], [rounded, mine])

    bases.append(core_rows(late_swapped, len(late), rows, weights, [last_rows], mine))
    last_pair = (last_rows, swap_cores(last_rows, n))
    bases.append(base_rows([last_pair], [1], rows, weights, bases[-1:]))
    return finish(
        n,
        rows,
        [near, late, [last]],
        [adapters, rows_per_block],
        bases,
        total,
        swap_cores(rounded, n),
        up,
    )


def solution(mesh):
    placed = (
        P(("groups", "seq", "adapter"), None),
        P(None, ("seq", "adapter")),
        P(("groups", "adapter"), "seq", None),
        P("groups", None, ("seq", "adapter")),
        P("groups", None),
        P("groups"),
    )
    return jax.shard_map(
        functools.partial(on_device, mesh.shape["seq"]),
        mesh=mesh,
        in_specs=placed,
        out_specs=P("groups", ("seq", "adapter")),
        check_vma=False,
    )
```

```python
import functools

import jax
import jax.numpy as jnp
from jax import lax
from jax.experimental import pallas as pl
from jax.experimental.pallas import tpu as pltpu
from jax.sharding import PartitionSpec as P

BLOCK = 128
AXES = ("seq", "adapter")
CHUNKS = 2


def ring_perm(n, way, other_way=None):
    order = [2 * z for z in range(n // 2)] + [2 * z + 1 for z in reversed(range(n // 2))]
    ways = (way, way if other_way is None else other_way)
    return [(2 * s + c, 2 * order[(pos + ways[c]) % n] + c) for pos, s in enumerate(order) for c in range(2)]


def swap_cores(x, n):
    return lax.ppermute(x, AXES, [(2 * s + c, 2 * s + 1 - c) for s in range(n) for c in range(2)])


def chip_at(distance, n):
    s = lax.axis_index("seq")
    z = s >> 1
    pos = jnp.where(s & 1 == 0, z, n - 1 - z) + distance
    pos = jnp.where(pos >= n, pos - n, pos)
    pos = jnp.where(pos < 0, pos + n, pos)
    return jnp.where(pos < n // 2, 2 * pos, 2 * (n - 1 - pos) + 1)


def y_perm(n):
    return [(2 * s + c, 2 * (s ^ 1) + c) for s in range(n) for c in range(2)]


def z_perm(n, shift):
    nz = n // 2
    return [
        (2 * (2 * z + y) + c, 2 * (2 * ((z - shift) % nz) + y) + c)
        for z in range(nz)
        for y in range(2)
        for c in range(2)
    ]


def hop_distances(hop, n):
    if hop == 0:
        return [0]
    return [-hop, hop] if hop < n // 2 else [hop]


def ring_hop(up, down, n):
    return [lax.ppermute(x, AXES, ring_perm(n, 1)) for x in up], [lax.ppermute(x, AXES, ring_perm(n, -1)) for x in down]


def join_kernel(ways, *refs):
    count = len(refs) - 1 - ways
    pieces, out, on = refs[:count], refs[count], refs[count + 1 :]
    first = 0
    for piece in pieces:
        out[first : first + piece.shape[0], :] = piece[...]
        first += piece.shape[0]
    arrived = pieces[len(pieces) - 2 * CHUNKS :]
    if ways == 1:
        c = lax.axis_index("adapter")
        rows = arrived[0].shape[0]
        for core in range(2):

            @pl.when(c == core)
            def _():
                for i, piece in enumerate(arrived[core * CHUNKS : (core + 1) * CHUNKS]):
                    on[0][i * rows : (i + 1) * rows, :] = piece[...]


def join(pieces, after, ways=0):
    (rows, depth), dtype = pieces[-1].shape, pieces[-1].dtype
    on = [CHUNKS * rows] * ways
    outs = [((count, depth), dtype) for count in [sum(x.shape[0] for x in pieces), *on]]
    return call(functools.partial(join_kernel, ways), pieces, after, outs)


def whole(count):
    return [pl.BlockSpec(memory_space=pltpu.VMEM)] * count


def in_vmem(arrays):
    return [pltpu.with_memory_space_constraint(x, pltpu.VMEM) for x in arrays]


def call(kernel, arrays, after, outs, scratch=(), limit=8, flops=0, outside=()):
    operands = len(arrays) + len(outside)

    def body(*refs):
        kernel(*refs[:operands], *refs[operands + len(after) :])

    return pl.pallas_call(
        body,
        out_shape=[pltpu.VMEM(shape, dtype) for shape, dtype in outs],
        in_specs=whole(len(arrays)) + [pl.BlockSpec(memory_space=pl.ANY)] * (len(outside) + len(after)),
        out_specs=whole(len(outs)),
        scratch_shapes=list(scratch),
        compiler_params=pltpu.CompilerParams(vmem_limit_bytes=limit << 20),
        cost_estimate=pl.CostEstimate(flops=flops, bytes_accessed=0, transcendentals=0),
    )(*in_vmem(arrays), *outside, *after)


class Window:
    def __init__(self, n, width, depth):
        self.width, self.depth = width, depth
        self.size = -(-(width + max(s * width % 128 for s in range(n))) // 128) * 128
        for s in range(n):
            start = s * width // 128 * 128
            assert start // depth == (start + self.size - 1) // depth

    def start(self, chip):
        return (chip * self.width) >> 7 << 7

    def shift(self, chip):
        return chip * self.width - self.start(chip)


def near_kernel(tokens, behind, ahead, factor, out, *chunks):
    held, rank, size = factor.shape
    rows, depth = chunks[0].shape
    for i, ref in enumerate((tokens, behind, ahead)):
        for k in range(CHUNKS):
            piece = ref[:, k * depth : (k + 1) * depth]
            at = (i * CHUNKS + k) * rows
            out[at : at + rows, :] = piece
            if i:
                chunks[(i - 1) * CHUNKS + k][...] = piece
    first = 3 * CHUNKS * rows
    out[first:, :] = jnp.zeros((rank, depth), out.dtype)
    for index in range(held):
        out[first:, index * size : (index + 1) * size] = factor[index]


def pack(parts, out):
    chips, rows, rank = parts.shape
    for t in range(chips):
        i, k = t % (chips // 2), t // (chips // 2)
        out[i * rows : (i + 1) * rows, k * rank : (k + 1) * rank] = parts[t].astype(out.dtype)


def partial_kernel(n, window, groups, far, *refs):
    *pieces, factor, other, adapters_ref, total, rounded, adapters, x, products, parts, sem = refs
    lookup = pltpu.make_async_copy(adapters_ref, adapters, sem)
    lookup.start()
    pieces, received = pieces[: len(groups)], pieces[len(groups) :]
    s, c = lax.axis_index("seq"), lax.axis_index("adapter")
    rows, size = received[0].shape
    held, rank, _ = factor.shape
    start = window.start(s)
    chunk = jnp.where(start >= window.depth, 1, 0)
    inside = pl.multiple_of(start - chunk * window.depth, 128)
    order = []
    for piece, distances in zip(pieces, groups):
        for i, distance in enumerate(distances):
            row = pl.multiple_of((i * CHUNKS + chunk) * rows, rows)
            x[len(order) * rows : (len(order) + 1) * rows, :] = piece[pl.ds(row, rows), pl.ds(inside, size)]
            order.append(distance)
    for piece, distance in zip(received, far):
        x[len(order) * rows : (len(order) + 1) * rows, :] = piece[...]
        order.append(distance)
    below = other.shape[0] - rank
    for index in range(held):
        theirs = other[below:, index * size : (index + 1) * size]
        for core, weights in ((c, factor[index]), (1 - c, theirs)):
            products[core * held + index] = lax.dot_general(
                x[...], weights, (((1,), (1,)), ((), ())), preferred_element_type=jnp.float32
            )
    lookup.wait()
    for i, distance in enumerate(order):
        chip = chip_at(distance, n)
        parts[chip] = products[adapters[chip * 2 * rows // BLOCK], i * rows : (i + 1) * rows, :]
    pack(parts, total)
    rounded[...] = total[...].astype(jnp.bfloat16)


def add_kernel(total, *refs):
    *received, out, rounded = refs
    value = total[...]
    for x in received:
        value += x[...].astype(jnp.float32)
    out[...] = value
    rounded[...] = value.astype(jnp.bfloat16)


def prepare_kernel(n, window, distances, tokens, down_ref, factor, *refs):
    *sends, down, sems = refs
    copies = [pltpu.make_async_copy(down_ref, down, sems.at[0])]
    for k, (distance, send) in enumerate(zip(distances, sends)):
        start = pl.multiple_of(window.start(chip_at(distance, n)), 128)
        copies.append(pltpu.make_async_copy(tokens.at[:, pl.ds(start, window.size)], send, sems.at[1 + k]))
    for copy in copies:
        copy.start()
    copies[0].wait()
    zeros = jnp.zeros((down.shape[1], window.size - window.width), jnp.float32)
    for index in range(down.shape[0]):
        wide = jnp.concatenate([down[index], zeros], 1)
        factor[index] = pltpu.roll(wide, window.shift(lax.axis_index("seq")), 1).astype(jnp.bfloat16)
    for copy in copies[1:]:
        copy.wait()


def full_rows(rows):
    return max(rows, 128)


def assemble_core(ref, chips, rows, held):
    depth = ref.shape[1]
    for i in range(chips):
        for k in range(CHUNKS):
            at = (i * CHUNKS + k) * rows
            held[i * rows : (i + 1) * rows, k * depth : (k + 1) * depth] = ref[at : at + rows, :]


def core_kernel(rows, ref, *refs):
    *weights, base, held = refs
    assemble_core(ref, base.shape[0] // rows, rows, held)
    columns = tile_width(base.shape[1])
    for j in range(0, base.shape[1], columns):
        at = slice(j, j + columns)
        base[:, at] = multiply(held, weights, at)[: base.shape[0]]


def both_kernel(rows, ref, mine, *refs):
    *weights, base, held = refs
    chips = base.shape[0] // (2 * rows)
    c = lax.axis_index("adapter")
    assemble_core(ref, chips, rows, held)
    columns = tile_width(base.shape[1])
    for j in range(0, base.shape[1], columns):
        at = slice(j, j + columns)
        tile = multiply(held, weights, at)
        for i in range(chips):
            here = slice(i * rows, (i + 1) * rows)
            for core, value in ((c, mine[here, at]), (1 - c, tile[here])):
                base[pl.ds(pl.multiple_of((2 * i + core) * rows, rows), rows), at] = value


def core_rows(ref, chips, rows, weights, after, mine=None):
    total, depth, width = rows * chips, sum(w.shape[0] for w in weights), weights[0].shape[1]
    (base,) = call(
        functools.partial(core_kernel if mine is None else both_kernel, rows),
        [ref] + ([] if mine is None else [mine]) + weights,
        after,
        [((total if mine is None else 2 * total, width), jnp.float32)],
        [pltpu.VMEM((full_rows(total), depth), jnp.bfloat16)],
        limit=8 + (2 * total * depth >> 20),
        flops=2 * total * depth * width,
    )
    return base


def cast_kernel(source, out):
    out[...] = source[...].astype(out.dtype)


def in_hbm(arrays):
    return [pltpu.with_memory_space_constraint(x, pltpu.HBM) for x in arrays]


def prepare(kernel, arrays, later, outs, scratch):
    operands = len(arrays)

    def body(*refs):
        kernel(*refs[:operands], *refs[operands + len(later) :])

    return pl.pallas_call(
        body,
        out_shape=[pltpu.VMEM(shape, dtype) for shape, dtype in outs],
        in_specs=[pl.BlockSpec(memory_space=pltpu.HBM)] * (operands + len(later)),
        out_specs=whole(len(outs)),
        scratch_shapes=scratch,
        compiler_params=pltpu.CompilerParams(vmem_limit_bytes=8 << 20),
        cost_estimate=pl.CostEstimate(flops=0, bytes_accessed=0, transcendentals=0),
    )(*in_hbm(arrays), *in_hbm(later))


def assemble(pairs, counts, rows, held):
    c = lax.axis_index("adapter")
    first = 0
    for pair, chips in zip(pairs, counts):
        depth = pair[0].shape[1]
        for chip in range(chips):
            for k in range(CHUNKS):
                at = (chip * CHUNKS + k) * rows
                for ref, core in zip(pair, (c, 1 - c)):
                    row = pl.multiple_of(first + core * rows, rows)
                    held[pl.ds(row, rows), k * depth : (k + 1) * depth] = ref[at : at + rows, :]
            first += 2 * rows


def tile_width(width):
    return 768 if width % 768 == 0 else width


def multiply(held, weights, at):
    total, first = 0.0, 0
    for w in weights:
        columns = held[:, first : first + w.shape[0]]
        total += jnp.dot(columns, w[:, at], preferred_element_type=jnp.float32)
        first += w.shape[0]
    return total


def finish_kernel(n, rows, groups, skipped, *refs):
    count = len(groups) - 1
    bases, refs = refs[:count], refs[count:]
    mine, others, weight, own, other, up_ref, adapters_ref, live_ref = refs[:8]
    out_ref, held, shrink, block, adapters, live, sems, small_sems = refs[8 + skipped :]
    lookups = [
        pltpu.make_async_copy(source, to, small_sems.at[k])
        for k, (source, to) in enumerate(((adapters_ref, adapters), (live_ref, live)))
    ]
    for lookup in lookups:
        lookup.start()
    c = lax.axis_index("adapter")
    chip_rows, rank = 2 * rows, up_ref.shape[1]
    tiles, _, columns = block.shape
    assemble([(mine, others)], [1], rows, held)
    for t in range(n):
        i, k = t % (n // 2), t // (n // 2)
        for ref, core in ((own, c), (other, 1 - c)):
            part = ref[i * rows : (i + 1) * rows, k * rank : (k + 1) * rank]
            shrink[t, pl.ds(pl.multiple_of(core * rows, rows), rows), :] = part.astype(jnp.bfloat16)
    places = [
        (distance, base, i * chip_rows)
        for base, distances in zip([*bases, None], groups)
        for i, distance in enumerate(distances)
    ]
    for lookup in lookups:
        lookup.wait()
    copies = []
    for j in range(tiles):
        at = slice(j * columns, (j + 1) * columns)
        last = multiply(held, [weight], at)
        for i, (distance, base, row) in enumerate(places):
            chip = chip_at(distance, n)
            first = chip * chip_rows
            of_block = first // BLOCK
            delta = jnp.dot(shrink[chip], up_ref[adapters[of_block], :, at], preferred_element_type=jnp.float32)
            index = lax.broadcasted_iota(jnp.int32, delta.shape, 0) + (first - of_block * BLOCK)
            value = last[:chip_rows] if base is None else base[row : row + chip_rows, at]
            place = pl.ds(i * chip_rows, chip_rows)
            block[j, place, :] = jnp.where(index < live[of_block], value + delta, 0.0).astype(out_ref.dtype)
            copies.append(
                pltpu.make_async_copy(
                    block.at[j, place, :],
                    out_ref.at[pl.ds(pl.multiple_of(first, chip_rows), chip_rows), pl.ds(j * columns, columns)],
                    sems.at[j, i],
                )
            )
            copies[-1].start()
    for copy in copies:
        copy.wait()


def finish(n, rows, groups, lookups, bases, last_pair, weight, sums, up, after):
    (rank, width), depth = up.shape[1:], weight.shape[0]
    total, columns = 2 * n * rows, tile_width(width)
    arrays = [*bases, *last_pair, weight, *sums, up]
    held = full_rows(2 * rows)
    return pl.pallas_call(
        functools.partial(finish_kernel, n, rows, groups, len(after)),
        out_shape=jax.ShapeDtypeStruct((total, width), jnp.bfloat16),
        in_specs=whole(len(arrays)) + [pl.BlockSpec(memory_space=pl.ANY)] * (len(lookups) + len(after)),
        out_specs=pl.BlockSpec(memory_space=pl.ANY),
        scratch_shapes=[
            pltpu.VMEM((held, depth), jnp.bfloat16),
            pltpu.VMEM((n, 2 * rows, rank), jnp.bfloat16),
            pltpu.VMEM((width // columns, total, columns), jnp.bfloat16),
            *(pltpu.SMEM(x.shape, x.dtype) for x in lookups),
            pltpu.SemaphoreType.DMA((width // columns, n)),
            pltpu.SemaphoreType.DMA((len(lookups),)),
        ],
        compiler_params=pltpu.CompilerParams(vmem_limit_bytes=10 << 20),
        cost_estimate=pl.CostEstimate(
            flops=2 * held * depth * width, bytes_accessed=2 * total * width, transcendentals=0
        ),
    )(*in_vmem(arrays), *lookups, *after)


def on_device(n, tokens, weight, down, up, adapter_per_block, rows_per_block):
    rows, features = tokens.shape
    depth = features // CHUNKS
    held, width, rank = down.shape
    last = n // 2
    adapters = adapter_per_block[:, 0]
    window = Window(n, width, depth)
    near, mid, far = ([d for hop in hops for d in hop_distances(hop, n)] for hops in ((0, 1), range(2, last - 1), [last - 1]))
    half = (n // 2 * rows, 2 * rank)
    sums = [(half, jnp.float32), (half, jnp.bfloat16)]

    (behind,), (ahead,) = ring_hop([tokens], [tokens], n)
    ends = far + [last]
    bf16 = jnp.bfloat16
    factor, *sends = prepare(
        functools.partial(prepare_kernel, n, window, ends),
        [tokens, jnp.swapaxes(down, 1, 2)],
        [weight, up],
        [((held, rank, window.size), bf16)] + [((rows, window.size), bf16)] * len(ends),
        [
            pltpu.VMEM((held, rank, width), down.dtype),
            pltpu.SemaphoreType.DMA((1 + len(ends),)),
        ],
    )
    received = [lax.ppermute(x, AXES, ring_perm(n, d)) for d, x in zip(ends, sends)]
    come_from = [-d for d in far] + [last]
    piece = ((rows, depth), bf16)
    near_rows, *chunks = call(
        near_kernel,
        [tokens, behind, ahead, factor],
        received,
        [((len(near) * CHUNKS * rows + rank, depth), bf16)] + [piece] * (2 * CHUNKS),
    )

    up_way, down_way = chunks[:CHUNKS], chunks[CHUNKS:]
    weights = [weight]
    near_swapped = swap_cores(near_rows, n)
    mine = core_rows(near_rows, len(near), rows, weights, [])
    (up,) = call(cast_kernel, [up], [mine], [(up.shape, bf16)])
    arrived = []
    for _ in range(2, last - 1):
        up_way, down_way = ring_hop(up_way, down_way, n)
        arrived += up_way + down_way
    (mid_rows,) = join(arrived, [mine, up])

    total, rounded = call(
        functools.partial(partial_kernel, n, window, [near, mid], come_from),
        [near_rows, mid_rows, *received, factor, near_swapped],
        [],
        sums,
        [
            pltpu.SMEM(adapters.shape, jnp.int32),
            pltpu.VMEM((n * rows, window.size), bf16),
            pltpu.VMEM((2 * held, n * rows, rank), jnp.float32),
            pltpu.VMEM((n, rows, rank), jnp.float32),
            pltpu.SemaphoreType.DMA,
        ],
        outside=[adapters],
    )
    bases = [core_rows(near_swapped, len(near), rows, weights, [rounded], mine)]
    total, rounded = call(add_kernel, [total, lax.ppermute(rounded, AXES, y_perm(n))], [], sums)
    up_way, down_way = ring_hop(up_way, down_way, n)
    late_rows, turned = join([mid_rows, *up_way, *down_way], [rounded, *bases], 1)

    late = mid + far
    late_swapped = swap_cores(late_rows, n)
    mine = core_rows(late_rows, len(late), rows, weights, [])
    total, rounded = call(
        add_kernel,
        [total] + [lax.ppermute(rounded, AXES, z_perm(n, shift)) for shift in range(1, n // 2)],
        [],
        sums,
    )
    (last_rows,) = join([lax.ppermute(turned, AXES, ring_perm(n, 1, -1))], [rounded, mine])

    bases.append(core_rows(late_swapped, len(late), rows, weights, [last_rows], mine))
    last_pair = (last_rows, swap_cores(last_rows, n))
    return finish(
        n,
        rows,
        [near, late, [last]],
        [adapters, rows_per_block],
        bases,
        last_pair,
        weight,
        [total, swap_cores(rounded, n)],
        up,
        [],
    )


def solution(mesh):
    placed = (
        P(("groups", "seq", "adapter"), None),
        P(None, ("seq", "adapter")),
        P(("groups", "adapter"), "seq", None),
        P("groups", None, ("seq", "adapter")),
        P("groups", None),
        P("groups"),
    )
    return jax.shard_map(
        functools.partial(on_device, mesh.shape["seq"]),
        mesh=mesh,
        in_specs=placed,
        out_specs=P("groups", ("seq", "adapter")),
        check_vma=False,
    )
```

```python
import functools

import jax
import jax.numpy as jnp
from jax import lax
from jax.experimental import pallas as pl
from jax.experimental.pallas import tpu as pltpu
from jax.sharding import PartitionSpec as P

BLOCK = 128
AXES = ("seq", "adapter")
CHUNKS = 2


def ring_perm(n, way, other_way=None):
    order = [2 * z for z in range(n // 2)] + [2 * z + 1 for z in reversed(range(n // 2))]
    ways = (way, way if other_way is None else other_way)
    return [(2 * s + c, 2 * order[(pos + ways[c]) % n] + c) for pos, s in enumerate(order) for c in range(2)]


def swap_cores(x, n):
    return lax.ppermute(x, AXES, [(2 * s + c, 2 * s + 1 - c) for s in range(n) for c in range(2)])


def chip_at(distance, n):
    s = lax.axis_index("seq")
    z = s >> 1
    pos = jnp.where(s & 1 == 0, z, n - 1 - z) + distance
    pos = jnp.where(pos >= n, pos - n, pos)
    pos = jnp.where(pos < 0, pos + n, pos)
    return jnp.where(pos < n // 2, 2 * pos, 2 * (n - 1 - pos) + 1)


def y_perm(n):
    return [(2 * s + c, 2 * (s ^ 1) + c) for s in range(n) for c in range(2)]


def z_perm(n, shift):
    nz = n // 2
    return [
        (2 * (2 * z + y) + c, 2 * (2 * ((z - shift) % nz) + y) + c)
        for z in range(nz)
        for y in range(2)
        for c in range(2)
    ]


def hop_distances(hop, n):
    if hop == 0:
        return [0]
    return [-hop, hop] if hop < n // 2 else [hop]


def ring_hop(up, down, n):
    return [lax.ppermute(x, AXES, ring_perm(n, 1)) for x in up], [lax.ppermute(x, AXES, ring_perm(n, -1)) for x in down]


def join_kernel(ways, *refs):
    count = len(refs) - 1 - ways
    pieces, out, on = refs[:count], refs[count], refs[count + 1 :]
    first = 0
    for piece in pieces:
        out[first : first + piece.shape[0], :] = piece[...]
        first += piece.shape[0]
    arrived = pieces[len(pieces) - 2 * CHUNKS :]
    if ways == 1:
        c = lax.axis_index("adapter")
        rows = arrived[0].shape[0]
        for core in range(2):

            @pl.when(c == core)
            def _():
                for i, piece in enumerate(arrived[core * CHUNKS : (core + 1) * CHUNKS]):
                    on[0][i * rows : (i + 1) * rows, :] = piece[...]


def join(pieces, after, ways=0):
    (rows, depth), dtype = pieces[-1].shape, pieces[-1].dtype
    on = [CHUNKS * rows] * ways
    outs = [((count, depth), dtype) for count in [sum(x.shape[0] for x in pieces), *on]]
    return call(functools.partial(join_kernel, ways), pieces, after, outs)


def whole(count):
    return [pl.BlockSpec(memory_space=pltpu.VMEM)] * count


def in_vmem(arrays):
    return [pltpu.with_memory_space_constraint(x, pltpu.VMEM) for x in arrays]


def call(kernel, arrays, after, outs, scratch=(), limit=8, flops=0, outside=()):
    operands = len(arrays) + len(outside)

    def body(*refs):
        kernel(*refs[:operands], *refs[operands + len(after) :])

    return pl.pallas_call(
        body,
        out_shape=[pltpu.VMEM(shape, dtype) for shape, dtype in outs],
        in_specs=whole(len(arrays)) + [pl.BlockSpec(memory_space=pl.ANY)] * (len(outside) + len(after)),
        out_specs=whole(len(outs)),
        scratch_shapes=list(scratch),
        compiler_params=pltpu.CompilerParams(vmem_limit_bytes=limit << 20),
        cost_estimate=pl.CostEstimate(flops=flops, bytes_accessed=0, transcendentals=0),
    )(*in_vmem(arrays), *outside, *after)


class Window:
    def __init__(self, n, width, depth):
        self.width, self.depth = width, depth
        self.size = -(-(width + max(s * width % 128 for s in range(n))) // 128) * 128
        for s in range(n):
            start = s * width // 128 * 128
            assert start // depth == (start + self.size - 1) // depth

    def start(self, chip):
        return (chip * self.width) >> 7 << 7

    def shift(self, chip):
        return chip * self.width - self.start(chip)


def near_kernel(tokens, behind, ahead, factor, out, *chunks):
    held, rank, size = factor.shape
    rows, depth = chunks[0].shape
    for i, ref in enumerate((tokens, behind, ahead)):
        for k in range(CHUNKS):
            piece = ref[:, k * depth : (k + 1) * depth]
            at = (i * CHUNKS + k) * rows
            out[at : at + rows, :] = piece
            if i:
                chunks[(i - 1) * CHUNKS + k][...] = piece
    first = 3 * CHUNKS * rows
    out[first:, :] = jnp.zeros((rank, depth), out.dtype)
    for index in range(held):
        out[first:, index * size : (index + 1) * size] = factor[index]


def pack(parts, out):
    chips, rows, rank = parts.shape
    for t in range(chips):
        i, k = t % (chips // 2), t // (chips // 2)
        out[i * rows : (i + 1) * rows, k * rank : (k + 1) * rank] = parts[t].astype(out.dtype)


def partial_kernel(n, window, groups, far, *refs):
    *pieces, factor, other, adapters_ref, total, rounded, adapters, x, products, parts, sem = refs
    lookup = pltpu.make_async_copy(adapters_ref, adapters, sem)
    lookup.start()
    pieces, received = pieces[: len(groups)], pieces[len(groups) :]
    s, c = lax.axis_index("seq"), lax.axis_index("adapter")
    rows, size = received[0].shape
    held, rank, _ = factor.shape
    start = window.start(s)
    chunk = jnp.where(start >= window.depth, 1, 0)
    inside = pl.multiple_of(start - chunk * window.depth, 128)
    order = []
    for piece, distances in zip(pieces, groups):
        for i, distance in enumerate(distances):
            row = pl.multiple_of((i * CHUNKS + chunk) * rows, rows)
            x[len(order) * rows : (len(order) + 1) * rows, :] = piece[pl.ds(row, rows), pl.ds(inside, size)]
            order.append(distance)
    for piece, distance in zip(received, far):
        x[len(order) * rows : (len(order) + 1) * rows, :] = piece[...]
        order.append(distance)
    below = other.shape[0] - rank
    for index in range(held):
        theirs = other[below:, index * size : (index + 1) * size]
        for core, weights in ((c, factor[index]), (1 - c, theirs)):
            products[core * held + index] = lax.dot_general(
                x[...], weights, (((1,), (1,)), ((), ())), preferred_element_type=jnp.float32
            )
    lookup.wait()
    for i, distance in enumerate(order):
        chip = chip_at(distance, n)
        parts[chip] = products[adapters[chip * 2 * rows // BLOCK], i * rows : (i + 1) * rows, :]
    pack(parts, total)
    rounded[...] = total[...].astype(jnp.bfloat16)


def add_kernel(total, *refs):
    *received, out, rounded = refs
    value = total[...]
    for x in received:
        value += x[...].astype(jnp.float32)
    out[...] = value
    rounded[...] = value.astype(jnp.bfloat16)


def prepare_kernel(n, window, distances, tokens, down_ref, factor, *refs):
    *sends, down, sems = refs
    copies = [pltpu.make_async_copy(down_ref, down, sems.at[0])]
    for k, (distance, send) in enumerate(zip(distances, sends)):
        start = pl.multiple_of(window.start(chip_at(distance, n)), 128)
        copies.append(pltpu.make_async_copy(tokens.at[:, pl.ds(start, window.size)], send, sems.at[1 + k]))
    for copy in copies:
        copy.start()
    copies[0].wait()
    zeros = jnp.zeros((down.shape[1], window.size - window.width), jnp.float32)
    for index in range(down.shape[0]):
        wide = jnp.concatenate([down[index], zeros], 1)
        factor[index] = pltpu.roll(wide, window.shift(lax.axis_index("seq")), 1).astype(jnp.bfloat16)
    for copy in copies[1:]:
        copy.wait()


def full_rows(rows):
    return max(rows, 128)


def assemble_core(ref, chips, rows, held, skip=0, first=0):
    depth = ref.shape[1]
    for i in range(chips):
        for k in range(CHUNKS):
            at = ((skip + i) * CHUNKS + k) * rows
            held[first + i * rows : first + (i + 1) * rows, k * depth : (k + 1) * depth] = ref[at : at + rows, :]


def interleave(rows, chips, mine, others, base, at):
    c = lax.axis_index("adapter")
    for i in range(chips):
        here = slice(i * rows, (i + 1) * rows)
        for core, value in ((c, mine[here]), (1 - c, others[here])):
            base[pl.ds(pl.multiple_of((2 * i + core) * rows, rows), rows), at] = value


def core_kernel(rows, ref, *refs):
    *weights, base, held = refs
    assemble_core(ref, base.shape[0] // rows, rows, held)
    columns = tile_width(base.shape[1])
    for j in range(0, base.shape[1], columns):
        at = slice(j, j + columns)
        base[:, at] = multiply(held, weights, at)[: base.shape[0]]


def near_base_kernel(rows, near, mid, swapped, mine, mid_rows, weight, base, mid_base, held):
    assemble_core(swapped, near, rows, held)
    assemble_core(mid_rows, mid, rows, held, 0, near * rows)
    columns = tile_width(base.shape[1])
    for j in range(0, base.shape[1], columns):
        at = slice(j, j + columns)
        tile = multiply(held, [weight], at)
        interleave(rows, near, mine[: near * rows, at], tile, base, at)
        mid_base[:, at] = tile[near * rows : (near + mid) * rows]


def late_base_kernel(rows, mid, far, swapped, mine, weight, base, far_base, held):
    assemble_core(swapped, mid + far, rows, held)
    columns = tile_width(base.shape[1])
    for j in range(0, base.shape[1], columns):
        at = slice(j, j + columns)
        tile = multiply(held, [weight], at)
        interleave(rows, mid, mine[:, at], tile, base, at)
        far_base[:, at] = tile[mid * rows : (mid + far) * rows]


def product(kernel, arrays, weight, after, total, outs):
    (depth, width), total = weight.shape, full_rows(total)
    return call(
        kernel,
        [*arrays, weight],
        after,
        [((rows, width), jnp.float32) for rows in outs],
        [pltpu.VMEM((total, depth), jnp.bfloat16)],
        limit=8 + (2 * total * depth >> 20),
        flops=2 * total * depth * width,
    )


def cast_kernel(source, out):
    out[...] = source[...].astype(out.dtype)


def in_hbm(arrays):
    return [pltpu.with_memory_space_constraint(x, pltpu.HBM) for x in arrays]


def prepare(kernel, arrays, later, outs, scratch):
    operands = len(arrays)

    def body(*refs):
        kernel(*refs[:operands], *refs[operands + len(later) :])

    return pl.pallas_call(
        body,
        out_shape=[pltpu.VMEM(shape, dtype) for shape, dtype in outs],
        in_specs=[pl.BlockSpec(memory_space=pltpu.HBM)] * (operands + len(later)),
        out_specs=whole(len(outs)),
        scratch_shapes=scratch,
        compiler_params=pltpu.CompilerParams(vmem_limit_bytes=8 << 20),
        cost_estimate=pl.CostEstimate(flops=0, bytes_accessed=0, transcendentals=0),
    )(*in_hbm(arrays), *in_hbm(later))


def assemble(pairs, counts, rows, held):
    c = lax.axis_index("adapter")
    first = 0
    for pair, chips in zip(pairs, counts):
        depth = pair[0].shape[1]
        for chip in range(chips):
            for k in range(CHUNKS):
                at = (chip * CHUNKS + k) * rows
                for ref, core in zip(pair, (c, 1 - c)):
                    row = pl.multiple_of(first + core * rows, rows)
                    held[pl.ds(row, rows), k * depth : (k + 1) * depth] = ref[at : at + rows, :]
            first += 2 * rows


def tile_width(width):
    return 768 if width % 768 == 0 else width


def multiply(held, weights, at):
    total, first = 0.0, 0
    for w in weights:
        columns = held[:, first : first + w.shape[0]]
        total += jnp.dot(columns, w[:, at], preferred_element_type=jnp.float32)
        first += w.shape[0]
    return total


def finish_kernel(n, rows, groups, *refs):
    near_base, mid_base, far_base, late_rows, mine, others, weight, own, other, up_ref = refs[:10]
    adapters_ref, live_ref, out_ref, held, shrink, far_rows, block, adapters, live, sems, small_sems = refs[10:]
    lookups = [
        pltpu.make_async_copy(source, to, small_sems.at[k])
        for k, (source, to) in enumerate(((adapters_ref, adapters), (live_ref, live)))
    ]
    for lookup in lookups:
        lookup.start()
    c = lax.axis_index("adapter")
    chip_rows, rank = 2 * rows, up_ref.shape[1]
    tiles, _, columns = block.shape
    _, mid, far, _ = (len(group) for group in groups)
    assemble([(mine, others)], [1], rows, held)
    assemble_core(late_rows, far, rows, held, mid, chip_rows)
    for t in range(n):
        i, k = t % (n // 2), t // (n // 2)
        for ref, core in ((own, c), (other, 1 - c)):
            part = ref[i * rows : (i + 1) * rows, k * rank : (k + 1) * rank]
            shrink[t, pl.ds(pl.multiple_of(core * rows, rows), rows), :] = part.astype(jnp.bfloat16)
    for lookup in lookups:
        lookup.wait()
    early = [(base, i) for base, group in ((near_base, groups[0]), (mid_base, groups[1])) for i in range(len(group))]
    sources = [distance for group in groups for distance in group]
    copies = []

    def put(j, which, value_of):
        at = slice(j * columns, (j + 1) * columns)
        for i in which:
            first = chip_at(sources[i], n) * chip_rows
            of_block = first // BLOCK
            delta = jnp.dot(
                shrink[chip_at(sources[i], n)],
                up_ref[adapters[of_block], :, at],
                preferred_element_type=jnp.float32,
            )
            index = lax.broadcasted_iota(jnp.int32, delta.shape, 0) + (first - of_block * BLOCK)
            value = jnp.where(index < live[of_block], value_of(i, at) + delta, 0.0)
            block[j, i * chip_rows : (i + 1) * chip_rows, :] = value.astype(out_ref.dtype)

    def send(j, which):
        for i in which:
            first = pl.multiple_of(chip_at(sources[i], n) * chip_rows, chip_rows)
            copies.append(
                pltpu.make_async_copy(
                    block.at[j, pl.ds(i * chip_rows, chip_rows), :],
                    out_ref.at[pl.ds(first, chip_rows), pl.ds(j * columns, columns)],
                    sems.at[j, i],
                )
            )
            copies[-1].start()

    def early_value(i, at):
        base, k = early[i]
        return base[k * chip_rows : (k + 1) * chip_rows, at]

    begun, rest = range(len(early)), range(len(early), n)
    tile = None
    for j in range(tiles + 1):
        done, tile = tile, multiply(held, [weight], slice(j * columns, (j + 1) * columns)) if j < tiles else None
        if j < tiles:
            put(j, begun, early_value)
        if done is not None:
            at = slice((j - 1) * columns, j * columns)
            own_far = done[chip_rows : chip_rows + far * rows]
            interleave(rows, far, own_far, far_base[:, at], far_rows, slice(0, columns))

            def rest_value(i, at, done=done):
                k = i - len(early)
                return far_rows[k * chip_rows : (k + 1) * chip_rows, :] if k < far else done[:chip_rows]

            put(j - 1, rest, rest_value)
        if j < tiles:
            send(j, begun)
        if done is not None:
            send(j - 1, rest)
    for copy in copies:
        copy.wait()


def finish(n, rows, groups, lookups, bases, late, weight, sums, up):
    (rank, width), depth = up.shape[1:], weight.shape[0]
    total, columns = 2 * n * rows, tile_width(width)
    arrays = [*bases, *late, weight, *sums, up]
    far = len(groups[2])
    held = full_rows((2 + far) * rows)
    return pl.pallas_call(
        functools.partial(finish_kernel, n, rows, groups),
        out_shape=jax.ShapeDtypeStruct((total, width), jnp.bfloat16),
        in_specs=whole(len(arrays)) + [pl.BlockSpec(memory_space=pl.ANY)] * len(lookups),
        out_specs=pl.BlockSpec(memory_space=pl.ANY),
        scratch_shapes=[
            pltpu.VMEM((held, depth), jnp.bfloat16),
            pltpu.VMEM((n, 2 * rows, rank), jnp.bfloat16),
            pltpu.VMEM((2 * far * rows, columns), jnp.float32),
            pltpu.VMEM((width // columns, total, columns), jnp.bfloat16),
            *(pltpu.SMEM(x.shape, x.dtype) for x in lookups),
            pltpu.SemaphoreType.DMA((width // columns, n)),
            pltpu.SemaphoreType.DMA((len(lookups),)),
        ],
        compiler_params=pltpu.CompilerParams(vmem_limit_bytes=10 << 20),
        cost_estimate=pl.CostEstimate(
            flops=2 * held * depth * width, bytes_accessed=2 * total * width, transcendentals=0
        ),
    )(*in_vmem(arrays), *lookups)


def on_device(n, tokens, weight, down, up, adapter_per_block, rows_per_block):
    rows, features = tokens.shape
    depth = features // CHUNKS
    held, width, rank = down.shape
    last = n // 2
    adapters = adapter_per_block[:, 0]
    window = Window(n, width, depth)
    near, mid, far = ([d for hop in hops for d in hop_distances(hop, n)] for hops in ((0, 1), range(2, last - 1), [last - 1]))
    half = (n // 2 * rows, 2 * rank)
    sums = [(half, jnp.float32), (half, jnp.bfloat16)]

    (behind,), (ahead,) = ring_hop([tokens], [tokens], n)
    ends = far + [last]
    bf16 = jnp.bfloat16
    factor, *sends = prepare(
        functools.partial(prepare_kernel, n, window, ends),
        [tokens, jnp.swapaxes(down, 1, 2)],
        [weight, up],
        [((held, rank, window.size), bf16)] + [((rows, window.size), bf16)] * len(ends),
        [
            pltpu.VMEM((held, rank, width), down.dtype),
            pltpu.SemaphoreType.DMA((1 + len(ends),)),
        ],
    )
    received = [lax.ppermute(x, AXES, ring_perm(n, d)) for d, x in zip(ends, sends)]
    come_from = [-d for d in far] + [last]
    piece = ((rows, depth), bf16)
    near_rows, *chunks = call(
        near_kernel,
        [tokens, behind, ahead, factor],
        received,
        [((len(near) * CHUNKS * rows + rank, depth), bf16)] + [piece] * (2 * CHUNKS),
    )

    up_way, down_way = chunks[:CHUNKS], chunks[CHUNKS:]
    near_swapped = swap_cores(near_rows, n)
    own = len(near) * rows
    (mine,) = product(functools.partial(core_kernel, rows), [near_rows], weight, [], own, [own])
    (up,) = call(cast_kernel, [up], [mine], [(up.shape, bf16)])
    arrived = []
    for _ in range(2, last - 1):
        up_way, down_way = ring_hop(up_way, down_way, n)
        arrived += up_way + down_way
    (mid_rows,) = join(arrived, [mine, up])

    total, rounded = call(
        functools.partial(partial_kernel, n, window, [near, mid], come_from),
        [near_rows, mid_rows, *received, factor, near_swapped],
        [],
        sums,
        [
            pltpu.SMEM(adapters.shape, jnp.int32),
            pltpu.VMEM((n * rows, window.size), bf16),
            pltpu.VMEM((2 * held, n * rows, rank), jnp.float32),
            pltpu.VMEM((n, rows, rank), jnp.float32),
            pltpu.SemaphoreType.DMA,
        ],
        outside=[adapters],
    )
    near_base, mine = product(
        functools.partial(near_base_kernel, rows, len(near), len(mid)),
        [near_swapped, mine, mid_rows],
        weight,
        [rounded],
        own + len(mid) * rows,
        [2 * own, len(mid) * rows],
    )
    total, rounded = call(add_kernel, [total, lax.ppermute(rounded, AXES, y_perm(n))], [], sums)
    up_way, down_way = ring_hop(up_way, down_way, n)
    late_rows, turned = join([mid_rows, *up_way, *down_way], [rounded, near_base], 1)

    late_swapped = swap_cores(late_rows, n)
    total, rounded = call(
        add_kernel,
        [total] + [lax.ppermute(rounded, AXES, z_perm(n, shift)) for shift in range(1, n // 2)],
        [],
        sums,
    )
    (last_rows,) = join([lax.ppermute(turned, AXES, ring_perm(n, 1, -1))], [rounded])
    last_pair = (last_rows, swap_cores(last_rows, n))

    late = len(mid) + len(far)
    mid_base, far_base = product(
        functools.partial(late_base_kernel, rows, len(mid), len(far)),
        [late_swapped, mine],
        weight,
        [last_rows],
        late * rows,
        [2 * len(mid) * rows, len(far) * rows],
    )
    return finish(
        n,
        rows,
        [near, mid, far, [last]],
        [adapters, rows_per_block],
        [near_base, mid_base, far_base],
        [late_rows, *last_pair],
        weight,
        [total, swap_cores(rounded, n)],
        up,
    )


def solution(mesh):
    placed = (
        P(("groups", "seq", "adapter"), None),
        P(None, ("seq", "adapter")),
        P(("groups", "adapter"), "seq", None),
        P("groups", None, ("seq", "adapter")),
        P("groups", None),
        P("groups"),
    )
    return jax.shard_map(
        functools.partial(on_device, mesh.shape["seq"]),
        mesh=mesh,
        in_specs=placed,
        out_specs=P("groups", ("seq", "adapter")),
        check_vma=False,
    )
```

```python
import functools

import jax
import jax.numpy as jnp
from jax import lax
from jax.experimental import pallas as pl
from jax.experimental.pallas import tpu as pltpu
from jax.sharding import PartitionSpec as P

BLOCK = 128
AXES = ("seq", "adapter")
CHUNKS = 2


def ring_perm(n, way, other_way=None):
    order = [2 * z for z in range(n // 2)] + [2 * z + 1 for z in reversed(range(n // 2))]
    ways = (way, way if other_way is None else other_way)
    return [(2 * s + c, 2 * order[(pos + ways[c]) % n] + c) for pos, s in enumerate(order) for c in range(2)]


def swap_cores(x, n):
    return lax.ppermute(x, AXES, [(2 * s + c, 2 * s + 1 - c) for s in range(n) for c in range(2)])


def chip_at(distance, n):
    s = lax.axis_index("seq")
    z = s >> 1
    pos = jnp.where(s & 1 == 0, z, n - 1 - z) + distance
    pos = jnp.where(pos >= n, pos - n, pos)
    pos = jnp.where(pos < 0, pos + n, pos)
    return jnp.where(pos < n // 2, 2 * pos, 2 * (n - 1 - pos) + 1)


def y_perm(n):
    return [(2 * s + c, 2 * (s ^ 1) + c) for s in range(n) for c in range(2)]


def z_perm(n, shift):
    nz = n // 2
    return [
        (2 * (2 * z + y) + c, 2 * (2 * ((z - shift) % nz) + y) + c)
        for z in range(nz)
        for y in range(2)
        for c in range(2)
    ]


def hop_distances(hop, n):
    if hop == 0:
        return [0]
    return [-hop, hop] if hop < n // 2 else [hop]


def ring_hop(up, down, n):
    return [lax.ppermute(x, AXES, ring_perm(n, 1)) for x in up], [lax.ppermute(x, AXES, ring_perm(n, -1)) for x in down]


def join_kernel(ways, *refs):
    count = len(refs) - 1 - ways
    pieces, out, on = refs[:count], refs[count], refs[count + 1 :]
    first = 0
    for piece in pieces:
        out[first : first + piece.shape[0], :] = piece[...]
        first += piece.shape[0]
    arrived = pieces[len(pieces) - 2 * CHUNKS :]
    if ways == 1:
        c = lax.axis_index("adapter")
        rows = arrived[0].shape[0]
        for core in range(2):

            @pl.when(c == core)
            def _():
                for i, piece in enumerate(arrived[core * CHUNKS : (core + 1) * CHUNKS]):
                    on[0][i * rows : (i + 1) * rows, :] = piece[...]


def join(pieces, after, ways=0):
    (rows, depth), dtype = pieces[-1].shape, pieces[-1].dtype
    on = [CHUNKS * rows] * ways
    outs = [((count, depth), dtype) for count in [sum(x.shape[0] for x in pieces), *on]]
    return call(functools.partial(join_kernel, ways), pieces, after, outs)


def whole(count):
    return [pl.BlockSpec(memory_space=pltpu.VMEM)] * count


def in_vmem(arrays):
    return [pltpu.with_memory_space_constraint(x, pltpu.VMEM) for x in arrays]


def call(kernel, arrays, after, outs, scratch=(), limit=8, flops=0, outside=()):
    operands = len(arrays) + len(outside)

    def body(*refs):
        kernel(*refs[:operands], *refs[operands + len(after) :])

    return pl.pallas_call(
        body,
        out_shape=[pltpu.VMEM(shape, dtype) for shape, dtype in outs],
        in_specs=whole(len(arrays)) + [pl.BlockSpec(memory_space=pl.ANY)] * (len(outside) + len(after)),
        out_specs=whole(len(outs)),
        scratch_shapes=list(scratch),
        compiler_params=pltpu.CompilerParams(vmem_limit_bytes=limit << 20),
        cost_estimate=pl.CostEstimate(flops=flops, bytes_accessed=0, transcendentals=0),
    )(*in_vmem(arrays), *outside, *after)


class Window:
    def __init__(self, n, width, depth):
        self.width, self.depth = width, depth
        self.size = -(-(width + max(s * width % 128 for s in range(n))) // 128) * 128
        for s in range(n):
            start = s * width // 128 * 128
            assert start // depth == (start + self.size - 1) // depth

    def start(self, chip):
        return (chip * self.width) >> 7 << 7

    def shift(self, chip):
        return chip * self.width - self.start(chip)


def near_kernel(tokens, behind, ahead, factor, out, *chunks):
    held, rank, size = factor.shape
    rows, depth = chunks[0].shape
    for i, ref in enumerate((tokens, behind, ahead)):
        for k in range(CHUNKS):
            piece = ref[:, k * depth : (k + 1) * depth]
            at = (i * CHUNKS + k) * rows
            out[at : at + rows, :] = piece
            if i:
                chunks[(i - 1) * CHUNKS + k][...] = piece
    first = 3 * CHUNKS * rows
    out[first:, :] = jnp.zeros((rank, depth), out.dtype)
    for index in range(held):
        out[first:, index * size : (index + 1) * size] = factor[index]


def pack(parts, out):
    chips, rows, rank = parts.shape
    for t in range(chips):
        i, k = t % (chips // 2), t // (chips // 2)
        out[i * rows : (i + 1) * rows, k * rank : (k + 1) * rank] = parts[t].astype(out.dtype)


def partial_kernel(n, window, groups, far, *refs):
    *pieces, factor, other, adapters_ref, total, rounded, adapters, x, products, parts, sem = refs
    lookup = pltpu.make_async_copy(adapters_ref, adapters, sem)
    lookup.start()
    pieces, received = pieces[: len(groups)], pieces[len(groups) :]
    s, c = lax.axis_index("seq"), lax.axis_index("adapter")
    rows, size = received[0].shape
    held, rank, _ = factor.shape
    start = window.start(s)
    chunk = jnp.where(start >= window.depth, 1, 0)
    inside = pl.multiple_of(start - chunk * window.depth, 128)
    order = []
    for piece, distances in zip(pieces, groups):
        for i, distance in enumerate(distances):
            row = pl.multiple_of((i * CHUNKS + chunk) * rows, rows)
            x[len(order) * rows : (len(order) + 1) * rows, :] = piece[pl.ds(row, rows), pl.ds(inside, size)]
            order.append(distance)
    for piece, distance in zip(received, far):
        x[len(order) * rows : (len(order) + 1) * rows, :] = piece[...]
        order.append(distance)
    below = other.shape[0] - rank
    for index in range(held):
        theirs = other[below:, index * size : (index + 1) * size]
        for core, weights in ((c, factor[index]), (1 - c, theirs)):
            products[core * held + index] = lax.dot_general(
                x[...], weights, (((1,), (1,)), ((), ())), preferred_element_type=jnp.float32
            )
    lookup.wait()
    for i, distance in enumerate(order):
        chip = chip_at(distance, n)
        parts[chip] = products[adapters[chip * 2 * rows // BLOCK], i * rows : (i + 1) * rows, :]
    pack(parts, total)
    rounded[...] = total[...].astype(jnp.bfloat16)


def add_kernel(total, *refs):
    *received, out, rounded = refs
    value = total[...]
    for x in received:
        value += x[...].astype(jnp.float32)
    out[...] = value
    rounded[...] = value.astype(jnp.bfloat16)


def prepare_kernel(n, window, distances, tokens, down_ref, factor, *refs):
    *sends, down, sems = refs
    copies = [pltpu.make_async_copy(down_ref, down, sems.at[0])]
    for k, (distance, send) in enumerate(zip(distances, sends)):
        start = pl.multiple_of(window.start(chip_at(distance, n)), 128)
        copies.append(pltpu.make_async_copy(tokens.at[:, pl.ds(start, window.size)], send, sems.at[1 + k]))
    for copy in copies:
        copy.start()
    copies[0].wait()
    zeros = jnp.zeros((down.shape[1], window.size - window.width), jnp.float32)
    for index in range(down.shape[0]):
        wide = jnp.concatenate([down[index], zeros], 1)
        factor[index] = pltpu.roll(wide, window.shift(lax.axis_index("seq")), 1).astype(jnp.bfloat16)
    for copy in copies[1:]:
        copy.wait()


def full_rows(rows):
    return max(rows, 128)


def assemble_core(ref, chips, rows, held):
    depth = ref.shape[1]
    for i in range(chips):
        for k in range(CHUNKS):
            at = (i * CHUNKS + k) * rows
            held[i * rows : (i + 1) * rows, k * depth : (k + 1) * depth] = ref[at : at + rows, :]


def core_kernel(rows, ref, *refs):
    *weights, base, held = refs
    assemble_core(ref, base.shape[0] // rows, rows, held)
    columns = tile_width(base.shape[1])
    for j in range(0, base.shape[1], columns):
        at = slice(j, j + columns)
        base[:, at] = multiply(held, weights, at)[: base.shape[0]]


def both_kernel(rows, ref, mine, *refs):
    *weights, base, held = refs
    chips = base.shape[0] // (2 * rows)
    c = lax.axis_index("adapter")
    assemble_core(ref, chips, rows, held)
    columns = tile_width(base.shape[1])
    for j in range(0, base.shape[1], columns):
        at = slice(j, j + columns)
        tile = multiply(held, weights, at)
        for i in range(chips):
            here = slice(i * rows, (i + 1) * rows)
            for core, value in ((c, mine[here, at]), (1 - c, tile[here])):
                base[pl.ds(pl.multiple_of((2 * i + core) * rows, rows), rows), at] = value


def core_rows(ref, chips, rows, weights, after, mine=None):
    total, depth, width = rows * chips, sum(w.shape[0] for w in weights), weights[0].shape[1]
    (base,) = call(
        functools.partial(core_kernel if mine is None else both_kernel, rows),
        [ref] + ([] if mine is None else [mine]) + weights,
        after,
        [((total if mine is None else 2 * total, width), jnp.float32)],
        [pltpu.VMEM((full_rows(total), depth), jnp.bfloat16)],
        limit=8 + (2 * total * depth >> 20),
        flops=2 * total * depth * width,
    )
    return base


def cast_kernel(source, out):
    out[...] = source[...].astype(out.dtype)


def in_hbm(arrays):
    return [pltpu.with_memory_space_constraint(x, pltpu.HBM) for x in arrays]


def prepare(kernel, arrays, later, outs, scratch):
    operands = len(arrays)

    def body(*refs):
        kernel(*refs[:operands], *refs[operands + len(later) :])

    return pl.pallas_call(
        body,
        out_shape=[pltpu.VMEM(shape, dtype) for shape, dtype in outs],
        in_specs=[pl.BlockSpec(memory_space=pltpu.HBM)] * (operands + len(later)),
        out_specs=whole(len(outs)),
        scratch_shapes=scratch,
        compiler_params=pltpu.CompilerParams(vmem_limit_bytes=8 << 20),
        cost_estimate=pl.CostEstimate(flops=0, bytes_accessed=0, transcendentals=0),
    )(*in_hbm(arrays), *in_hbm(later))


def assemble(pairs, counts, rows, held):
    c = lax.axis_index("adapter")
    first = 0
    for pair, chips in zip(pairs, counts):
        depth = pair[0].shape[1]
        for chip in range(chips):
            for k in range(CHUNKS):
                at = (chip * CHUNKS + k) * rows
                for ref, core in zip(pair, (c, 1 - c)):
                    row = pl.multiple_of(first + core * rows, rows)
                    held[pl.ds(row, rows), k * depth : (k + 1) * depth] = ref[at : at + rows, :]
            first += 2 * rows


def tile_width(width):
    return 768 if width % 768 == 0 else width


def multiply(held, weights, at):
    total, first = 0.0, 0
    for w in weights:
        columns = held[:, first : first + w.shape[0]]
        total += jnp.dot(columns, w[:, at], preferred_element_type=jnp.float32)
        first += w.shape[0]
    return total


def finish_kernel(n, rows, groups, skipped, *refs):
    count = len(groups) - 1
    bases, refs = refs[:count], refs[count:]
    mine, others, weight, own, other, up_ref, adapters_ref, live_ref = refs[:8]
    out_ref, held, shrink, block, adapters, live, sems, small_sems = refs[8 + skipped :]
    lookups = [
        pltpu.make_async_copy(source, to, small_sems.at[k])
        for k, (source, to) in enumerate(((adapters_ref, adapters), (live_ref, live)))
    ]
    for lookup in lookups:
        lookup.start()
    c = lax.axis_index("adapter")
    chip_rows, rank = 2 * rows, up_ref.shape[1]
    tiles, _, columns = block.shape
    assemble([(mine, others)], [1], rows, held)
    for t in range(n):
        i, k = t % (n // 2), t // (n // 2)
        for ref, core in ((own, c), (other, 1 - c)):
            part = ref[i * rows : (i + 1) * rows, k * rank : (k + 1) * rank]
            shrink[t, pl.ds(pl.multiple_of(core * rows, rows), rows), :] = part.astype(jnp.bfloat16)
    early = [
        (base, i * chip_rows) for base, group in zip(bases, groups) for i in range(len(group))
    ]
    sources = [distance for group in groups for distance in group]
    for lookup in lookups:
        lookup.wait()
    copies = []

    def put(j, i, value):
        at = slice(j * columns, (j + 1) * columns)
        chip = chip_at(sources[i], n)
        first = chip * chip_rows
        of_block = first // BLOCK
        delta = jnp.dot(shrink[chip], up_ref[adapters[of_block], :, at], preferred_element_type=jnp.float32)
        index = lax.broadcasted_iota(jnp.int32, delta.shape, 0) + (first - of_block * BLOCK)
        value = jnp.where(index < live[of_block], value + delta, 0.0)
        block[j, i * chip_rows : (i + 1) * chip_rows, :] = value.astype(out_ref.dtype)

    def send(j, i):
        first = pl.multiple_of(chip_at(sources[i], n) * chip_rows, chip_rows)
        copies.append(
            pltpu.make_async_copy(
                block.at[j, pl.ds(i * chip_rows, chip_rows), :],
                out_ref.at[pl.ds(first, chip_rows), pl.ds(j * columns, columns)],
                sems.at[j, i],
            )
        )
        copies[-1].start()

    for j in range(tiles):
        at = slice(j * columns, (j + 1) * columns)
        tile = multiply(held, [weight], at)
        for i, (base, row) in enumerate(early):
            put(j, i, base[row : row + chip_rows, at])
        put(j, n - 1, tile[:chip_rows])
        for i in range(n):
            send(j, i)
    for copy in copies:
        copy.wait()


def finish(n, rows, groups, lookups, bases, last_pair, weight, sums, up, after):
    (rank, width), depth = up.shape[1:], weight.shape[0]
    total, columns = 2 * n * rows, tile_width(width)
    arrays = [*bases, *last_pair, weight, *sums, up]
    held = full_rows(2 * rows)
    return pl.pallas_call(
        functools.partial(finish_kernel, n, rows, groups, len(after)),
        out_shape=jax.ShapeDtypeStruct((total, width), jnp.bfloat16),
        in_specs=whole(len(arrays)) + [pl.BlockSpec(memory_space=pl.ANY)] * (len(lookups) + len(after)),
        out_specs=pl.BlockSpec(memory_space=pl.ANY),
        scratch_shapes=[
            pltpu.VMEM((held, depth), jnp.bfloat16),
            pltpu.VMEM((n, 2 * rows, rank), jnp.bfloat16),
            pltpu.VMEM((width // columns, total, columns), jnp.bfloat16),
            *(pltpu.SMEM(x.shape, x.dtype) for x in lookups),
            pltpu.SemaphoreType.DMA((width // columns, n)),
            pltpu.SemaphoreType.DMA((len(lookups),)),
        ],
        compiler_params=pltpu.CompilerParams(vmem_limit_bytes=10 << 20),
        cost_estimate=pl.CostEstimate(
            flops=2 * held * depth * width, bytes_accessed=2 * total * width, transcendentals=0
        ),
    )(*in_vmem(arrays), *lookups, *after)


def on_device(n, tokens, weight, down, up, adapter_per_block, rows_per_block):
    rows, features = tokens.shape
    depth = features // CHUNKS
    held, width, rank = down.shape
    last = n // 2
    adapters = adapter_per_block[:, 0]
    window = Window(n, width, depth)
    near, mid, far = ([d for hop in hops for d in hop_distances(hop, n)] for hops in ((0, 1), range(2, last - 1), [last - 1]))
    half = (n // 2 * rows, 2 * rank)
    sums = [(half, jnp.float32), (half, jnp.bfloat16)]

    (behind,), (ahead,) = ring_hop([tokens], [tokens], n)
    ends = far + [last]
    bf16 = jnp.bfloat16
    factor, *sends = prepare(
        functools.partial(prepare_kernel, n, window, ends),
        [tokens, jnp.swapaxes(down, 1, 2)],
        [weight, up],
        [((held, rank, window.size), bf16)] + [((rows, window.size), bf16)] * len(ends),
        [
            pltpu.VMEM((held, rank, width), down.dtype),
            pltpu.SemaphoreType.DMA((1 + len(ends),)),
        ],
    )
    received = [lax.ppermute(x, AXES, ring_perm(n, d)) for d, x in zip(ends, sends)]
    come_from = [-d for d in far] + [last]
    piece = ((rows, depth), bf16)
    near_rows, *chunks = call(
        near_kernel,
        [tokens, behind, ahead, factor],
        received,
        [((len(near) * CHUNKS * rows + rank, depth), bf16)] + [piece] * (2 * CHUNKS),
    )

    up_way, down_way = chunks[:CHUNKS], chunks[CHUNKS:]
    weights = [weight]
    near_swapped = swap_cores(near_rows, n)
    mine = core_rows(near_rows, len(near), rows, weights, [])
    (up,) = call(cast_kernel, [up], [mine], [(up.shape, bf16)])
    arrived = []
    for _ in range(2, last - 1):
        up_way, down_way = ring_hop(up_way, down_way, n)
        arrived += up_way + down_way
    (mid_rows,) = join(arrived, [mine, up])

    total, rounded = call(
        functools.partial(partial_kernel, n, window, [near, mid], come_from),
        [near_rows, mid_rows, *received, factor, near_swapped],
        [],
        sums,
        [
            pltpu.SMEM(adapters.shape, jnp.int32),
            pltpu.VMEM((n * rows, window.size), bf16),
            pltpu.VMEM((2 * held, n * rows, rank), jnp.float32),
            pltpu.VMEM((n, rows, rank), jnp.float32),
            pltpu.SemaphoreType.DMA,
        ],
        outside=[adapters],
    )
    bases = [core_rows(near_swapped, len(near), rows, weights, [rounded], mine)]
    total, rounded = call(add_kernel, [total, lax.ppermute(rounded, AXES, y_perm(n))], [], sums)
    up_way, down_way = ring_hop(up_way, down_way, n)
    late_rows, turned = join([mid_rows, *up_way, *down_way], [rounded, *bases], 1)

    late = mid + far
    late_swapped = swap_cores(late_rows, n)
    mine = core_rows(late_rows, len(late), rows, weights, [])
    total, rounded = call(
        add_kernel,
        [total] + [lax.ppermute(rounded, AXES, z_perm(n, shift)) for shift in range(1, n // 2)],
        [],
        sums,
    )
    (last_rows,) = join([lax.ppermute(turned, AXES, ring_perm(n, 1, -1))], [rounded, mine])

    bases.append(core_rows(late_swapped, len(late), rows, weights, [last_rows], mine))
    last_pair = (last_rows, swap_cores(last_rows, n))
    return finish(
        n,
        rows,
        [near, late, [last]],
        [adapters, rows_per_block],
        bases,
        last_pair,
        weight,
        [total, swap_cores(rounded, n)],
        up,
        [],
    )


def solution(mesh):
    placed = (
        P(("groups", "seq", "adapter"), None),
        P(None, ("seq", "adapter")),
        P(("groups", "adapter"), "seq", None),
        P("groups", None, ("seq", "adapter")),
        P("groups", None),
        P("groups"),
    )
    return jax.shard_map(
        functools.partial(on_device, mesh.shape["seq"]),
        mesh=mesh,
        in_specs=placed,
        out_specs=P("groups", ("seq", "adapter")),
        check_vma=False,
    )
```

```python
import functools

import jax
import jax.numpy as jnp
from jax import lax
from jax.experimental import pallas as pl
from jax.experimental.pallas import tpu as pltpu
from jax.sharding import PartitionSpec as P

BLOCK = 128
AXES = ("seq", "adapter")
CHUNKS = 2


def ring_perm(n, way, other_way=None):
    order = [2 * z for z in range(n // 2)] + [2 * z + 1 for z in reversed(range(n // 2))]
    ways = (way, way if other_way is None else other_way)
    return [(2 * s + c, 2 * order[(pos + ways[c]) % n] + c) for pos, s in enumerate(order) for c in range(2)]


def swap_cores(x, n):
    return lax.ppermute(x, AXES, [(2 * s + c, 2 * s + 1 - c) for s in range(n) for c in range(2)])


def chip_at(distance, n):
    s = lax.axis_index("seq")
    z = s >> 1
    pos = jnp.where(s & 1 == 0, z, n - 1 - z) + distance
    pos = jnp.where(pos >= n, pos - n, pos)
    pos = jnp.where(pos < 0, pos + n, pos)
    return jnp.where(pos < n // 2, 2 * pos, 2 * (n - 1 - pos) + 1)


def y_perm(n):
    return [(2 * s + c, 2 * (s ^ 1) + c) for s in range(n) for c in range(2)]


def z_perm(n, shift):
    nz = n // 2
    return [
        (2 * (2 * z + y) + c, 2 * (2 * ((z - shift) % nz) + y) + c)
        for z in range(nz)
        for y in range(2)
        for c in range(2)
    ]


def hop_distances(hop, n):
    if hop == 0:
        return [0]
    return [-hop, hop] if hop < n // 2 else [hop]


def ring_hop(up, down, n):
    return [lax.ppermute(x, AXES, ring_perm(n, 1)) for x in up], [lax.ppermute(x, AXES, ring_perm(n, -1)) for x in down]


def join_kernel(ways, *refs):
    count = len(refs) - 1 - ways
    pieces, out, on = refs[:count], refs[count], refs[count + 1 :]
    first = 0
    for piece in pieces:
        out[first : first + piece.shape[0], :] = piece[...]
        first += piece.shape[0]
    arrived = pieces[len(pieces) - 2 * CHUNKS :]
    if ways == 1:
        c = lax.axis_index("adapter")
        rows = arrived[0].shape[0]
        for core in range(2):

            @pl.when(c == core)
            def _():
                for i, piece in enumerate(arrived[core * CHUNKS : (core + 1) * CHUNKS]):
                    on[0][i * rows : (i + 1) * rows, :] = piece[...]


def join(pieces, after, ways=0):
    (rows, depth), dtype = pieces[-1].shape, pieces[-1].dtype
    on = [CHUNKS * rows] * ways
    outs = [((count, depth), dtype) for count in [sum(x.shape[0] for x in pieces), *on]]
    return call(functools.partial(join_kernel, ways), pieces, after, outs)


def whole(count):
    return [pl.BlockSpec(memory_space=pltpu.VMEM)] * count


def in_vmem(arrays):
    return [pltpu.with_memory_space_constraint(x, pltpu.VMEM) for x in arrays]


def call(kernel, arrays, after, outs, scratch=(), limit=8, flops=0, outside=()):
    operands = len(arrays) + len(outside)

    def body(*refs):
        kernel(*refs[:operands], *refs[operands + len(after) :])

    return pl.pallas_call(
        body,
        out_shape=[pltpu.VMEM(shape, dtype) for shape, dtype in outs],
        in_specs=whole(len(arrays)) + [pl.BlockSpec(memory_space=pl.ANY)] * (len(outside) + len(after)),
        out_specs=whole(len(outs)),
        scratch_shapes=list(scratch),
        compiler_params=pltpu.CompilerParams(vmem_limit_bytes=limit << 20),
        cost_estimate=pl.CostEstimate(flops=flops, bytes_accessed=0, transcendentals=0),
    )(*in_vmem(arrays), *outside, *after)


class Window:
    def __init__(self, n, width, depth):
        self.width, self.depth = width, depth
        self.size = -(-(width + max(s * width % 128 for s in range(n))) // 128) * 128
        for s in range(n):
            start = s * width // 128 * 128
            assert start // depth == (start + self.size - 1) // depth

    def start(self, chip):
        return (chip * self.width) >> 7 << 7

    def shift(self, chip):
        return chip * self.width - self.start(chip)


def near_kernel(tokens, behind, ahead, factor, out, *chunks):
    held, rank, size = factor.shape
    rows, depth = chunks[0].shape
    for i, ref in enumerate((tokens, behind, ahead)):
        for k in range(CHUNKS):
            piece = ref[:, k * depth : (k + 1) * depth]
            at = (i * CHUNKS + k) * rows
            out[at : at + rows, :] = piece
            if i:
                chunks[(i - 1) * CHUNKS + k][...] = piece
    first = 3 * CHUNKS * rows
    out[first:, :] = jnp.zeros((rank, depth), out.dtype)
    for index in range(held):
        out[first:, index * size : (index + 1) * size] = factor[index]


def pack(parts, out):
    chips, rows, rank = parts.shape
    for t in range(chips):
        i, k = t % (chips // 2), t // (chips // 2)
        out[i * rows : (i + 1) * rows, k * rank : (k + 1) * rank] = parts[t].astype(out.dtype)


def partial_kernel(n, window, groups, far, *refs):
    *pieces, factor, other, adapters_ref, total, rounded, adapters, x, stacked, products, parts, sem = refs
    lookup = pltpu.make_async_copy(adapters_ref, adapters, sem)
    lookup.start()
    pieces, received = pieces[: len(groups)], pieces[len(groups) :]
    s, c = lax.axis_index("seq"), lax.axis_index("adapter")
    rows, size = received[0].shape
    held, rank, _ = factor.shape
    start = window.start(s)
    chunk = jnp.where(start >= window.depth, 1, 0)
    inside = pl.multiple_of(start - chunk * window.depth, 128)
    order = []
    for piece, distances in zip(pieces, groups):
        for i, distance in enumerate(distances):
            row = pl.multiple_of((i * CHUNKS + chunk) * rows, rows)
            x[len(order) * rows : (len(order) + 1) * rows, :] = piece[pl.ds(row, rows), pl.ds(inside, size)]
            order.append(distance)
    for piece, distance in zip(received, far):
        x[len(order) * rows : (len(order) + 1) * rows, :] = piece[...]
        order.append(distance)
    below = other.shape[0] - rank
    for index in range(held):
        theirs = other[below:, index * size : (index + 1) * size]
        for core, weights in ((c, factor[index]), (1 - c, theirs)):
            at = pl.multiple_of((core * held + index) * rank, rank)
            stacked[pl.ds(at, rank), :] = weights
    products[...] = lax.dot_general(
        x[...], stacked[...], (((1,), (1,)), ((), ())), preferred_element_type=jnp.float32
    )
    lookup.wait()
    for i, distance in enumerate(order):
        chip = chip_at(distance, n)
        adapter = adapters[chip * 2 * rows // BLOCK]
        value = products[i * rows : (i + 1) * rows, :rank]
        for k in range(1, 2 * held):
            value = jnp.where(adapter == k, products[i * rows : (i + 1) * rows, k * rank : (k + 1) * rank], value)
        parts[chip] = value
    pack(parts, total)
    rounded[...] = total[...].astype(jnp.bfloat16)


def add_kernel(total, *refs):
    *received, out, rounded = refs
    value = total[...]
    for x in received:
        value += x[...].astype(jnp.float32)
    out[...] = value
    rounded[...] = value.astype(jnp.bfloat16)


def prepare_kernel(n, window, distances, tokens, down_ref, factor, *refs):
    *sends, down, sems = refs
    copies = [pltpu.make_async_copy(down_ref, down, sems.at[0])]
    for k, (distance, send) in enumerate(zip(distances, sends)):
        start = pl.multiple_of(window.start(chip_at(distance, n)), 128)
        copies.append(pltpu.make_async_copy(tokens.at[:, pl.ds(start, window.size)], send, sems.at[1 + k]))
    for copy in copies:
        copy.start()
    copies[0].wait()
    zeros = jnp.zeros((down.shape[1], window.size - window.width), jnp.float32)
    for index in range(down.shape[0]):
        wide = jnp.concatenate([down[index], zeros], 1)
        factor[index] = pltpu.roll(wide, window.shift(lax.axis_index("seq")), 1).astype(jnp.bfloat16)
    for copy in copies[1:]:
        copy.wait()


def full_rows(rows):
    return max(rows, 128)


def assemble_core(ref, chips, rows, held):
    depth = ref.shape[1]
    for i in range(chips):
        for k in range(CHUNKS):
            at = (i * CHUNKS + k) * rows
            held[i * rows : (i + 1) * rows, k * depth : (k + 1) * depth] = ref[at : at + rows, :]


def core_kernel(rows, ref, *refs):
    *weights, base, held = refs
    assemble_core(ref, base.shape[0] // rows, rows, held)
    columns = tile_width(base.shape[1])
    for j in range(0, base.shape[1], columns):
        at = slice(j, j + columns)
        base[:, at] = multiply(held, weights, at)[: base.shape[0]]


def both_kernel(rows, ref, mine, *refs):
    *weights, base, held = refs
    chips = base.shape[0] // (2 * rows)
    c = lax.axis_index("adapter")
    assemble_core(ref, chips, rows, held)
    columns = tile_width(base.shape[1])
    for j in range(0, base.shape[1], columns):
        at = slice(j, j + columns)
        tile = multiply(held, weights, at)
        for i in range(chips):
            here = slice(i * rows, (i + 1) * rows)
            for core, value in ((c, mine[here, at]), (1 - c, tile[here])):
                base[pl.ds(pl.multiple_of((2 * i + core) * rows, rows), rows), at] = value


def core_rows(ref, chips, rows, weights, after, mine=None):
    total, depth, width = rows * chips, sum(w.shape[0] for w in weights), weights[0].shape[1]
    (base,) = call(
        functools.partial(core_kernel if mine is None else both_kernel, rows),
        [ref] + ([] if mine is None else [mine]) + weights,
        after,
        [((total if mine is None else 2 * total, width), jnp.float32)],
        [pltpu.VMEM((full_rows(total), depth), jnp.bfloat16)],
        limit=8 + (2 * total * depth >> 20),
        flops=2 * total * depth * width,
    )
    return base


def cast_kernel(source, out):
    rank = source.shape[1]
    for adapter in range(source.shape[0]):
        out[adapter * rank : (adapter + 1) * rank, :] = source[adapter].astype(out.dtype)


def in_hbm(arrays):
    return [pltpu.with_memory_space_constraint(x, pltpu.HBM) for x in arrays]


def prepare(kernel, arrays, later, outs, scratch):
    operands = len(arrays)

    def body(*refs):
        kernel(*refs[:operands], *refs[operands + len(later) :])

    return pl.pallas_call(
        body,
        out_shape=[pltpu.VMEM(shape, dtype) for shape, dtype in outs],
        in_specs=[pl.BlockSpec(memory_space=pltpu.HBM)] * (operands + len(later)),
        out_specs=whole(len(outs)),
        scratch_shapes=scratch,
        compiler_params=pltpu.CompilerParams(vmem_limit_bytes=8 << 20),
        cost_estimate=pl.CostEstimate(flops=0, bytes_accessed=0, transcendentals=0),
    )(*in_hbm(arrays), *in_hbm(later))


def assemble(pairs, counts, rows, held):
    c = lax.axis_index("adapter")
    first = 0
    for pair, chips in zip(pairs, counts):
        depth = pair[0].shape[1]
        for chip in range(chips):
            for k in range(CHUNKS):
                at = (chip * CHUNKS + k) * rows
                for ref, core in zip(pair, (c, 1 - c)):
                    row = pl.multiple_of(first + core * rows, rows)
                    held[pl.ds(row, rows), k * depth : (k + 1) * depth] = ref[at : at + rows, :]
            first += 2 * rows


def tile_width(width):
    return 768 if width % 768 == 0 else width


def multiply(held, weights, at):
    total, first = 0.0, 0
    for w in weights:
        columns = held[:, first : first + w.shape[0]]
        total += jnp.dot(columns, w[:, at], preferred_element_type=jnp.float32)
        first += w.shape[0]
    return total


def finish_kernel(n, rows, groups, skipped, *refs):
    count = len(groups) - 1
    bases, refs = refs[:count], refs[count:]
    mine, others, weight, own, other, up_ref, adapters_ref, live_ref = refs[:8]
    out_ref, held, shrink, spread, block, adapters, live, sems, small_sems = refs[8 + skipped :]
    lookups = [
        pltpu.make_async_copy(source, to, small_sems.at[k])
        for k, (source, to) in enumerate(((adapters_ref, adapters), (live_ref, live)))
    ]
    for lookup in lookups:
        lookup.start()
    c = lax.axis_index("adapter")
    chip_rows, rank = 2 * rows, own.shape[1] // 2
    tiles, _, columns = block.shape
    assemble([(mine, others)], [1], rows, held)
    for t in range(n):
        i, k = t % (n // 2), t // (n // 2)
        for ref, core in ((own, c), (other, 1 - c)):
            part = ref[i * rows : (i + 1) * rows, k * rank : (k + 1) * rank]
            shrink[t, pl.ds(pl.multiple_of(core * rows, rows), rows), :] = part.astype(jnp.bfloat16)
    places = [
        (distance, base, i * chip_rows)
        for base, distances in zip([*bases, None], groups)
        for i, distance in enumerate(distances)
    ]
    for lookup in lookups:
        lookup.wait()
    for i, (distance, _, _) in enumerate(places):
        chip = chip_at(distance, n)
        adapter = adapters[chip * chip_rows // BLOCK]
        value = shrink[chip]
        for k in range(up_ref.shape[0] // rank):
            spread[i * chip_rows : (i + 1) * chip_rows, k * rank : (k + 1) * rank] = jnp.where(
                adapter == k, value, jnp.zeros_like(value)
            )
    copies = []
    for j in range(tiles):
        at = slice(j * columns, (j + 1) * columns)
        last = multiply(held, [weight], at)
        for pair in range(0, n, 2):
            both = slice(pair * chip_rows, (pair + 2) * chip_rows)
            deltas = jnp.dot(spread[both, :], up_ref[:, at], preferred_element_type=jnp.float32)
            for i in (pair, pair + 1):
                distance, base, row = places[i]
                first = chip_at(distance, n) * chip_rows
                of_block = first // BLOCK
                delta = deltas[(i - pair) * chip_rows : (i - pair + 1) * chip_rows]
                index = lax.broadcasted_iota(jnp.int32, delta.shape, 0) + (first - of_block * BLOCK)
                value = last[:chip_rows] if base is None else base[row : row + chip_rows, at]
                place = pl.ds(i * chip_rows, chip_rows)
                block[j, place, :] = jnp.where(index < live[of_block], value + delta, 0.0).astype(out_ref.dtype)
                copies.append(
                    pltpu.make_async_copy(
                        block.at[j, place, :],
                        out_ref.at[pl.ds(pl.multiple_of(first, chip_rows), chip_rows), pl.ds(j * columns, columns)],
                        sems.at[j, i],
                    )
                )
                copies[-1].start()
    for copy in copies:
        copy.wait()


def finish(n, rows, groups, lookups, bases, last_pair, weight, sums, up, after):
    (deep, width), depth, rank = up.shape, weight.shape[0], sums[0].shape[1] // 2
    total, columns = 2 * n * rows, tile_width(width)
    arrays = [*bases, *last_pair, weight, *sums, up]
    held = full_rows(2 * rows)
    return pl.pallas_call(
        functools.partial(finish_kernel, n, rows, groups, len(after)),
        out_shape=jax.ShapeDtypeStruct((total, width), jnp.bfloat16),
        in_specs=whole(len(arrays)) + [pl.BlockSpec(memory_space=pl.ANY)] * (len(lookups) + len(after)),
        out_specs=pl.BlockSpec(memory_space=pl.ANY),
        scratch_shapes=[
            pltpu.VMEM((held, depth), jnp.bfloat16),
            pltpu.VMEM((n, 2 * rows, rank), jnp.bfloat16),
            pltpu.VMEM((total, deep), jnp.bfloat16),
            pltpu.VMEM((width // columns, total, columns), jnp.bfloat16),
            *(pltpu.SMEM(x.shape, x.dtype) for x in lookups),
            pltpu.SemaphoreType.DMA((width // columns, n)),
            pltpu.SemaphoreType.DMA((len(lookups),)),
        ],
        compiler_params=pltpu.CompilerParams(vmem_limit_bytes=10 << 20),
        cost_estimate=pl.CostEstimate(
            flops=2 * held * depth * width, bytes_accessed=2 * total * width, transcendentals=0
        ),
    )(*in_vmem(arrays), *lookups, *after)


def on_device(n, tokens, weight, down, up, adapter_per_block, rows_per_block):
    rows, features = tokens.shape
    depth = features // CHUNKS
    held, width, rank = down.shape
    last = n // 2
    adapters = adapter_per_block[:, 0]
    window = Window(n, width, depth)
    near, mid, far = ([d for hop in hops for d in hop_distances(hop, n)] for hops in ((0, 1), range(2, last - 1), [last - 1]))
    half = (n // 2 * rows, 2 * rank)
    sums = [(half, jnp.float32), (half, jnp.bfloat16)]

    (behind,), (ahead,) = ring_hop([tokens], [tokens], n)
    ends = far + [last]
    bf16 = jnp.bfloat16
    factor, *sends = prepare(
        functools.partial(prepare_kernel, n, window, ends),
        [tokens, jnp.swapaxes(down, 1, 2)],
        [weight, up],
        [((held, rank, window.size), bf16)] + [((rows, window.size), bf16)] * len(ends),
        [
            pltpu.VMEM((held, rank, width), down.dtype),
            pltpu.SemaphoreType.DMA((1 + len(ends),)),
        ],
    )
    received = [lax.ppermute(x, AXES, ring_perm(n, d)) for d, x in zip(ends, sends)]
    come_from = [-d for d in far] + [last]
    piece = ((rows, depth), bf16)
    near_rows, *chunks = call(
        near_kernel,
        [tokens, behind, ahead, factor],
        received,
        [((len(near) * CHUNKS * rows + rank, depth), bf16)] + [piece] * (2 * CHUNKS),
    )

    up_way, down_way = chunks[:CHUNKS], chunks[CHUNKS:]
    weights = [weight]
    near_swapped = swap_cores(near_rows, n)
    mine = core_rows(near_rows, len(near), rows, weights, [])
    (up,) = call(cast_kernel, [up], [mine], [((up.shape[0] * rank, up.shape[2]), bf16)])
    arrived = []
    for _ in range(2, last - 1):
        up_way, down_way = ring_hop(up_way, down_way, n)
        arrived += up_way + down_way
    (mid_rows,) = join(arrived, [mine, up])

    total, rounded = call(
        functools.partial(partial_kernel, n, window, [near, mid], come_from),
        [near_rows, mid_rows, *received, factor, near_swapped],
        [],
        sums,
        [
            pltpu.SMEM(adapters.shape, jnp.int32),
            pltpu.VMEM((n * rows, window.size), bf16),
            pltpu.VMEM((2 * held * rank, window.size), bf16),
            pltpu.VMEM((n * rows, 2 * held * rank), jnp.float32),
            pltpu.VMEM((n, rows, rank), jnp.float32),
            pltpu.SemaphoreType.DMA,
        ],
        outside=[adapters],
    )
    bases = [core_rows(near_swapped, len(near), rows, weights, [rounded], mine)]
    total, rounded = call(add_kernel, [total, lax.ppermute(rounded, AXES, y_perm(n))], [], sums)
    up_way, down_way = ring_hop(up_way, down_way, n)
    late_rows, turned = join([mid_rows, *up_way, *down_way], [rounded, *bases], 1)

    late = mid + far
    late_swapped = swap_cores(late_rows, n)
    mine = core_rows(late_rows, len(late), rows, weights, [])
    total, rounded = call(
        add_kernel,
        [total] + [lax.ppermute(rounded, AXES, z_perm(n, shift)) for shift in range(1, n // 2)],
        [],
        sums,
    )
    (last_rows,) = join([lax.ppermute(turned, AXES, ring_perm(n, 1, -1))], [rounded, mine])

    bases.append(core_rows(late_swapped, len(late), rows, weights, [last_rows], mine))
    last_pair = (last_rows, swap_cores(last_rows, n))
    return finish(
        n,
        rows,
        [near, late, [last]],
        [adapters, rows_per_block],
        bases,
        last_pair,
        weight,
        [total, swap_cores(rounded, n)],
        up,
        [],
    )


def solution(mesh):
    placed = (
        P(("groups", "seq", "adapter"), None),
        P(None, ("seq", "adapter")),
        P(("groups", "adapter"), "seq", None),
        P("groups", None, ("seq", "adapter")),
        P("groups", None),
        P("groups"),
    )
    return jax.shard_map(
        functools.partial(on_device, mesh.shape["seq"]),
        mesh=mesh,
        in_specs=placed,
        out_specs=P("groups", ("seq", "adapter")),
        check_vma=False,
    )
```

```python
import functools

import jax
import jax.numpy as jnp
from jax import lax
from jax.experimental import pallas as pl
from jax.experimental.pallas import tpu as pltpu
from jax.sharding import PartitionSpec as P

BLOCK = 128
AXES = ("seq", "adapter")
CHUNKS = 2


def ring_perm(n, way, other_way=None):
    order = [2 * z for z in range(n // 2)] + [2 * z + 1 for z in reversed(range(n // 2))]
    ways = (way, way if other_way is None else other_way)
    return [(2 * s + c, 2 * order[(pos + ways[c]) % n] + c) for pos, s in enumerate(order) for c in range(2)]


def swap_cores(x, n):
    return lax.ppermute(x, AXES, [(2 * s + c, 2 * s + 1 - c) for s in range(n) for c in range(2)])


def chip_at(distance, n):
    s = lax.axis_index("seq")
    z = s >> 1
    pos = jnp.where(s & 1 == 0, z, n - 1 - z) + distance
    pos = jnp.where(pos >= n, pos - n, pos)
    pos = jnp.where(pos < 0, pos + n, pos)
    return jnp.where(pos < n // 2, 2 * pos, 2 * (n - 1 - pos) + 1)


def y_perm(n):
    return [(2 * s + c, 2 * (s ^ 1) + c) for s in range(n) for c in range(2)]


def z_perm(n, shift):
    nz = n // 2
    return [
        (2 * (2 * z + y) + c, 2 * (2 * ((z - shift) % nz) + y) + c)
        for z in range(nz)
        for y in range(2)
        for c in range(2)
    ]


def hop_distances(hop, n):
    if hop == 0:
        return [0]
    return [-hop, hop] if hop < n // 2 else [hop]


def ring_hop(up, down, n):
    return [lax.ppermute(x, AXES, ring_perm(n, 1)) for x in up], [lax.ppermute(x, AXES, ring_perm(n, -1)) for x in down]


def join_kernel(ways, *refs):
    count = len(refs) - 1 - ways
    pieces, out, on = refs[:count], refs[count], refs[count + 1 :]
    first = 0
    for piece in pieces:
        out[first : first + piece.shape[0], :] = piece[...]
        first += piece.shape[0]
    arrived = pieces[len(pieces) - 2 * CHUNKS :]
    if ways == 1:
        c = lax.axis_index("adapter")
        rows = arrived[0].shape[0]
        for core in range(2):

            @pl.when(c == core)
            def _():
                for i, piece in enumerate(arrived[core * CHUNKS : (core + 1) * CHUNKS]):
                    on[0][i * rows : (i + 1) * rows, :] = piece[...]


def join(pieces, after, ways=0):
    (rows, depth), dtype = pieces[-1].shape, pieces[-1].dtype
    on = [CHUNKS * rows] * ways
    outs = [((count, depth), dtype) for count in [sum(x.shape[0] for x in pieces), *on]]
    return call(functools.partial(join_kernel, ways), pieces, after, outs)


def whole(count):
    return [pl.BlockSpec(memory_space=pltpu.VMEM)] * count


def in_vmem(arrays):
    return [pltpu.with_memory_space_constraint(x, pltpu.VMEM) for x in arrays]


def call(kernel, arrays, after, outs, scratch=(), limit=8, flops=0, outside=()):
    operands = len(arrays) + len(outside)

    def body(*refs):
        kernel(*refs[:operands], *refs[operands + len(after) :])

    return pl.pallas_call(
        body,
        out_shape=[pltpu.VMEM(shape, dtype) for shape, dtype in outs],
        in_specs=whole(len(arrays)) + [pl.BlockSpec(memory_space=pl.ANY)] * (len(outside) + len(after)),
        out_specs=whole(len(outs)),
        scratch_shapes=list(scratch),
        compiler_params=pltpu.CompilerParams(vmem_limit_bytes=limit << 20),
        cost_estimate=pl.CostEstimate(flops=flops, bytes_accessed=0, transcendentals=0),
    )(*in_vmem(arrays), *outside, *after)


class Window:
    def __init__(self, n, width, depth):
        self.width, self.depth = width, depth
        self.size = -(-(width + max(s * width % 128 for s in range(n))) // 128) * 128
        for s in range(n):
            start = s * width // 128 * 128
            assert start // depth == (start + self.size - 1) // depth

    def start(self, chip):
        return (chip * self.width) >> 7 << 7

    def shift(self, chip):
        return chip * self.width - self.start(chip)


def near_kernel(tokens, behind, ahead, factor, out, *chunks):
    held, rank, size = factor.shape
    rows, depth = chunks[0].shape
    for i, ref in enumerate((tokens, behind, ahead)):
        for k in range(CHUNKS):
            piece = ref[:, k * depth : (k + 1) * depth]
            at = (i * CHUNKS + k) * rows
            out[at : at + rows, :] = piece
            if i:
                chunks[(i - 1) * CHUNKS + k][...] = piece
    first = 3 * CHUNKS * rows
    out[first:, :] = jnp.zeros((rank, depth), out.dtype)
    for index in range(held):
        out[first:, index * size : (index + 1) * size] = factor[index]


def pack(parts, out):
    chips, rows, rank = parts.shape
    for t in range(chips):
        i, k = t % (chips // 2), t // (chips // 2)
        out[i * rows : (i + 1) * rows, k * rank : (k + 1) * rank] = parts[t].astype(out.dtype)


def partial_kernel(n, window, groups, far, *refs):
    *pieces, factor, other, adapters_ref, total, rounded, adapters, x, products, parts, sem = refs
    lookup = pltpu.make_async_copy(adapters_ref, adapters, sem)
    lookup.start()
    pieces, received = pieces[: len(groups)], pieces[len(groups) :]
    s, c = lax.axis_index("seq"), lax.axis_index("adapter")
    rows, size = received[0].shape
    held, rank, _ = factor.shape
    start = window.start(s)
    chunk = jnp.where(start >= window.depth, 1, 0)
    inside = pl.multiple_of(start - chunk * window.depth, 128)
    order = []
    for piece, distances in zip(pieces, groups):
        for i, distance in enumerate(distances):
            row = pl.multiple_of((i * CHUNKS + chunk) * rows, rows)
            x[len(order) * rows : (len(order) + 1) * rows, :] = piece[pl.ds(row, rows), pl.ds(inside, size)]
            order.append(distance)
    for piece, distance in zip(received, far):
        x[len(order) * rows : (len(order) + 1) * rows, :] = piece[...]
        order.append(distance)
    below = other.shape[0] - rank
    for index in range(held):
        theirs = other[below:, index * size : (index + 1) * size]
        for core, weights in ((c, factor[index]), (1 - c, theirs)):
            products[core * held + index] = lax.dot_general(
                x[...], weights, (((1,), (1,)), ((), ())), preferred_element_type=jnp.float32
            )
    lookup.wait()
    for i, distance in enumerate(order):
        chip = chip_at(distance, n)
        parts[chip] = products[adapters[chip * 2 * rows // BLOCK], i * rows : (i + 1) * rows, :]
    pack(parts, total)
    rounded[...] = total[...].astype(jnp.bfloat16)


def add_kernel(total, *refs):
    *received, out, rounded = refs
    value = total[...]
    for x in received:
        value += x[...].astype(jnp.float32)
    out[...] = value
    rounded[...] = value.astype(jnp.bfloat16)


def prepare_kernel(n, window, distances, tokens, down_ref, factor, *refs):
    *sends, down, sems = refs
    copies = [pltpu.make_async_copy(down_ref, down, sems.at[0])]
    for k, (distance, send) in enumerate(zip(distances, sends)):
        start = pl.multiple_of(window.start(chip_at(distance, n)), 128)
        copies.append(pltpu.make_async_copy(tokens.at[:, pl.ds(start, window.size)], send, sems.at[1 + k]))
    for copy in copies:
        copy.start()
    copies[0].wait()
    zeros = jnp.zeros((down.shape[1], window.size - window.width), jnp.float32)
    for index in range(down.shape[0]):
        wide = jnp.concatenate([down[index], zeros], 1)
        factor[index] = pltpu.roll(wide, window.shift(lax.axis_index("seq")), 1).astype(jnp.bfloat16)
    for copy in copies[1:]:
        copy.wait()


def full_rows(rows):
    return max(rows, 128)


def assemble_core(ref, chips, rows, held):
    depth = ref.shape[1]
    for i in range(chips):
        for k in range(CHUNKS):
            at = (i * CHUNKS + k) * rows
            held[i * rows : (i + 1) * rows, k * depth : (k + 1) * depth] = ref[at : at + rows, :]


def core_kernel(rows, ref, *refs):
    *weights, base, held = refs
    assemble_core(ref, base.shape[0] // rows, rows, held)
    columns = tile_width(base.shape[1])
    for j in range(0, base.shape[1], columns):
        at = slice(j, j + columns)
        base[:, at] = multiply(held, weights, at)[: base.shape[0]]


def both_kernel(rows, ref, mine, *refs):
    *weights, base, held = refs
    chips = base.shape[0] // (2 * rows)
    c = lax.axis_index("adapter")
    assemble_core(ref, chips, rows, held)
    columns = tile_width(base.shape[1])
    for j in range(0, base.shape[1], columns):
        at = slice(j, j + columns)
        tile = multiply(held, weights, at)
        for i in range(chips):
            here = slice(i * rows, (i + 1) * rows)
            for core, value in ((c, mine[here, at]), (1 - c, tile[here])):
                base[pl.ds(pl.multiple_of((2 * i + core) * rows, rows), rows), at] = value


def core_rows(ref, chips, rows, weights, after, mine=None):
    total, depth, width = rows * chips, sum(w.shape[0] for w in weights), weights[0].shape[1]
    (base,) = call(
        functools.partial(core_kernel if mine is None else both_kernel, rows),
        [ref] + ([] if mine is None else [mine]) + weights,
        after,
        [((total if mine is None else 2 * total, width), jnp.float32)],
        [pltpu.VMEM((full_rows(total), depth), jnp.bfloat16)],
        limit=8 + (2 * total * depth >> 20),
        flops=2 * total * depth * width,
    )
    return base


def cast_kernel(source, out):
    out[...] = source[...].astype(out.dtype)


def in_hbm(arrays):
    return [pltpu.with_memory_space_constraint(x, pltpu.HBM) for x in arrays]


def prepare(kernel, arrays, later, outs, scratch):
    operands = len(arrays)

    def body(*refs):
        kernel(*refs[:operands], *refs[operands + len(later) :])

    return pl.pallas_call(
        body,
        out_shape=[pltpu.VMEM(shape, dtype) for shape, dtype in outs],
        in_specs=[pl.BlockSpec(memory_space=pltpu.HBM)] * (operands + len(later)),
        out_specs=whole(len(outs)),
        scratch_shapes=scratch,
        compiler_params=pltpu.CompilerParams(vmem_limit_bytes=8 << 20),
        cost_estimate=pl.CostEstimate(flops=0, bytes_accessed=0, transcendentals=0),
    )(*in_hbm(arrays), *in_hbm(later))


def assemble(pairs, counts, rows, held):
    c = lax.axis_index("adapter")
    first = 0
    for pair, chips in zip(pairs, counts):
        depth = pair[0].shape[1]
        for chip in range(chips):
            for k in range(CHUNKS):
                at = (chip * CHUNKS + k) * rows
                for ref, core in zip(pair, (c, 1 - c)):
                    row = pl.multiple_of(first + core * rows, rows)
                    held[pl.ds(row, rows), k * depth : (k + 1) * depth] = ref[at : at + rows, :]
            first += 2 * rows


def tile_width(width):
    return 768 if width % 768 == 0 else width


def multiply(held, weights, at):
    total, first = 0.0, 0
    for w in weights:
        columns = held[:, first : first + w.shape[0]]
        total += jnp.dot(columns, w[:, at], preferred_element_type=jnp.float32)
        first += w.shape[0]
    return total


def finish_kernel(n, rows, groups, skipped, *refs):
    count = len(groups) - 1
    bases, refs = refs[:count], refs[count:]
    mine, others, weight, own, other, up_ref, adapters_ref, live_ref = refs[:8]
    out_ref, held, shrink, block, adapters, live, sems, small_sems = refs[8 + skipped :]
    lookups = [
        pltpu.make_async_copy(source, to, small_sems.at[k])
        for k, (source, to) in enumerate(((adapters_ref, adapters), (live_ref, live)))
    ]
    for lookup in lookups:
        lookup.start()
    c = lax.axis_index("adapter")
    chip_rows, rank = 2 * rows, up_ref.shape[1]
    tiles, _, columns = block.shape
    assemble([(mine, others)], [1], rows, held)
    last = multiply(held, [weight], slice(0, columns))
    for t in range(n):
        i, k = t % (n // 2), t // (n // 2)
        for ref, core in ((own, c), (other, 1 - c)):
            part = ref[i * rows : (i + 1) * rows, k * rank : (k + 1) * rank]
            shrink[t, pl.ds(pl.multiple_of(core * rows, rows), rows), :] = part.astype(jnp.bfloat16)
    places = [
        (distance, base, i * chip_rows)
        for base, distances in zip([*bases, None], groups)
        for i, distance in enumerate(distances)
    ]
    for lookup in lookups:
        lookup.wait()
    copies = []
    for j in range(tiles):
        at = slice(j * columns, (j + 1) * columns)
        if j:
            last = multiply(held, [weight], at)
        for i, (distance, base, row) in enumerate(places):
            chip = chip_at(distance, n)
            first = chip * chip_rows
            of_block = first // BLOCK
            delta = jnp.dot(shrink[chip], up_ref[adapters[of_block], :, at], preferred_element_type=jnp.float32)
            index = lax.broadcasted_iota(jnp.int32, delta.shape, 0) + (first - of_block * BLOCK)
            value = last[:chip_rows] if base is None else base[row : row + chip_rows, at]
            place = pl.ds(i * chip_rows, chip_rows)
            block[j, place, :] = jnp.where(index < live[of_block], value + delta, 0.0).astype(out_ref.dtype)
            copies.append(
                pltpu.make_async_copy(
                    block.at[j, place, :],
                    out_ref.at[pl.ds(pl.multiple_of(first, chip_rows), chip_rows), pl.ds(j * columns, columns)],
                    sems.at[j, i],
                )
            )
            copies[-1].start()
    for copy in copies:
        copy.wait()


def finish(n, rows, groups, lookups, bases, last_pair, weight, sums, up, after):
    (rank, width), depth = up.shape[1:], weight.shape[0]
    total, columns = 2 * n * rows, tile_width(width)
    arrays = [*bases, *last_pair, weight, *sums, up]
    held = full_rows(2 * rows)
    return pl.pallas_call(
        functools.partial(finish_kernel, n, rows, groups, len(after)),
        out_shape=jax.ShapeDtypeStruct((total, width), jnp.bfloat16),
        in_specs=whole(len(arrays)) + [pl.BlockSpec(memory_space=pl.ANY)] * (len(lookups) + len(after)),
        out_specs=pl.BlockSpec(memory_space=pl.ANY),
        scratch_shapes=[
            pltpu.VMEM((held, depth), jnp.bfloat16),
            pltpu.VMEM((n, 2 * rows, rank), jnp.bfloat16),
            pltpu.VMEM((width // columns, total, columns), jnp.bfloat16),
            *(pltpu.SMEM(x.shape, x.dtype) for x in lookups),
            pltpu.SemaphoreType.DMA((width // columns, n)),
            pltpu.SemaphoreType.DMA((len(lookups),)),
        ],
        compiler_params=pltpu.CompilerParams(vmem_limit_bytes=10 << 20),
        cost_estimate=pl.CostEstimate(
            flops=2 * held * depth * width, bytes_accessed=2 * total * width, transcendentals=0
        ),
    )(*in_vmem(arrays), *lookups, *after)


def on_device(n, tokens, weight, down, up, adapter_per_block, rows_per_block):
    rows, features = tokens.shape
    depth = features // CHUNKS
    held, width, rank = down.shape
    last = n // 2
    adapters = adapter_per_block[:, 0]
    window = Window(n, width, depth)
    near, mid, far = ([d for hop in hops for d in hop_distances(hop, n)] for hops in ((0, 1), range(2, last - 1), [last - 1]))
    half = (n // 2 * rows, 2 * rank)
    sums = [(half, jnp.float32), (half, jnp.bfloat16)]

    (behind,), (ahead,) = ring_hop([tokens], [tokens], n)
    ends = far + [last]
    bf16 = jnp.bfloat16
    factor, *sends = prepare(
        functools.partial(prepare_kernel, n, window, ends),
        [tokens, jnp.swapaxes(down, 1, 2)],
        [weight, up],
        [((held, rank, window.size), bf16)] + [((rows, window.size), bf16)] * len(ends),
        [
            pltpu.VMEM((held, rank, width), down.dtype),
            pltpu.SemaphoreType.DMA((1 + len(ends),)),
        ],
    )
    received = [lax.ppermute(x, AXES, ring_perm(n, d)) for d, x in zip(ends, sends)]
    come_from = [-d for d in far] + [last]
    piece = ((rows, depth), bf16)
    near_rows, *chunks = call(
        near_kernel,
        [tokens, behind, ahead, factor],
        received,
        [((len(near) * CHUNKS * rows + rank, depth), bf16)] + [piece] * (2 * CHUNKS),
    )

    up_way, down_way = chunks[:CHUNKS], chunks[CHUNKS:]
    weights = [weight]
    near_swapped = swap_cores(near_rows, n)
    mine = core_rows(near_rows, len(near), rows, weights, [])
    (up,) = call(cast_kernel, [up], [mine], [(up.shape, bf16)])
    arrived = []
    for _ in range(2, last - 1):
        up_way, down_way = ring_hop(up_way, down_way, n)
        arrived += up_way + down_way
    (mid_rows,) = join(arrived, [mine, up])

    total, rounded = call(
        functools.partial(partial_kernel, n, window, [near, mid], come_from),
        [near_rows, mid_rows, *received, factor, near_swapped],
        [],
        sums,
        [
            pltpu.SMEM(adapters.shape, jnp.int32),
            pltpu.VMEM((n * rows, window.size), bf16),
            pltpu.VMEM((2 * held, n * rows, rank), jnp.float32),
            pltpu.VMEM((n, rows, rank), jnp.float32),
            pltpu.SemaphoreType.DMA,
        ],
        outside=[adapters],
    )
    bases = [core_rows(near_swapped, len(near), rows, weights, [rounded], mine)]
    total, rounded = call(add_kernel, [total, lax.ppermute(rounded, AXES, y_perm(n))], [], sums)
    up_way, down_way = ring_hop(up_way, down_way, n)
    late_rows, turned = join([mid_rows, *up_way, *down_way], [rounded, *bases], 1)

    late = mid + far
    late_swapped = swap_cores(late_rows, n)
    mine = core_rows(late_rows, len(late), rows, weights, [])
    total, rounded = call(
        add_kernel,
        [total] + [lax.ppermute(rounded, AXES, z_perm(n, shift)) for shift in range(1, n // 2)],
        [],
        sums,
    )
    (last_rows,) = join([lax.ppermute(turned, AXES, ring_perm(n, 1, -1))], [rounded, mine])

    bases.append(core_rows(late_swapped, len(late), rows, weights, [last_rows], mine))
    last_pair = (last_rows, swap_cores(last_rows, n))
    return finish(
        n,
        rows,
        [near, late, [last]],
        [adapters, rows_per_block],
        bases,
        last_pair,
        weight,
        [total, swap_cores(rounded, n)],
        up,
        [],
    )


def solution(mesh):
    placed = (
        P(("groups", "seq", "adapter"), None),
        P(None, ("seq", "adapter")),
        P(("groups", "adapter"), "seq", None),
        P("groups", None, ("seq", "adapter")),
        P("groups", None),
        P("groups"),
    )
    return jax.shard_map(
        functools.partial(on_device, mesh.shape["seq"]),
        mesh=mesh,
        in_specs=placed,
        out_specs=P("groups", ("seq", "adapter")),
        check_vma=False,
    )
```

```python
import functools

import jax
import jax.numpy as jnp
from jax import lax
from jax.experimental import pallas as pl
from jax.experimental.pallas import tpu as pltpu
from jax.sharding import PartitionSpec as P

BLOCK = 128
AXES = ("seq", "adapter")
CHUNKS = 2


def ring_perm(n, way, other_way=None):
    order = [2 * z for z in range(n // 2)] + [2 * z + 1 for z in reversed(range(n // 2))]
    ways = (way, way if other_way is None else other_way)
    return [(2 * s + c, 2 * order[(pos + ways[c]) % n] + c) for pos, s in enumerate(order) for c in range(2)]


def swap_cores(x, n):
    return lax.ppermute(x, AXES, [(2 * s + c, 2 * s + 1 - c) for s in range(n) for c in range(2)])


def chip_at(distance, n):
    s = lax.axis_index("seq")
    z = s >> 1
    pos = jnp.where(s & 1 == 0, z, n - 1 - z) + distance
    pos = jnp.where(pos >= n, pos - n, pos)
    pos = jnp.where(pos < 0, pos + n, pos)
    return jnp.where(pos < n // 2, 2 * pos, 2 * (n - 1 - pos) + 1)


def y_perm(n):
    return [(2 * s + c, 2 * (s ^ 1) + c) for s in range(n) for c in range(2)]


def z_perm(n, shift):
    nz = n // 2
    return [
        (2 * (2 * z + y) + c, 2 * (2 * ((z - shift) % nz) + y) + c)
        for z in range(nz)
        for y in range(2)
        for c in range(2)
    ]


def hop_distances(hop, n):
    if hop == 0:
        return [0]
    return [-hop, hop] if hop < n // 2 else [hop]


def ring_hop(up, down, n):
    return [lax.ppermute(x, AXES, ring_perm(n, 1)) for x in up], [lax.ppermute(x, AXES, ring_perm(n, -1)) for x in down]


def join_kernel(ways, *refs):
    count = len(refs) - 1 - ways
    pieces, out, on = refs[:count], refs[count], refs[count + 1 :]
    first = 0
    for piece in pieces:
        out[first : first + piece.shape[0], :] = piece[...]
        first += piece.shape[0]
    arrived = pieces[len(pieces) - 2 * CHUNKS :]
    if ways == 1:
        c = lax.axis_index("adapter")
        rows = arrived[0].shape[0]
        for core in range(2):

            @pl.when(c == core)
            def _():
                for i, piece in enumerate(arrived[core * CHUNKS : (core + 1) * CHUNKS]):
                    on[0][i * rows : (i + 1) * rows, :] = piece[...]


def join(pieces, after, ways=0):
    (rows, depth), dtype = pieces[-1].shape, pieces[-1].dtype
    on = [CHUNKS * rows] * ways
    outs = [((count, depth), dtype) for count in [sum(x.shape[0] for x in pieces), *on]]
    return call(functools.partial(join_kernel, ways), pieces, after, outs)


def whole(count):
    return [pl.BlockSpec(memory_space=pltpu.VMEM)] * count


def in_vmem(arrays):
    return [pltpu.with_memory_space_constraint(x, pltpu.VMEM) for x in arrays]


def call(kernel, arrays, after, outs, scratch=(), limit=8, flops=0, outside=()):
    operands = len(arrays) + len(outside)

    def body(*refs):
        kernel(*refs[:operands], *refs[operands + len(after) :])

    return pl.pallas_call(
        body,
        out_shape=[pltpu.VMEM(shape, dtype) for shape, dtype in outs],
        in_specs=whole(len(arrays)) + [pl.BlockSpec(memory_space=pl.ANY)] * (len(outside) + len(after)),
        out_specs=whole(len(outs)),
        scratch_shapes=list(scratch),
        compiler_params=pltpu.CompilerParams(vmem_limit_bytes=limit << 20),
        cost_estimate=pl.CostEstimate(flops=flops, bytes_accessed=0, transcendentals=0),
    )(*in_vmem(arrays), *outside, *after)


class Window:
    def __init__(self, n, width, depth):
        self.width, self.depth = width, depth
        self.size = -(-(width + max(s * width % 128 for s in range(n))) // 128) * 128
        for s in range(n):
            start = s * width // 128 * 128
            assert start // depth == (start + self.size - 1) // depth

    def start(self, chip):
        return (chip * self.width) >> 7 << 7

    def shift(self, chip):
        return chip * self.width - self.start(chip)


def near_kernel(tokens, behind, ahead, factor, out, *chunks):
    held, rank, size = factor.shape
    rows, depth = chunks[0].shape
    for i, ref in enumerate((tokens, behind, ahead)):
        for k in range(CHUNKS):
            piece = ref[:, k * depth : (k + 1) * depth]
            at = (i * CHUNKS + k) * rows
            out[at : at + rows, :] = piece
            if i:
                chunks[(i - 1) * CHUNKS + k][...] = piece
    first = 3 * CHUNKS * rows
    out[first:, :] = jnp.zeros((rank, depth), out.dtype)
    for index in range(held):
        out[first:, index * size : (index + 1) * size] = factor[index]


def pack(parts, out):
    chips, rows, rank = parts.shape
    for t in range(chips):
        i, k = t % (chips // 2), t // (chips // 2)
        out[i * rows : (i + 1) * rows, k * rank : (k + 1) * rank] = parts[t].astype(out.dtype)


def partial_kernel(n, window, groups, far, *refs):
    *pieces, factor, other, adapters_ref, total, rounded, adapters, x, products, parts, sem = refs
    lookup = pltpu.make_async_copy(adapters_ref, adapters, sem)
    lookup.start()
    pieces, received = pieces[: len(groups)], pieces[len(groups) :]
    s, c = lax.axis_index("seq"), lax.axis_index("adapter")
    rows, size = received[0].shape
    held, rank, _ = factor.shape
    start = window.start(s)
    chunk = jnp.where(start >= window.depth, 1, 0)
    inside = pl.multiple_of(start - chunk * window.depth, 128)
    order = []
    for piece, distances in zip(pieces, groups):
        for i, distance in enumerate(distances):
            row = pl.multiple_of((i * CHUNKS + chunk) * rows, rows)
            x[len(order) * rows : (len(order) + 1) * rows, :] = piece[pl.ds(row, rows), pl.ds(inside, size)]
            order.append(distance)
    for piece, distance in zip(received, far):
        x[len(order) * rows : (len(order) + 1) * rows, :] = piece[...]
        order.append(distance)
    below = other.shape[0] - rank
    for index in range(held):
        theirs = other[below:, index * size : (index + 1) * size]
        for core, weights in ((c, factor[index]), (1 - c, theirs)):
            products[core * held + index] = lax.dot_general(
                x[...], weights, (((1,), (1,)), ((), ())), preferred_element_type=jnp.float32
            )
    lookup.wait()
    for i, distance in enumerate(order):
        chip = chip_at(distance, n)
        parts[chip] = products[adapters[chip * 2 * rows // BLOCK], i * rows : (i + 1) * rows, :]
    pack(parts, total)
    rounded[...] = total[...].astype(jnp.bfloat16)


def add_kernel(total, *refs):
    *received, out, rounded = refs
    value = total[...]
    for x in received:
        value += x[...].astype(jnp.float32)
    out[...] = value
    rounded[...] = value.astype(jnp.bfloat16)


def prepare_kernel(n, window, distances, tokens, down_ref, factor, *refs):
    *sends, down, sems = refs
    copies = [pltpu.make_async_copy(down_ref, down, sems.at[0])]
    for k, (distance, send) in enumerate(zip(distances, sends)):
        start = pl.multiple_of(window.start(chip_at(distance, n)), 128)
        copies.append(pltpu.make_async_copy(tokens.at[:, pl.ds(start, window.size)], send, sems.at[1 + k]))
    for copy in copies:
        copy.start()
    copies[0].wait()
    zeros = jnp.zeros((down.shape[1], window.size - window.width), jnp.float32)
    for index in range(down.shape[0]):
        wide = jnp.concatenate([down[index], zeros], 1)
        factor[index] = pltpu.roll(wide, window.shift(lax.axis_index("seq")), 1).astype(jnp.bfloat16)
    for copy in copies[1:]:
        copy.wait()


def full_rows(rows):
    return max(rows, 128)


def assemble_core(ref, chips, rows, held):
    depth = ref.shape[1]
    for i in range(chips):
        for k in range(CHUNKS):
            at = (i * CHUNKS + k) * rows
            held[i * rows : (i + 1) * rows, k * depth : (k + 1) * depth] = ref[at : at + rows, :]


def core_kernel(rows, ref, *refs):
    *weights, base, held = refs
    assemble_core(ref, base.shape[0] // rows, rows, held)
    columns = tile_width(base.shape[1])
    for j in range(0, base.shape[1], columns):
        at = slice(j, j + columns)
        base[:, at] = multiply(held, weights, at)[: base.shape[0]]


def both_kernel(rows, ref, mine, *refs):
    *weights, base, held = refs
    chips = base.shape[0] // (2 * rows)
    c = lax.axis_index("adapter")
    assemble_core(ref, chips, rows, held)
    columns = tile_width(base.shape[1])
    for j in range(0, base.shape[1], columns):
        at = slice(j, j + columns)
        tile = multiply(held, weights, at)
        for i in range(chips):
            here = slice(i * rows, (i + 1) * rows)
            for core, value in ((c, mine[here, at]), (1 - c, tile[here])):
                base[pl.ds(pl.multiple_of((2 * i + core) * rows, rows), rows), at] = value


def core_rows(ref, chips, rows, weights, after, mine=None):
    total, depth, width = rows * chips, sum(w.shape[0] for w in weights), weights[0].shape[1]
    (base,) = call(
        functools.partial(core_kernel if mine is None else both_kernel, rows),
        [ref] + ([] if mine is None else [mine]) + weights,
        after,
        [((total if mine is None else 2 * total, width), jnp.float32)],
        [pltpu.VMEM((full_rows(total), depth), jnp.bfloat16)],
        limit=8 + (2 * total * depth >> 20),
        flops=2 * total * depth * width,
    )
    return base


def cast_kernel(source, out):
    out[...] = source[...].astype(out.dtype)


def in_hbm(arrays):
    return [pltpu.with_memory_space_constraint(x, pltpu.HBM) for x in arrays]


def prepare(kernel, arrays, later, outs, scratch):
    operands = len(arrays)

    def body(*refs):
        kernel(*refs[:operands], *refs[operands + len(later) :])

    return pl.pallas_call(
        body,
        out_shape=[pltpu.VMEM(shape, dtype) for shape, dtype in outs],
        in_specs=[pl.BlockSpec(memory_space=pltpu.HBM)] * (operands + len(later)),
        out_specs=whole(len(outs)),
        scratch_shapes=scratch,
        compiler_params=pltpu.CompilerParams(vmem_limit_bytes=8 << 20),
        cost_estimate=pl.CostEstimate(flops=0, bytes_accessed=0, transcendentals=0),
    )(*in_hbm(arrays), *in_hbm(later))


def assemble(pairs, counts, rows, held):
    c = lax.axis_index("adapter")
    first = 0
    for pair, chips in zip(pairs, counts):
        depth = pair[0].shape[1]
        for chip in range(chips):
            for k in range(CHUNKS):
                at = (chip * CHUNKS + k) * rows
                for ref, core in zip(pair, (c, 1 - c)):
                    row = pl.multiple_of(first + core * rows, rows)
                    held[pl.ds(row, rows), k * depth : (k + 1) * depth] = ref[at : at + rows, :]
            first += 2 * rows


def tile_width(width):
    return 768 if width % 768 == 0 else width


def multiply(held, weights, at):
    total, first = 0.0, 0
    for w in weights:
        columns = held[:, first : first + w.shape[0]]
        total += jnp.dot(columns, w[:, at], preferred_element_type=jnp.float32)
        first += w.shape[0]
    return total


def finish_kernel(n, rows, groups, skipped, *refs):
    count = len(groups) - 1
    bases, refs = refs[:count], refs[count:]
    mine, others, weight, own, other, up_ref, adapters_ref, live_ref = refs[:8]
    out_ref, held, shrink, block, adapters, live, sems, small_sems = refs[8 + skipped :]
    lookups = [
        pltpu.make_async_copy(source, to, small_sems.at[k])
        for k, (source, to) in enumerate(((adapters_ref, adapters), (live_ref, live)))
    ]
    for lookup in lookups:
        lookup.start()
    c = lax.axis_index("adapter")
    chip_rows, rank = 2 * rows, up_ref.shape[1]
    tiles, _, columns = block.shape
    assemble([(mine, others)], [1], rows, held)
    for t in range(n):
        i, k = t % (n // 2), t // (n // 2)
        for ref, core in ((own, c), (other, 1 - c)):
            part = ref[i * rows : (i + 1) * rows, k * rank : (k + 1) * rank]
            shrink[t, pl.ds(pl.multiple_of(core * rows, rows), rows), :] = part.astype(jnp.bfloat16)
    places = [
        (distance, base, i * chip_rows)
        for base, distances in zip([*bases, None], groups)
        for i, distance in enumerate(distances)
    ]
    for lookup in lookups:
        lookup.wait()
    copies = []
    piece = 256 if columns % 256 == 0 else columns
    for j in range(tiles):
        at = slice(j * columns, (j + 1) * columns)
        last = multiply(held, [weight], at)
        for i, (distance, base, row) in enumerate(places):
            chip = chip_at(distance, n)
            first = chip * chip_rows
            of_block = first // BLOCK
            place = pl.ds(i * chip_rows, chip_rows)
            mine_shrink, adapter = shrink[chip], adapters[of_block]
            index = lax.broadcasted_iota(jnp.int32, (chip_rows, piece), 0) + (first - of_block * BLOCK)
            on = index < live[of_block]
            for k in range(0, columns, piece):
                cut = slice(j * columns + k, j * columns + k + piece)
                delta = jnp.dot(mine_shrink, up_ref[adapter, :, cut], preferred_element_type=jnp.float32)
                value = last[:chip_rows, k : k + piece] if base is None else base[row : row + chip_rows, cut]
                block[j, place, k : k + piece] = jnp.where(on, value + delta, 0.0).astype(out_ref.dtype)
            copies.append(
                pltpu.make_async_copy(
                    block.at[j, place, :],
                    out_ref.at[pl.ds(pl.multiple_of(first, chip_rows), chip_rows), pl.ds(j * columns, columns)],
                    sems.at[j, i],
                )
            )
            copies[-1].start()
    for copy in copies:
        copy.wait()


def finish(n, rows, groups, lookups, bases, last_pair, weight, sums, up, after):
    (rank, width), depth = up.shape[1:], weight.shape[0]
    total, columns = 2 * n * rows, tile_width(width)
    arrays = [*bases, *last_pair, weight, *sums, up]
    held = full_rows(2 * rows)
    return pl.pallas_call(
        functools.partial(finish_kernel, n, rows, groups, len(after)),
        out_shape=jax.ShapeDtypeStruct((total, width), jnp.bfloat16),
        in_specs=whole(len(arrays)) + [pl.BlockSpec(memory_space=pl.ANY)] * (len(lookups) + len(after)),
        out_specs=pl.BlockSpec(memory_space=pl.ANY),
        scratch_shapes=[
            pltpu.VMEM((held, depth), jnp.bfloat16),
            pltpu.VMEM((n, 2 * rows, rank), jnp.bfloat16),
            pltpu.VMEM((width // columns, total, columns), jnp.bfloat16),
            *(pltpu.SMEM(x.shape, x.dtype) for x in lookups),
            pltpu.SemaphoreType.DMA((width // columns, n)),
            pltpu.SemaphoreType.DMA((len(lookups),)),
        ],
        compiler_params=pltpu.CompilerParams(vmem_limit_bytes=10 << 20),
        cost_estimate=pl.CostEstimate(
            flops=2 * held * depth * width, bytes_accessed=2 * total * width, transcendentals=0
        ),
    )(*in_vmem(arrays), *lookups, *after)


def on_device(n, tokens, weight, down, up, adapter_per_block, rows_per_block):
    rows, features = tokens.shape
    depth = features // CHUNKS
    held, width, rank = down.shape
    last = n // 2
    adapters = adapter_per_block[:, 0]
    window = Window(n, width, depth)
    near, mid, far = ([d for hop in hops for d in hop_distances(hop, n)] for hops in ((0, 1), range(2, last - 1), [last - 1]))
    half = (n // 2 * rows, 2 * rank)
    sums = [(half, jnp.float32), (half, jnp.bfloat16)]

    (behind,), (ahead,) = ring_hop([tokens], [tokens], n)
    ends = far + [last]
    bf16 = jnp.bfloat16
    factor, *sends = prepare(
        functools.partial(prepare_kernel, n, window, ends),
        [tokens, jnp.swapaxes(down, 1, 2)],
        [weight, up],
        [((held, rank, window.size), bf16)] + [((rows, window.size), bf16)] * len(ends),
        [
            pltpu.VMEM((held, rank, width), down.dtype),
            pltpu.SemaphoreType.DMA((1 + len(ends),)),
        ],
    )
    received = [lax.ppermute(x, AXES, ring_perm(n, d)) for d, x in zip(ends, sends)]
    come_from = [-d for d in far] + [last]
    piece = ((rows, depth), bf16)
    near_rows, *chunks = call(
        near_kernel,
        [tokens, behind, ahead, factor],
        received,
        [((len(near) * CHUNKS * rows + rank, depth), bf16)] + [piece] * (2 * CHUNKS),
    )

    up_way, down_way = chunks[:CHUNKS], chunks[CHUNKS:]
    weights = [weight]
    near_swapped = swap_cores(near_rows, n)
    mine = core_rows(near_rows, len(near), rows, weights, [])
    (up,) = call(cast_kernel, [up], [mine], [(up.shape, bf16)])
    arrived = []
    for _ in range(2, last - 1):
        up_way, down_way = ring_hop(up_way, down_way, n)
        arrived += up_way + down_way
    (mid_rows,) = join(arrived, [mine, up])

    total, rounded = call(
        functools.partial(partial_kernel, n, window, [near, mid], come_from),
        [near_rows, mid_rows, *received, factor, near_swapped],
        [],
        sums,
        [
            pltpu.SMEM(adapters.shape, jnp.int32),
            pltpu.VMEM((n * rows, window.size), bf16),
            pltpu.VMEM((2 * held, n * rows, rank), jnp.float32),
            pltpu.VMEM((n, rows, rank), jnp.float32),
            pltpu.SemaphoreType.DMA,
        ],
        outside=[adapters],
    )
    bases = [core_rows(near_swapped, len(near), rows, weights, [rounded], mine)]
    total, rounded = call(add_kernel, [total, lax.ppermute(rounded, AXES, y_perm(n))], [], sums)
    up_way, down_way = ring_hop(up_way, down_way, n)
    late_rows, turned = join([mid_rows, *up_way, *down_way], [rounded, *bases], 1)

    late = mid + far
    late_swapped = swap_cores(late_rows, n)
    mine = core_rows(late_rows, len(late), rows, weights, [])
    total, rounded = call(
        add_kernel,
        [total] + [lax.ppermute(rounded, AXES, z_perm(n, shift)) for shift in range(1, n // 2)],
        [],
        sums,
    )
    (last_rows,) = join([lax.ppermute(turned, AXES, ring_perm(n, 1, -1))], [rounded, mine])

    bases.append(core_rows(late_swapped, len(late), rows, weights, [last_rows], mine))
    last_pair = (last_rows, swap_cores(last_rows, n))
    return finish(
        n,
        rows,
        [near, late, [last]],
        [adapters, rows_per_block],
        bases,
        last_pair,
        weight,
        [total, swap_cores(rounded, n)],
        up,
        [],
    )


def solution(mesh):
    placed = (
        P(("groups", "seq", "adapter"), None),
        P(None, ("seq", "adapter")),
        P(("groups", "adapter"), "seq", None),
        P("groups", None, ("seq", "adapter")),
        P("groups", None),
        P("groups"),
    )
    return jax.shard_map(
        functools.partial(on_device, mesh.shape["seq"]),
        mesh=mesh,
        in_specs=placed,
        out_specs=P("groups", ("seq", "adapter")),
        check_vma=False,
    )
```

```python
import functools

import jax
import jax.numpy as jnp
from jax import lax
from jax.experimental import pallas as pl
from jax.experimental.pallas import tpu as pltpu
from jax.sharding import PartitionSpec as P

BLOCK = 128
AXES = ("seq", "adapter")
CHUNKS = 2


def ring_perm(n, way, other_way=None):
    order = [2 * z for z in range(n // 2)] + [2 * z + 1 for z in reversed(range(n // 2))]
    ways = (way, way if other_way is None else other_way)
    return [(2 * s + c, 2 * order[(pos + ways[c]) % n] + c) for pos, s in enumerate(order) for c in range(2)]


def swap_cores(x, n):
    return lax.ppermute(x, AXES, [(2 * s + c, 2 * s + 1 - c) for s in range(n) for c in range(2)])


def chip_at(distance, n):
    s = lax.axis_index("seq")
    z = s >> 1
    pos = jnp.where(s & 1 == 0, z, n - 1 - z) + distance
    pos = jnp.where(pos >= n, pos - n, pos)
    pos = jnp.where(pos < 0, pos + n, pos)
    return jnp.where(pos < n // 2, 2 * pos, 2 * (n - 1 - pos) + 1)


def y_perm(n):
    return [(2 * s + c, 2 * (s ^ 1) + c) for s in range(n) for c in range(2)]


def z_perm(n, shift):
    nz = n // 2
    return [
        (2 * (2 * z + y) + c, 2 * (2 * ((z - shift) % nz) + y) + c)
        for z in range(nz)
        for y in range(2)
        for c in range(2)
    ]


def hop_distances(hop, n):
    if hop == 0:
        return [0]
    return [-hop, hop] if hop < n // 2 else [hop]


def ring_hop(up, down, n):
    return [lax.ppermute(x, AXES, ring_perm(n, 1)) for x in up], [lax.ppermute(x, AXES, ring_perm(n, -1)) for x in down]


def join_kernel(ways, *refs):
    count = len(refs) - 1 - ways
    pieces, out, on = refs[:count], refs[count], refs[count + 1 :]
    first = 0
    for piece in pieces:
        out[first : first + piece.shape[0], :] = piece[...]
        first += piece.shape[0]
    arrived = pieces[len(pieces) - 2 * CHUNKS :]
    if ways == 1:
        c = lax.axis_index("adapter")
        rows = arrived[0].shape[0]
        for core in range(2):

            @pl.when(c == core)
            def _():
                for i, piece in enumerate(arrived[core * CHUNKS : (core + 1) * CHUNKS]):
                    on[0][i * rows : (i + 1) * rows, :] = piece[...]


def join(pieces, after, ways=0):
    (rows, depth), dtype = pieces[-1].shape, pieces[-1].dtype
    on = [CHUNKS * rows] * ways
    outs = [((count, depth), dtype) for count in [sum(x.shape[0] for x in pieces), *on]]
    return call(functools.partial(join_kernel, ways), pieces, after, outs)


def whole(count):
    return [pl.BlockSpec(memory_space=pltpu.VMEM)] * count


def in_vmem(arrays):
    return [pltpu.with_memory_space_constraint(x, pltpu.VMEM) for x in arrays]


def call(kernel, arrays, after, outs, scratch=(), limit=8, flops=0, outside=()):
    operands = len(arrays) + len(outside)

    def body(*refs):
        kernel(*refs[:operands], *refs[operands + len(after) :])

    return pl.pallas_call(
        body,
        out_shape=[pltpu.VMEM(shape, dtype) for shape, dtype in outs],
        in_specs=whole(len(arrays)) + [pl.BlockSpec(memory_space=pl.ANY)] * (len(outside) + len(after)),
        out_specs=whole(len(outs)),
        scratch_shapes=list(scratch),
        compiler_params=pltpu.CompilerParams(vmem_limit_bytes=limit << 20),
        cost_estimate=pl.CostEstimate(flops=flops, bytes_accessed=0, transcendentals=0),
    )(*in_vmem(arrays), *outside, *after)


class Window:
    def __init__(self, n, width, depth):
        self.width, self.depth = width, depth
        self.size = -(-(width + max(s * width % 128 for s in range(n))) // 128) * 128
        for s in range(n):
            start = s * width // 128 * 128
            assert start // depth == (start + self.size - 1) // depth

    def start(self, chip):
        return (chip * self.width) >> 7 << 7

    def shift(self, chip):
        return chip * self.width - self.start(chip)


def near_kernel(tokens, behind, ahead, factor, out, *chunks):
    held, rank, size = factor.shape
    rows, depth = chunks[0].shape
    for i, ref in enumerate((tokens, behind, ahead)):
        for k in range(CHUNKS):
            piece = ref[:, k * depth : (k + 1) * depth]
            at = (i * CHUNKS + k) * rows
            out[at : at + rows, :] = piece
            if i:
                chunks[(i - 1) * CHUNKS + k][...] = piece
    first = 3 * CHUNKS * rows
    out[first:, :] = jnp.zeros((rank, depth), out.dtype)
    for index in range(held):
        out[first:, index * size : (index + 1) * size] = factor[index]


def pack(parts, out):
    chips, rows, rank = parts.shape
    for t in range(chips):
        i, k = t % (chips // 2), t // (chips // 2)
        out[i * rows : (i + 1) * rows, k * rank : (k + 1) * rank] = parts[t].astype(out.dtype)


def partial_kernel(n, window, groups, far, *refs):
    *pieces, factor, other, adapters_ref, total, rounded, adapters, x, products, parts, sem = refs
    lookup = pltpu.make_async_copy(adapters_ref, adapters, sem)
    lookup.start()
    pieces, received = pieces[: len(groups)], pieces[len(groups) :]
    s, c = lax.axis_index("seq"), lax.axis_index("adapter")
    rows, size = received[0].shape
    held, rank, _ = factor.shape
    start = window.start(s)
    chunk = jnp.where(start >= window.depth, 1, 0)
    inside = pl.multiple_of(start - chunk * window.depth, 128)
    order = []
    for piece, distances in zip(pieces, groups):
        for i, distance in enumerate(distances):
            row = pl.multiple_of((i * CHUNKS + chunk) * rows, rows)
            x[len(order) * rows : (len(order) + 1) * rows, :] = piece[pl.ds(row, rows), pl.ds(inside, size)]
            order.append(distance)
    for piece, distance in zip(received, far):
        x[len(order) * rows : (len(order) + 1) * rows, :] = piece[...]
        order.append(distance)
    below = other.shape[0] - rank
    for index in range(held):
        theirs = other[below:, index * size : (index + 1) * size]
        for core, weights in ((c, factor[index]), (1 - c, theirs)):
            products[core * held + index] = lax.dot_general(
                x[...], weights, (((1,), (1,)), ((), ())), preferred_element_type=jnp.float32
            )
    lookup.wait()
    for i, distance in enumerate(order):
        chip = chip_at(distance, n)
        parts[chip] = products[adapters[chip * 2 * rows // BLOCK], i * rows : (i + 1) * rows, :]
    pack(parts, total)
    rounded[...] = total[...].astype(jnp.bfloat16)


def add_kernel(total, *refs):
    *received, out, rounded = refs
    value = total[...]
    for x in received:
        value += x[...].astype(jnp.float32)
    out[...] = value
    rounded[...] = value.astype(jnp.bfloat16)


def prepare_kernel(n, window, distances, tokens, down_ref, factor, *refs):
    *sends, down, sems = refs
    copies = [pltpu.make_async_copy(down_ref, down, sems.at[0])]
    for k, (distance, send) in enumerate(zip(distances, sends)):
        start = pl.multiple_of(window.start(chip_at(distance, n)), 128)
        copies.append(pltpu.make_async_copy(tokens.at[:, pl.ds(start, window.size)], send, sems.at[1 + k]))
    for copy in copies:
        copy.start()
    copies[0].wait()
    zeros = jnp.zeros((down.shape[1], window.size - window.width), jnp.float32)
    for index in range(down.shape[0]):
        wide = jnp.concatenate([down[index], zeros], 1)
        factor[index] = pltpu.roll(wide, window.shift(lax.axis_index("seq")), 1).astype(jnp.bfloat16)
    for copy in copies[1:]:
        copy.wait()


def full_rows(rows):
    return max(rows, 128)


def assemble_core(ref, chips, rows, held, skip=0, first=0):
    depth = ref.shape[1]
    for i in range(chips):
        for k in range(CHUNKS):
            at = ((skip + i) * CHUNKS + k) * rows
            held[first + i * rows : first + (i + 1) * rows, k * depth : (k + 1) * depth] = ref[at : at + rows, :]


def interleave(rows, chips, mine, others, base, at):
    c = lax.axis_index("adapter")
    for i in range(chips):
        here = slice(i * rows, (i + 1) * rows)
        for core, value in ((c, mine[here]), (1 - c, others[here])):
            base[pl.ds(pl.multiple_of((2 * i + core) * rows, rows), rows), at] = value


def core_kernel(rows, ref, *refs):
    *weights, base, held = refs
    assemble_core(ref, base.shape[0] // rows, rows, held)
    columns = narrow_width(base.shape[1])
    for j in range(0, base.shape[1], columns):
        at = slice(j, j + columns)
        base[:, at] = multiply(held, weights, at)[: base.shape[0]]


def near_base_kernel(rows, near, mid, swapped, mine, mid_rows, weight, base, mid_base, held):
    assemble_core(swapped, near, rows, held)
    assemble_core(mid_rows, mid, rows, held, 0, near * rows)
    columns = narrow_width(base.shape[1])
    for j in range(0, base.shape[1], columns):
        at = slice(j, j + columns)
        tile = multiply(held, [weight], at)
        interleave(rows, near, mine[: near * rows, at], tile, base, at)
        mid_base[:, at] = tile[near * rows : (near + mid) * rows]


def late_base_kernel(rows, mid, far, swapped, mine, weight, base, far_base, held):
    assemble_core(swapped, mid + far, rows, held)
    columns = narrow_width(base.shape[1])
    for j in range(0, base.shape[1], columns):
        at = slice(j, j + columns)
        tile = multiply(held, [weight], at)
        interleave(rows, mid, mine[:, at], tile, base, at)
        far_base[:, at] = tile[mid * rows : (mid + far) * rows]


def product(kernel, arrays, weight, after, total, outs):
    (depth, width), total = weight.shape, full_rows(total)
    return call(
        kernel,
        [*arrays, weight],
        after,
        [((rows, width), jnp.float32) for rows in outs],
        [pltpu.VMEM((total, depth), jnp.bfloat16)],
        limit=8 + (2 * total * depth >> 20),
        flops=2 * total * depth * width,
    )


def cast_kernel(source, out):
    out[...] = source[...].astype(out.dtype)


def in_hbm(arrays):
    return [pltpu.with_memory_space_constraint(x, pltpu.HBM) for x in arrays]


def prepare(kernel, arrays, later, outs, scratch):
    operands = len(arrays)

    def body(*refs):
        kernel(*refs[:operands], *refs[operands + len(later) :])

    return pl.pallas_call(
        body,
        out_shape=[pltpu.VMEM(shape, dtype) for shape, dtype in outs],
        in_specs=[pl.BlockSpec(memory_space=pltpu.HBM)] * (operands + len(later)),
        out_specs=whole(len(outs)),
        scratch_shapes=scratch,
        compiler_params=pltpu.CompilerParams(vmem_limit_bytes=8 << 20),
        cost_estimate=pl.CostEstimate(flops=0, bytes_accessed=0, transcendentals=0),
    )(*in_hbm(arrays), *in_hbm(later))


def assemble(pairs, counts, rows, held):
    c = lax.axis_index("adapter")
    first = 0
    for pair, chips in zip(pairs, counts):
        depth = pair[0].shape[1]
        for chip in range(chips):
            for k in range(CHUNKS):
                at = (chip * CHUNKS + k) * rows
                for ref, core in zip(pair, (c, 1 - c)):
                    row = pl.multiple_of(first + core * rows, rows)
                    held[pl.ds(row, rows), k * depth : (k + 1) * depth] = ref[at : at + rows, :]
            first += 2 * rows


def narrow_width(width):
    return 256 if width % 256 == 0 else width


def tile_width(width):
    return 768 if width % 768 == 0 else width


def multiply(held, weights, at):
    total, first = 0.0, 0
    for w in weights:
        columns = held[:, first : first + w.shape[0]]
        total += jnp.dot(columns, w[:, at], preferred_element_type=jnp.float32)
        first += w.shape[0]
    return total


def finish_kernel(n, rows, groups, *refs):
    near_base, mid_base, far_base, late_rows, mine, others, weight, own, other, up_ref = refs[:10]
    adapters_ref, live_ref, out_ref, held, shrink, far_rows, block, adapters, live, sems, small_sems = refs[10:]
    lookups = [
        pltpu.make_async_copy(source, to, small_sems.at[k])
        for k, (source, to) in enumerate(((adapters_ref, adapters), (live_ref, live)))
    ]
    for lookup in lookups:
        lookup.start()
    c = lax.axis_index("adapter")
    chip_rows, rank = 2 * rows, up_ref.shape[1]
    tiles, _, columns = block.shape
    _, mid, far, _ = (len(group) for group in groups)
    assemble([(mine, others)], [1], rows, held)
    assemble_core(late_rows, far, rows, held, mid, chip_rows)
    for t in range(n):
        i, k = t % (n // 2), t // (n // 2)
        for ref, core in ((own, c), (other, 1 - c)):
            part = ref[i * rows : (i + 1) * rows, k * rank : (k + 1) * rank]
            shrink[t, pl.ds(pl.multiple_of(core * rows, rows), rows), :] = part.astype(jnp.bfloat16)
    for lookup in lookups:
        lookup.wait()
    early = [(base, i) for base, group in ((near_base, groups[0]), (mid_base, groups[1])) for i in range(len(group))]
    sources = [distance for group in groups for distance in group]
    copies = []

    def put(j, which, value_of):
        at = slice(j * columns, (j + 1) * columns)
        for i in which:
            first = chip_at(sources[i], n) * chip_rows
            of_block = first // BLOCK
            delta = jnp.dot(
                shrink[chip_at(sources[i], n)],
                up_ref[adapters[of_block], :, at],
                preferred_element_type=jnp.float32,
            )
            index = lax.broadcasted_iota(jnp.int32, delta.shape, 0) + (first - of_block * BLOCK)
            value = jnp.where(index < live[of_block], value_of(i, at) + delta, 0.0)
            block[j, i * chip_rows : (i + 1) * chip_rows, :] = value.astype(out_ref.dtype)

    def send(j, which):
        for i in which:
            first = pl.multiple_of(chip_at(sources[i], n) * chip_rows, chip_rows)
            copies.append(
                pltpu.make_async_copy(
                    block.at[j, pl.ds(i * chip_rows, chip_rows), :],
                    out_ref.at[pl.ds(first, chip_rows), pl.ds(j * columns, columns)],
                    sems.at[j, i],
                )
            )
            copies[-1].start()

    def early_value(i, at):
        base, k = early[i]
        return base[k * chip_rows : (k + 1) * chip_rows, at]

    begun, rest = range(len(early)), range(len(early), n)
    tile = None
    for j in range(tiles + 1):
        done, tile = tile, multiply(held, [weight], slice(j * columns, (j + 1) * columns)) if j < tiles else None
        if j < tiles:
            put(j, begun, early_value)
        if done is not None:
            at = slice((j - 1) * columns, j * columns)
            own_far = done[chip_rows : chip_rows + far * rows]
            interleave(rows, far, own_far, far_base[:, at], far_rows, slice(0, columns))

            def rest_value(i, at, done=done):
                k = i - len(early)
                return far_rows[k * chip_rows : (k + 1) * chip_rows, :] if k < far else done[:chip_rows]

            put(j - 1, rest, rest_value)
        if j < tiles:
            send(j, begun)
        if done is not None:
            send(j - 1, rest)
    for copy in copies:
        copy.wait()


def finish(n, rows, groups, lookups, bases, late, weight, sums, up):
    (rank, width), depth = up.shape[1:], weight.shape[0]
    total, columns = 2 * n * rows, tile_width(width)
    arrays = [*bases, *late, weight, *sums, up]
    far = len(groups[2])
    held = full_rows((2 + far) * rows)
    return pl.pallas_call(
        functools.partial(finish_kernel, n, rows, groups),
        out_shape=jax.ShapeDtypeStruct((total, width), jnp.bfloat16),
        in_specs=whole(len(arrays)) + [pl.BlockSpec(memory_space=pl.ANY)] * len(lookups),
        out_specs=pl.BlockSpec(memory_space=pl.ANY),
        scratch_shapes=[
            pltpu.VMEM((held, depth), jnp.bfloat16),
            pltpu.VMEM((n, 2 * rows, rank), jnp.bfloat16),
            pltpu.VMEM((2 * far * rows, columns), jnp.float32),
            pltpu.VMEM((width // columns, total, columns), jnp.bfloat16),
            *(pltpu.SMEM(x.shape, x.dtype) for x in lookups),
            pltpu.SemaphoreType.DMA((width // columns, n)),
            pltpu.SemaphoreType.DMA((len(lookups),)),
        ],
        compiler_params=pltpu.CompilerParams(vmem_limit_bytes=10 << 20),
        cost_estimate=pl.CostEstimate(
            flops=2 * held * depth * width, bytes_accessed=2 * total * width, transcendentals=0
        ),
    )(*in_vmem(arrays), *lookups)


def on_device(n, tokens, weight, down, up, adapter_per_block, rows_per_block):
    rows, features = tokens.shape
    depth = features // CHUNKS
    held, width, rank = down.shape
    last = n // 2
    adapters = adapter_per_block[:, 0]
    window = Window(n, width, depth)
    near, mid, far = ([d for hop in hops for d in hop_distances(hop, n)] for hops in ((0, 1), range(2, last - 1), [last - 1]))
    half = (n // 2 * rows, 2 * rank)
    sums = [(half, jnp.float32), (half, jnp.bfloat16)]

    (behind,), (ahead,) = ring_hop([tokens], [tokens], n)
    ends = far + [last]
    bf16 = jnp.bfloat16
    factor, *sends = prepare(
        functools.partial(prepare_kernel, n, window, ends),
        [tokens, jnp.swapaxes(down, 1, 2)],
        [weight, up],
        [((held, rank, window.size), bf16)] + [((rows, window.size), bf16)] * len(ends),
        [
            pltpu.VMEM((held, rank, width), down.dtype),
            pltpu.SemaphoreType.DMA((1 + len(ends),)),
        ],
    )
    received = [lax.ppermute(x, AXES, ring_perm(n, d)) for d, x in zip(ends, sends)]
    come_from = [-d for d in far] + [last]
    piece = ((rows, depth), bf16)
    near_rows, *chunks = call(
        near_kernel,
        [tokens, behind, ahead, factor],
        received,
        [((len(near) * CHUNKS * rows + rank, depth), bf16)] + [piece] * (2 * CHUNKS),
    )

    up_way, down_way = chunks[:CHUNKS], chunks[CHUNKS:]
    near_swapped = swap_cores(near_rows, n)
    own = len(near) * rows
    (mine,) = product(functools.partial(core_kernel, rows), [near_rows], weight, [], own, [own])
    (up,) = call(cast_kernel, [up], [mine], [(up.shape, bf16)])
    arrived = []
    for _ in range(2, last - 1):
        up_way, down_way = ring_hop(up_way, down_way, n)
        arrived += up_way + down_way
    (mid_rows,) = join(arrived, [mine, up])

    total, rounded = call(
        functools.partial(partial_kernel, n, window, [near, mid], come_from),
        [near_rows, mid_rows, *received, factor, near_swapped],
        [],
        sums,
        [
            pltpu.SMEM(adapters.shape, jnp.int32),
            pltpu.VMEM((n * rows, window.size), bf16),
            pltpu.VMEM((2 * held, n * rows, rank), jnp.float32),
            pltpu.VMEM((n, rows, rank), jnp.float32),
            pltpu.SemaphoreType.DMA,
        ],
        outside=[adapters],
    )
    near_base, mine = product(
        functools.partial(near_base_kernel, rows, len(near), len(mid)),
        [near_swapped, mine, mid_rows],
        weight,
        [rounded],
        own + len(mid) * rows,
        [2 * own, len(mid) * rows],
    )
    total, rounded = call(add_kernel, [total, lax.ppermute(rounded, AXES, y_perm(n))], [], sums)
    up_way, down_way = ring_hop(up_way, down_way, n)
    late_rows, turned = join([mid_rows, *up_way, *down_way], [rounded, near_base], 1)

    late_swapped = swap_cores(late_rows, n)
    total, rounded = call(
        add_kernel,
        [total] + [lax.ppermute(rounded, AXES, z_perm(n, shift)) for shift in range(1, n // 2)],
        [],
        sums,
    )
    (last_rows,) = join([lax.ppermute(turned, AXES, ring_perm(n, 1, -1))], [rounded])
    last_pair = (last_rows, swap_cores(last_rows, n))

    late = len(mid) + len(far)
    mid_base, far_base = product(
        functools.partial(late_base_kernel, rows, len(mid), len(far)),
        [late_swapped, mine],
        weight,
        [last_rows],
        late * rows,
        [2 * len(mid) * rows, len(far) * rows],
    )
    return finish(
        n,
        rows,
        [near, mid, far, [last]],
        [adapters, rows_per_block],
        [near_base, mid_base, far_base],
        [late_rows, *last_pair],
        weight,
        [total, swap_cores(rounded, n)],
        up,
    )


def solution(mesh):
    placed = (
        P(("groups", "seq", "adapter"), None),
        P(None, ("seq", "adapter")),
        P(("groups", "adapter"), "seq", None),
        P("groups", None, ("seq", "adapter")),
        P("groups", None),
        P("groups"),
    )
    return jax.shard_map(
        functools.partial(on_device, mesh.shape["seq"]),
        mesh=mesh,
        in_specs=placed,
        out_specs=P("groups", ("seq", "adapter")),
        check_vma=False,
    )
```

```python
import functools

import jax
import jax.numpy as jnp
from jax import lax
from jax.experimental import pallas as pl
from jax.experimental.pallas import tpu as pltpu
from jax.sharding import PartitionSpec as P

BLOCK = 128
AXES = ("seq", "adapter")
CHUNKS = 2


def ring_perm(n, way, other_way=None):
    order = [2 * z for z in range(n // 2)] + [2 * z + 1 for z in reversed(range(n // 2))]
    ways = (way, way if other_way is None else other_way)
    return [(2 * s + c, 2 * order[(pos + ways[c]) % n] + c) for pos, s in enumerate(order) for c in range(2)]


def swap_cores(x, n):
    return lax.ppermute(x, AXES, [(2 * s + c, 2 * s + 1 - c) for s in range(n) for c in range(2)])


def chip_at(distance, n):
    s = lax.axis_index("seq")
    z = s >> 1
    pos = jnp.where(s & 1 == 0, z, n - 1 - z) + distance
    pos = jnp.where(pos >= n, pos - n, pos)
    pos = jnp.where(pos < 0, pos + n, pos)
    return jnp.where(pos < n // 2, 2 * pos, 2 * (n - 1 - pos) + 1)


def y_perm(n):
    return [(2 * s + c, 2 * (s ^ 1) + c) for s in range(n) for c in range(2)]


def z_perm(n, shift):
    nz = n // 2
    return [
        (2 * (2 * z + y) + c, 2 * (2 * ((z - shift) % nz) + y) + c)
        for z in range(nz)
        for y in range(2)
        for c in range(2)
    ]


def hop_distances(hop, n):
    if hop == 0:
        return [0]
    return [-hop, hop] if hop < n // 2 else [hop]


def ring_hop(up, down, n):
    return [lax.ppermute(x, AXES, ring_perm(n, 1)) for x in up], [lax.ppermute(x, AXES, ring_perm(n, -1)) for x in down]


def join_kernel(ways, *refs):
    count = len(refs) - 1 - ways
    pieces, out, on = refs[:count], refs[count], refs[count + 1 :]
    first = 0
    for piece in pieces:
        out[first : first + piece.shape[0], :] = piece[...]
        first += piece.shape[0]
    arrived = pieces[len(pieces) - 2 * CHUNKS :]
    if ways == 1:
        c = lax.axis_index("adapter")
        rows = arrived[0].shape[0]
        for core in range(2):

            @pl.when(c == core)
            def _():
                for i, piece in enumerate(arrived[core * CHUNKS : (core + 1) * CHUNKS]):
                    on[0][i * rows : (i + 1) * rows, :] = piece[...]


def join(pieces, after, ways=0):
    (rows, depth), dtype = pieces[-1].shape, pieces[-1].dtype
    on = [CHUNKS * rows] * ways
    outs = [((count, depth), dtype) for count in [sum(x.shape[0] for x in pieces), *on]]
    return call(functools.partial(join_kernel, ways), pieces, after, outs)


def whole(count):
    return [pl.BlockSpec(memory_space=pltpu.VMEM)] * count


def in_vmem(arrays):
    return [pltpu.with_memory_space_constraint(x, pltpu.VMEM) for x in arrays]


def call(kernel, arrays, after, outs, scratch=(), limit=8, flops=0, outside=()):
    operands = len(arrays) + len(outside)

    def body(*refs):
        kernel(*refs[:operands], *refs[operands + len(after) :])

    return pl.pallas_call(
        body,
        out_shape=[pltpu.VMEM(shape, dtype) for shape, dtype in outs],
        in_specs=whole(len(arrays)) + [pl.BlockSpec(memory_space=pl.ANY)] * (len(outside) + len(after)),
        out_specs=whole(len(outs)),
        scratch_shapes=list(scratch),
        compiler_params=pltpu.CompilerParams(vmem_limit_bytes=limit << 20),
        cost_estimate=pl.CostEstimate(flops=flops, bytes_accessed=0, transcendentals=0),
    )(*in_vmem(arrays), *outside, *after)


class Window:
    def __init__(self, n, width, depth):
        self.width, self.depth = width, depth
        self.size = -(-(width + max(s * width % 128 for s in range(n))) // 128) * 128
        for s in range(n):
            start = s * width // 128 * 128
            assert start // depth == (start + self.size - 1) // depth

    def start(self, chip):
        return (chip * self.width) >> 7 << 7

    def shift(self, chip):
        return chip * self.width - self.start(chip)


def near_kernel(tokens, behind, ahead, factor, out, *chunks):
    held, rank, size = factor.shape
    rows, depth = chunks[0].shape
    for i, ref in enumerate((tokens, behind, ahead)):
        for k in range(CHUNKS):
            piece = ref[:, k * depth : (k + 1) * depth]
            at = (i * CHUNKS + k) * rows
            out[at : at + rows, :] = piece
            if i:
                chunks[(i - 1) * CHUNKS + k][...] = piece
    first = 3 * CHUNKS * rows
    out[first:, :] = jnp.zeros((rank, depth), out.dtype)
    for index in range(held):
        out[first:, index * size : (index + 1) * size] = factor[index]


def pack(parts, out):
    chips, rows, rank = parts.shape
    for t in range(chips):
        i, k = t % (chips // 2), t // (chips // 2)
        out[i * rows : (i + 1) * rows, k * rank : (k + 1) * rank] = parts[t].astype(out.dtype)


def partial_kernel(n, window, groups, far, *refs):
    *pieces, factor, other, adapters_ref, total, rounded, adapters, x, products, parts, sem = refs
    lookup = pltpu.make_async_copy(adapters_ref, adapters, sem)
    lookup.start()
    pieces, received = pieces[: len(groups)], pieces[len(groups) :]
    s, c = lax.axis_index("seq"), lax.axis_index("adapter")
    rows, size = received[0].shape
    held, rank, _ = factor.shape
    start = window.start(s)
    chunk = jnp.where(start >= window.depth, 1, 0)
    inside = pl.multiple_of(start - chunk * window.depth, 128)
    order = []
    for piece, distances in zip(pieces, groups):
        for i, distance in enumerate(distances):
            row = pl.multiple_of((i * CHUNKS + chunk) * rows, rows)
            x[len(order) * rows : (len(order) + 1) * rows, :] = piece[pl.ds(row, rows), pl.ds(inside, size)]
            order.append(distance)
    for piece, distance in zip(received, far):
        x[len(order) * rows : (len(order) + 1) * rows, :] = piece[...]
        order.append(distance)
    below = other.shape[0] - rank
    for index in range(held):
        theirs = other[below:, index * size : (index + 1) * size]
        for core, weights in ((c, factor[index]), (1 - c, theirs)):
            products[core * held + index] = lax.dot_general(
                x[...], weights, (((1,), (1,)), ((), ())), preferred_element_type=jnp.float32
            )
    lookup.wait()
    for i, distance in enumerate(order):
        chip = chip_at(distance, n)
        parts[chip] = products[adapters[chip * 2 * rows // BLOCK], i * rows : (i + 1) * rows, :]
    pack(parts, total)
    rounded[...] = total[...].astype(jnp.bfloat16)


def add_kernel(total, *refs):
    *received, out, rounded = refs
    value = total[...]
    for x in received:
        value += x[...].astype(jnp.float32)
    out[...] = value
    rounded[...] = value.astype(jnp.bfloat16)


def prepare_kernel(n, window, distances, tokens, down_ref, factor, *refs):
    *sends, down, sems = refs
    copies = [pltpu.make_async_copy(down_ref, down, sems.at[0])]
    for k, (distance, send) in enumerate(zip(distances, sends)):
        start = pl.multiple_of(window.start(chip_at(distance, n)), 128)
        copies.append(pltpu.make_async_copy(tokens.at[:, pl.ds(start, window.size)], send, sems.at[1 + k]))
    for copy in copies:
        copy.start()
    copies[0].wait()
    zeros = jnp.zeros((down.shape[1], window.size - window.width), jnp.float32)
    for index in range(down.shape[0]):
        wide = jnp.concatenate([down[index], zeros], 1)
        factor[index] = pltpu.roll(wide, window.shift(lax.axis_index("seq")), 1).astype(jnp.bfloat16)
    for copy in copies[1:]:
        copy.wait()


def full_rows(rows):
    return max(rows, 128)


def assemble_core(ref, chips, rows, held, skip=0, first=0):
    depth = ref.shape[1]
    for i in range(chips):
        for k in range(CHUNKS):
            at = ((skip + i) * CHUNKS + k) * rows
            held[first + i * rows : first + (i + 1) * rows, k * depth : (k + 1) * depth] = ref[at : at + rows, :]


def interleave(rows, chips, mine, others, base, at):
    c = lax.axis_index("adapter")
    for i in range(chips):
        here = slice(i * rows, (i + 1) * rows)
        for core, value in ((c, mine[here]), (1 - c, others[here])):
            base[pl.ds(pl.multiple_of((2 * i + core) * rows, rows), rows), at] = value


def core_kernel(rows, ref, *refs):
    *weights, base, held = refs
    assemble_core(ref, base.shape[0] // rows, rows, held)
    columns = tile_width(base.shape[1])
    for j in range(0, base.shape[1], columns):
        at = slice(j, j + columns)
        base[:, at] = multiply(held, weights, at)[: base.shape[0]]


def near_base_kernel(rows, near, mid, swapped, mine, mid_rows, weight, base, mid_base, held):
    assemble_core(swapped, near, rows, held)
    assemble_core(mid_rows, mid, rows, held, 0, near * rows)
    columns = tile_width(base.shape[1])
    for j in range(0, base.shape[1], columns):
        at = slice(j, j + columns)
        tile = multiply(held, [weight], at)
        interleave(rows, near, mine[: near * rows, at], tile, base, at)
        mid_base[:, at] = tile[near * rows : (near + mid) * rows]


def late_base_kernel(rows, mid, far, swapped, mine, weight, base, far_base, held):
    assemble_core(swapped, mid + far, rows, held)
    columns = tile_width(base.shape[1])
    for j in range(0, base.shape[1], columns):
        at = slice(j, j + columns)
        tile = multiply(held, [weight], at)
        interleave(rows, mid, mine[:, at], tile, base, at)
        far_base[:, at] = tile[mid * rows : (mid + far) * rows]


def product(kernel, arrays, weight, after, total, outs):
    (depth, width), total = weight.shape, full_rows(total)
    return call(
        kernel,
        [*arrays, weight],
        after,
        [((rows, width), jnp.float32) for rows in outs],
        [pltpu.VMEM((total, depth), jnp.bfloat16)],
        limit=8 + (2 * total * depth >> 20),
        flops=2 * total * depth * width,
    )


def cast_kernel(source, out):
    out[...] = source[...].astype(out.dtype)


def in_hbm(arrays):
    return [pltpu.with_memory_space_constraint(x, pltpu.HBM) for x in arrays]


def prepare(kernel, arrays, later, outs, scratch):
    operands = len(arrays)

    def body(*refs):
        kernel(*refs[:operands], *refs[operands + len(later) :])

    return pl.pallas_call(
        body,
        out_shape=[pltpu.VMEM(shape, dtype) for shape, dtype in outs],
        in_specs=[pl.BlockSpec(memory_space=pltpu.HBM)] * (operands + len(later)),
        out_specs=whole(len(outs)),
        scratch_shapes=scratch,
        compiler_params=pltpu.CompilerParams(vmem_limit_bytes=8 << 20),
        cost_estimate=pl.CostEstimate(flops=0, bytes_accessed=0, transcendentals=0),
    )(*in_hbm(arrays), *in_hbm(later))


def assemble(pairs, counts, rows, held):
    c = lax.axis_index("adapter")
    first = 0
    for pair, chips in zip(pairs, counts):
        depth = pair[0].shape[1]
        for chip in range(chips):
            for k in range(CHUNKS):
                at = (chip * CHUNKS + k) * rows
                for ref, core in zip(pair, (c, 1 - c)):
                    row = pl.multiple_of(first + core * rows, rows)
                    held[pl.ds(row, rows), k * depth : (k + 1) * depth] = ref[at : at + rows, :]
            first += 2 * rows


def tile_width(width):
    return 768 if width % 768 == 0 else width


def multiply(held, weights, at):
    total, first = 0.0, 0
    for w in weights:
        columns = held[:, first : first + w.shape[0]]
        total += jnp.dot(columns, w[:, at], preferred_element_type=jnp.float32)
        first += w.shape[0]
    return total


def finish_kernel(n, rows, groups, *refs):
    near_base, mid_base, far_base, late_rows, mine, others, weight, own, other, up_ref = refs[:10]
    adapters_ref, live_ref, out_ref, held, shrink, far_rows, block, adapters, live, sems, small_sems = refs[10:]
    lookups = [
        pltpu.make_async_copy(source, to, small_sems.at[k])
        for k, (source, to) in enumerate(((adapters_ref, adapters), (live_ref, live)))
    ]
    for lookup in lookups:
        lookup.start()
    c = lax.axis_index("adapter")
    chip_rows, rank = 2 * rows, up_ref.shape[1]
    tiles, _, columns = block.shape
    _, mid, far, _ = (len(group) for group in groups)
    assemble([(mine, others)], [1], rows, held)
    assemble_core(late_rows, far, rows, held, mid, chip_rows)
    for t in range(n):
        i, k = t % (n // 2), t // (n // 2)
        for ref, core in ((own, c), (other, 1 - c)):
            part = ref[i * rows : (i + 1) * rows, k * rank : (k + 1) * rank]
            shrink[t, pl.ds(pl.multiple_of(core * rows, rows), rows), :] = part.astype(jnp.bfloat16)
    for lookup in lookups:
        lookup.wait()
    early = [(base, i) for base, group in ((near_base, groups[0]), (mid_base, groups[1])) for i in range(len(group))]
    sources = [distance for group in groups for distance in group]
    copies = []

    def put(j, which, value_of):
        at = slice(j * columns, (j + 1) * columns)
        for i in which:
            first = chip_at(sources[i], n) * chip_rows
            of_block = first // BLOCK
            delta = jnp.dot(
                shrink[chip_at(sources[i], n)],
                up_ref[adapters[of_block], :, at],
                preferred_element_type=jnp.float32,
            )
            index = lax.broadcasted_iota(jnp.int32, delta.shape, 0) + (first - of_block * BLOCK)
            value = jnp.where(index < live[of_block], value_of(i, at) + delta, 0.0)
            block[j, i * chip_rows : (i + 1) * chip_rows, :] = value.astype(out_ref.dtype)

    def send(j, which):
        for i in which:
            first = pl.multiple_of(chip_at(sources[i], n) * chip_rows, chip_rows)
            copies.append(
                pltpu.make_async_copy(
                    block.at[j, pl.ds(i * chip_rows, chip_rows), :],
                    out_ref.at[pl.ds(first, chip_rows), pl.ds(j * columns, columns)],
                    sems.at[j, i],
                )
            )
            copies[-1].start()

    def early_value(i, at):
        base, k = early[i]
        return base[k * chip_rows : (k + 1) * chip_rows, at]

    begun, rest = range(len(early)), range(len(early), n)
    tile = None
    for j in range(tiles + 1):
        done, tile = tile, multiply(held, [weight], slice(j * columns, (j + 1) * columns)) if j < tiles else None
        if j < tiles:
            put(j, begun, early_value)
        if done is not None:
            at = slice((j - 1) * columns, j * columns)
            own_far = done[chip_rows : chip_rows + far * rows]
            interleave(rows, far, own_far, far_base[:, at], far_rows, slice(0, columns))

            def rest_value(i, at, done=done):
                k = i - len(early)
                return far_rows[k * chip_rows : (k + 1) * chip_rows, :] if k < far else done[:chip_rows]

            put(j - 1, rest, rest_value)
        if j < tiles:
            send(j, begun)
        if done is not None:
            send(j - 1, rest)
    for copy in copies:
        copy.wait()


def finish(n, rows, groups, lookups, bases, late, weight, sums, up):
    (rank, width), depth = up.shape[1:], weight.shape[0]
    total, columns = 2 * n * rows, tile_width(width)
    arrays = [*bases, *late, weight, *sums, up]
    far = len(groups[2])
    held = full_rows((2 + far) * rows)
    return pl.pallas_call(
        functools.partial(finish_kernel, n, rows, groups),
        out_shape=jax.ShapeDtypeStruct((total, width), jnp.bfloat16),
        in_specs=whole(len(arrays)) + [pl.BlockSpec(memory_space=pl.ANY)] * len(lookups),
        out_specs=pl.BlockSpec(memory_space=pl.ANY),
        scratch_shapes=[
            pltpu.VMEM((held, depth), jnp.bfloat16),
            pltpu.VMEM((n, 2 * rows, rank), jnp.bfloat16),
            pltpu.VMEM((2 * far * rows, columns), jnp.float32),
            pltpu.VMEM((width // columns, total, columns), jnp.bfloat16),
            *(pltpu.SMEM(x.shape, x.dtype) for x in lookups),
            pltpu.SemaphoreType.DMA((width // columns, n)),
            pltpu.SemaphoreType.DMA((len(lookups),)),
        ],
        compiler_params=pltpu.CompilerParams(vmem_limit_bytes=10 << 20),
        cost_estimate=pl.CostEstimate(
            flops=2 * held * depth * width, bytes_accessed=2 * total * width, transcendentals=0
        ),
    )(*in_vmem(arrays), *lookups)


def on_device(n, tokens, weight, down, up, adapter_per_block, rows_per_block):
    rows, features = tokens.shape
    depth = features // CHUNKS
    held, width, rank = down.shape
    last = n // 2
    adapters = adapter_per_block[:, 0]
    window = Window(n, width, depth)
    near, mid, far = ([d for hop in hops for d in hop_distances(hop, n)] for hops in ((0, 1), range(2, last - 1), [last - 1]))
    half = (n // 2 * rows, 2 * rank)
    sums = [(half, jnp.float32), (half, jnp.bfloat16)]

    (behind,), (ahead,) = ring_hop([tokens], [tokens], n)
    ends = far + [last]
    bf16 = jnp.bfloat16
    factor, *sends = prepare(
        functools.partial(prepare_kernel, n, window, ends),
        [tokens, jnp.swapaxes(down, 1, 2)],
        [weight, up],
        [((held, rank, window.size), bf16)] + [((rows, window.size), bf16)] * len(ends),
        [
            pltpu.VMEM((held, rank, width), down.dtype),
            pltpu.SemaphoreType.DMA((1 + len(ends),)),
        ],
    )
    received = [lax.ppermute(x, AXES, ring_perm(n, d)) for d, x in zip(ends, sends)]
    come_from = [-d for d in far] + [last]
    piece = ((rows, depth), bf16)
    near_rows, *chunks = call(
        near_kernel,
        [tokens, behind, ahead, factor],
        received,
        [((len(near) * CHUNKS * rows + rank, depth), bf16)] + [piece] * (2 * CHUNKS),
    )

    up_way, down_way = chunks[:CHUNKS], chunks[CHUNKS:]
    near_swapped = swap_cores(near_rows, n)
    own = len(near) * rows
    (mine,) = product(functools.partial(core_kernel, rows), [near_rows], weight, [], own, [own])
    (up,) = call(cast_kernel, [up], [mine], [(up.shape, bf16)])
    arrived = []
    for _ in range(2, last - 1):
        up_way, down_way = ring_hop(up_way, down_way, n)
        arrived += up_way + down_way
    (mid_rows,) = join(arrived, [mine, up])

    total, rounded = call(
        functools.partial(partial_kernel, n, window, [near, mid], come_from),
        [near_rows, mid_rows, *received, factor, near_swapped],
        [],
        sums,
        [
            pltpu.SMEM(adapters.shape, jnp.int32),
            pltpu.VMEM((n * rows, window.size), bf16),
            pltpu.VMEM((2 * held, n * rows, rank), jnp.float32),
            pltpu.VMEM((n, rows, rank), jnp.float32),
            pltpu.SemaphoreType.DMA,
        ],
        outside=[adapters],
    )
    near_base, mine = product(
        functools.partial(near_base_kernel, rows, len(near), len(mid)),
        [near_swapped, mine, mid_rows],
        weight,
        [rounded],
        own + len(mid) * rows,
        [2 * own, len(mid) * rows],
    )
    total, rounded = call(add_kernel, [total, lax.ppermute(rounded, AXES, y_perm(n))], [], sums)
    up_way, down_way = ring_hop(up_way, down_way, n)
    late_rows, turned = join([mid_rows, *up_way, *down_way], [rounded, near_base], 1)

    late_swapped = swap_cores(late_rows, n)
    late = len(mid) + len(far)
    mid_base, far_base = product(
        functools.partial(late_base_kernel, rows, len(mid), len(far)),
        [late_swapped, mine],
        weight,
        [],
        late * rows,
        [2 * len(mid) * rows, len(far) * rows],
    )
    total, rounded = call(
        add_kernel,
        [total] + [lax.ppermute(rounded, AXES, z_perm(n, shift)) for shift in range(1, n // 2)],
        [mid_base],
        sums,
    )
    (last_rows,) = join([lax.ppermute(turned, AXES, ring_perm(n, 1, -1))], [rounded])
    last_pair = (last_rows, swap_cores(last_rows, n))

    return finish(
        n,
        rows,
        [near, mid, far, [last]],
        [adapters, rows_per_block],
        [near_base, mid_base, far_base],
        [late_rows, *last_pair],
        weight,
        [total, swap_cores(rounded, n)],
        up,
    )


def solution(mesh):
    placed = (
        P(("groups", "seq", "adapter"), None),
        P(None, ("seq", "adapter")),
        P(("groups", "adapter"), "seq", None),
        P("groups", None, ("seq", "adapter")),
        P("groups", None),
        P("groups"),
    )
    return jax.shard_map(
        functools.partial(on_device, mesh.shape["seq"]),
        mesh=mesh,
        in_specs=placed,
        out_specs=P("groups", ("seq", "adapter")),
        check_vma=False,
    )
```

```python
import functools

import jax
import jax.numpy as jnp
from jax import lax
from jax.experimental import pallas as pl
from jax.experimental.pallas import tpu as pltpu
from jax.sharding import PartitionSpec as P

BLOCK = 128
AXES = ("seq", "adapter")
CHUNKS = 2


def ring_perm(n, way, other_way=None):
    order = [2 * z for z in range(n // 2)] + [2 * z + 1 for z in reversed(range(n // 2))]
    ways = (way, way if other_way is None else other_way)
    return [(2 * s + c, 2 * order[(pos + ways[c]) % n] + c) for pos, s in enumerate(order) for c in range(2)]


def swap_cores(x, n):
    return lax.ppermute(x, AXES, [(2 * s + c, 2 * s + 1 - c) for s in range(n) for c in range(2)])


def chip_at(distance, n):
    s = lax.axis_index("seq")
    z = s >> 1
    pos = jnp.where(s & 1 == 0, z, n - 1 - z) + distance
    pos = jnp.where(pos >= n, pos - n, pos)
    pos = jnp.where(pos < 0, pos + n, pos)
    return jnp.where(pos < n // 2, 2 * pos, 2 * (n - 1 - pos) + 1)


def y_perm(n):
    return [(2 * s + c, 2 * (s ^ 1) + c) for s in range(n) for c in range(2)]


def z_perm(n, shift):
    nz = n // 2
    return [
        (2 * (2 * z + y) + c, 2 * (2 * ((z - shift) % nz) + y) + c)
        for z in range(nz)
        for y in range(2)
        for c in range(2)
    ]


def hop_distances(hop, n):
    if hop == 0:
        return [0]
    return [-hop, hop] if hop < n // 2 else [hop]


def ring_hop(up, down, n):
    return [lax.ppermute(x, AXES, ring_perm(n, 1)) for x in up], [lax.ppermute(x, AXES, ring_perm(n, -1)) for x in down]


def join_kernel(ways, *refs):
    count = len(refs) - 1 - ways
    pieces, out, on = refs[:count], refs[count], refs[count + 1 :]
    first = 0
    for piece in pieces:
        out[first : first + piece.shape[0], :] = piece[...]
        first += piece.shape[0]
    arrived = pieces[len(pieces) - 2 * CHUNKS :]
    if ways == 1:
        c = lax.axis_index("adapter")
        rows = arrived[0].shape[0]
        for core in range(2):

            @pl.when(c == core)
            def _():
                for i, piece in enumerate(arrived[core * CHUNKS : (core + 1) * CHUNKS]):
                    on[0][i * rows : (i + 1) * rows, :] = piece[...]


def join(pieces, after, ways=0):
    (rows, depth), dtype = pieces[-1].shape, pieces[-1].dtype
    on = [CHUNKS * rows] * ways
    outs = [((count, depth), dtype) for count in [sum(x.shape[0] for x in pieces), *on]]
    return call(functools.partial(join_kernel, ways), pieces, after, outs)


def whole(count):
    return [pl.BlockSpec(memory_space=pltpu.VMEM)] * count


def in_vmem(arrays):
    return [pltpu.with_memory_space_constraint(x, pltpu.VMEM) for x in arrays]


def call(kernel, arrays, after, outs, scratch=(), limit=8, flops=0, outside=()):
    operands = len(arrays) + len(outside)

    def body(*refs):
        kernel(*refs[:operands], *refs[operands + len(after) :])

    return pl.pallas_call(
        body,
        out_shape=[pltpu.VMEM(shape, dtype) for shape, dtype in outs],
        in_specs=whole(len(arrays)) + [pl.BlockSpec(memory_space=pl.ANY)] * (len(outside) + len(after)),
        out_specs=whole(len(outs)),
        scratch_shapes=list(scratch),
        compiler_params=pltpu.CompilerParams(vmem_limit_bytes=limit << 20),
        cost_estimate=pl.CostEstimate(flops=flops, bytes_accessed=0, transcendentals=0),
    )(*in_vmem(arrays), *outside, *after)


class Window:
    def __init__(self, n, width, depth):
        self.width, self.depth = width, depth
        self.size = -(-(width + max(s * width % 128 for s in range(n))) // 128) * 128
        for s in range(n):
            start = s * width // 128 * 128
            assert start // depth == (start + self.size - 1) // depth

    def start(self, chip):
        return (chip * self.width) >> 7 << 7

    def shift(self, chip):
        return chip * self.width - self.start(chip)


def near_kernel(tokens, behind, ahead, factor, out, *chunks):
    held, rank, size = factor.shape
    rows, depth = chunks[0].shape
    for i, ref in enumerate((tokens, behind, ahead)):
        for k in range(CHUNKS):
            piece = ref[:, k * depth : (k + 1) * depth]
            at = (i * CHUNKS + k) * rows
            out[at : at + rows, :] = piece
            if i:
                chunks[(i - 1) * CHUNKS + k][...] = piece
    first = 3 * CHUNKS * rows
    out[first:, :] = jnp.zeros((rank, depth), out.dtype)
    for index in range(held):
        out[first:, index * size : (index + 1) * size] = factor[index]


def pack(parts, out):
    chips, rows, rank = parts.shape
    for t in range(chips):
        i, k = t % (chips // 2), t // (chips // 2)
        out[i * rows : (i + 1) * rows, k * rank : (k + 1) * rank] = parts[t].astype(out.dtype)


def partial_kernel(n, window, groups, far, *refs):
    *pieces, factor, other, adapters_ref, total, rounded, adapters, x, products, parts, sem = refs
    lookup = pltpu.make_async_copy(adapters_ref, adapters, sem)
    lookup.start()
    pieces, received = pieces[: len(groups)], pieces[len(groups) :]
    s, c = lax.axis_index("seq"), lax.axis_index("adapter")
    rows, size = received[0].shape
    held, rank, _ = factor.shape
    start = window.start(s)
    chunk = jnp.where(start >= window.depth, 1, 0)
    inside = pl.multiple_of(start - chunk * window.depth, 128)
    order = []
    for piece, distances in zip(pieces, groups):
        for i, distance in enumerate(distances):
            row = pl.multiple_of((i * CHUNKS + chunk) * rows, rows)
            x[len(order) * rows : (len(order) + 1) * rows, :] = piece[pl.ds(row, rows), pl.ds(inside, size)]
            order.append(distance)
    for piece, distance in zip(received, far):
        x[len(order) * rows : (len(order) + 1) * rows, :] = piece[...]
        order.append(distance)
    below = other.shape[0] - rank
    for index in range(held):
        theirs = other[below:, index * size : (index + 1) * size]
        for core, weights in ((c, factor[index]), (1 - c, theirs)):
            products[core * held + index] = lax.dot_general(
                x[...], weights, (((1,), (1,)), ((), ())), preferred_element_type=jnp.float32
            )
    lookup.wait()
    for i, distance in enumerate(order):
        chip = chip_at(distance, n)
        parts[chip] = products[adapters[chip * 2 * rows // BLOCK], i * rows : (i + 1) * rows, :]
    pack(parts, total)
    rounded[...] = total[...].astype(jnp.bfloat16)


def add_kernel(total, *refs):
    *received, out, rounded = refs
    value = total[...]
    for x in received:
        value += x[...].astype(jnp.float32)
    out[...] = value
    rounded[...] = value.astype(jnp.bfloat16)


def prepare_kernel(n, window, distances, tokens, down_ref, factor, *refs):
    *sends, down, sems = refs
    copies = [pltpu.make_async_copy(down_ref, down, sems.at[0])]
    for k, (distance, send) in enumerate(zip(distances, sends)):
        start = pl.multiple_of(window.start(chip_at(distance, n)), 128)
        copies.append(pltpu.make_async_copy(tokens.at[:, pl.ds(start, window.size)], send, sems.at[1 + k]))
    for copy in copies:
        copy.start()
    copies[0].wait()
    zeros = jnp.zeros((down.shape[1], window.size - window.width), jnp.float32)
    for index in range(down.shape[0]):
        wide = jnp.concatenate([down[index], zeros], 1)
        factor[index] = pltpu.roll(wide, window.shift(lax.axis_index("seq")), 1).astype(jnp.bfloat16)
    for copy in copies[1:]:
        copy.wait()


def full_rows(rows):
    return max(rows, 128)


def assemble_core(ref, chips, rows, held, skip=0, first=0):
    depth = ref.shape[1]
    for i in range(chips):
        for k in range(CHUNKS):
            at = ((skip + i) * CHUNKS + k) * rows
            held[first + i * rows : first + (i + 1) * rows, k * depth : (k + 1) * depth] = ref[at : at + rows, :]


def interleave(rows, chips, mine, others, base, at):
    c = lax.axis_index("adapter")
    for i in range(chips):
        here = slice(i * rows, (i + 1) * rows)
        for core, value in ((c, mine[here]), (1 - c, others[here])):
            base[pl.ds(pl.multiple_of((2 * i + core) * rows, rows), rows), at] = value


def core_kernel(rows, ref, *refs):
    *weights, base, held = refs
    assemble_core(ref, base.shape[0] // rows, rows, held)
    columns = tile_width(base.shape[1])
    for j in range(0, base.shape[1], columns):
        at = slice(j, j + columns)
        base[:, at] = multiply(held, weights, at)[: base.shape[0]]


def near_base_kernel(rows, near, mid, swapped, mine, mid_rows, weight, base, mid_base, held):
    assemble_core(swapped, near, rows, held)
    assemble_core(mid_rows, mid, rows, held, 0, near * rows)
    columns = tile_width(base.shape[1])
    for j in range(0, base.shape[1], columns):
        at = slice(j, j + columns)
        tile = multiply(held, [weight], at)
        interleave(rows, near, mine[: near * rows, at], tile, base, at)
        mid_base[:, at] = tile[near * rows : (near + mid) * rows]


def late_base_kernel(rows, mid, far, swapped, mine, weight, base, far_base, held):
    assemble_core(swapped, mid + far, rows, held)
    columns = tile_width(base.shape[1])
    for j in range(0, base.shape[1], columns):
        at = slice(j, j + columns)
        tile = multiply(held, [weight], at)
        interleave(rows, mid, mine[:, at], tile, base, at)
        far_base[:, at] = tile[mid * rows : (mid + far) * rows]


def product(kernel, arrays, weight, after, total, outs):
    (depth, width), total = weight.shape, full_rows(total)
    return call(
        kernel,
        [*arrays, weight],
        after,
        [((rows, width), jnp.float32) for rows in outs],
        [pltpu.VMEM((total, depth), jnp.bfloat16)],
        limit=8 + (2 * total * depth >> 20),
        flops=2 * total * depth * width,
    )


def cast_kernel(source, out):
    out[...] = source[...].astype(out.dtype)


def in_hbm(arrays):
    return [pltpu.with_memory_space_constraint(x, pltpu.HBM) for x in arrays]


def prepare(kernel, arrays, later, outs, scratch):
    operands = len(arrays)

    def body(*refs):
        kernel(*refs[:operands], *refs[operands + len(later) :])

    return pl.pallas_call(
        body,
        out_shape=[pltpu.VMEM(shape, dtype) for shape, dtype in outs],
        in_specs=[pl.BlockSpec(memory_space=pltpu.HBM)] * (operands + len(later)),
        out_specs=whole(len(outs)),
        scratch_shapes=scratch,
        compiler_params=pltpu.CompilerParams(vmem_limit_bytes=8 << 20),
        cost_estimate=pl.CostEstimate(flops=0, bytes_accessed=0, transcendentals=0),
    )(*in_hbm(arrays), *in_hbm(later))


def assemble(pairs, counts, rows, held):
    c = lax.axis_index("adapter")
    first = 0
    for pair, chips in zip(pairs, counts):
        depth = pair[0].shape[1]
        for chip in range(chips):
            for k in range(CHUNKS):
                at = (chip * CHUNKS + k) * rows
                for ref, core in zip(pair, (c, 1 - c)):
                    row = pl.multiple_of(first + core * rows, rows)
                    held[pl.ds(row, rows), k * depth : (k + 1) * depth] = ref[at : at + rows, :]
            first += 2 * rows


def tile_width(width):
    return 768 if width % 768 == 0 else width


def multiply(held, weights, at):
    total, first = 0.0, 0
    for w in weights:
        columns = held[:, first : first + w.shape[0]]
        total += jnp.dot(columns, w[:, at], preferred_element_type=jnp.float32)
        first += w.shape[0]
    return total


def finish_kernel(n, rows, groups, *refs):
    near_base, mid_base, far_base, late_rows, mine, others, weight, own, other, up_ref = refs[:10]
    adapters_ref, live_ref, out_ref, held, shrink, far_rows, block, adapters, live, sems, small_sems = refs[10:]
    lookups = [
        pltpu.make_async_copy(source, to, small_sems.at[k])
        for k, (source, to) in enumerate(((adapters_ref, adapters), (live_ref, live)))
    ]
    for lookup in lookups:
        lookup.start()
    c = lax.axis_index("adapter")
    chip_rows, rank = 2 * rows, up_ref.shape[1]
    tiles, _, columns = block.shape
    _, mid, far, _ = (len(group) for group in groups)
    assemble([(mine, others)], [1], rows, held)
    assemble_core(late_rows, far, rows, held, mid, chip_rows)
    for t in range(n):
        i, k = t % (n // 2), t // (n // 2)
        for ref, core in ((own, c), (other, 1 - c)):
            part = ref[i * rows : (i + 1) * rows, k * rank : (k + 1) * rank]
            shrink[t, pl.ds(pl.multiple_of(core * rows, rows), rows), :] = part.astype(jnp.bfloat16)
    for lookup in lookups:
        lookup.wait()
    early = [(base, i) for base, group in ((near_base, groups[0]), (mid_base, groups[1])) for i in range(len(group))]
    sources = [distance for group in groups for distance in group]
    copies = []

    def put(j, which, value_of):
        at = slice(j * columns, (j + 1) * columns)
        for i in which:
            first = chip_at(sources[i], n) * chip_rows
            of_block = first // BLOCK
            delta = jnp.dot(
                shrink[chip_at(sources[i], n)],
                up_ref[adapters[of_block], :, at],
                preferred_element_type=jnp.float32,
            )
            index = lax.broadcasted_iota(jnp.int32, delta.shape, 0) + (first - of_block * BLOCK)
            value = jnp.where(index < live[of_block], value_of(i, at) + delta, 0.0)
            block[j, i * chip_rows : (i + 1) * chip_rows, :] = value.astype(out_ref.dtype)

    def send(j, which):
        for i in which:
            first = pl.multiple_of(chip_at(sources[i], n) * chip_rows, chip_rows)
            copies.append(
                pltpu.make_async_copy(
                    block.at[j, pl.ds(i * chip_rows, chip_rows), :],
                    out_ref.at[pl.ds(first, chip_rows), pl.ds(j * columns, columns)],
                    sems.at[j, i],
                )
            )
            copies[-1].start()

    def early_value(i, at):
        base, k = early[i]
        return base[k * chip_rows : (k + 1) * chip_rows, at]

    for j in range(tiles):
        at = slice(j * columns, (j + 1) * columns)
        tile = multiply(held, [weight], at)
        interleave(rows, far, tile[chip_rows : chip_rows + far * rows], far_base[:, at], far_rows, slice(0, columns))

        def value_of(i, at, tile=tile):
            if i < len(early):
                return early_value(i, at)
            k = i - len(early)
            return far_rows[k * chip_rows : (k + 1) * chip_rows, :] if k < far else tile[:chip_rows]

        for i in range(n):
            put(j, [i], value_of)
            send(j, [i])
    for copy in copies:
        copy.wait()


def finish(n, rows, groups, lookups, bases, late, weight, sums, up):
    (rank, width), depth = up.shape[1:], weight.shape[0]
    total, columns = 2 * n * rows, tile_width(width)
    arrays = [*bases, *late, weight, *sums, up]
    far = len(groups[2])
    held = full_rows((2 + far) * rows)
    return pl.pallas_call(
        functools.partial(finish_kernel, n, rows, groups),
        out_shape=jax.ShapeDtypeStruct((total, width), jnp.bfloat16),
        in_specs=whole(len(arrays)) + [pl.BlockSpec(memory_space=pl.ANY)] * len(lookups),
        out_specs=pl.BlockSpec(memory_space=pl.ANY),
        scratch_shapes=[
            pltpu.VMEM((held, depth), jnp.bfloat16),
            pltpu.VMEM((n, 2 * rows, rank), jnp.bfloat16),
            pltpu.VMEM((2 * far * rows, columns), jnp.float32),
            pltpu.VMEM((width // columns, total, columns), jnp.bfloat16),
            *(pltpu.SMEM(x.shape, x.dtype) for x in lookups),
            pltpu.SemaphoreType.DMA((width // columns, n)),
            pltpu.SemaphoreType.DMA((len(lookups),)),
        ],
        compiler_params=pltpu.CompilerParams(vmem_limit_bytes=10 << 20),
        cost_estimate=pl.CostEstimate(
            flops=2 * held * depth * width, bytes_accessed=2 * total * width, transcendentals=0
        ),
    )(*in_vmem(arrays), *lookups)


def on_device(n, tokens, weight, down, up, adapter_per_block, rows_per_block):
    rows, features = tokens.shape
    depth = features // CHUNKS
    held, width, rank = down.shape
    last = n // 2
    adapters = adapter_per_block[:, 0]
    window = Window(n, width, depth)
    near, mid, far = ([d for hop in hops for d in hop_distances(hop, n)] for hops in ((0, 1), range(2, last - 1), [last - 1]))
    half = (n // 2 * rows, 2 * rank)
    sums = [(half, jnp.float32), (half, jnp.bfloat16)]

    (behind,), (ahead,) = ring_hop([tokens], [tokens], n)
    ends = far + [last]
    bf16 = jnp.bfloat16
    factor, *sends = prepare(
        functools.partial(prepare_kernel, n, window, ends),
        [tokens, jnp.swapaxes(down, 1, 2)],
        [weight, up],
        [((held, rank, window.size), bf16)] + [((rows, window.size), bf16)] * len(ends),
        [
            pltpu.VMEM((held, rank, width), down.dtype),
            pltpu.SemaphoreType.DMA((1 + len(ends),)),
        ],
    )
    received = [lax.ppermute(x, AXES, ring_perm(n, d)) for d, x in zip(ends, sends)]
    come_from = [-d for d in far] + [last]
    piece = ((rows, depth), bf16)
    near_rows, *chunks = call(
        near_kernel,
        [tokens, behind, ahead, factor],
        received,
        [((len(near) * CHUNKS * rows + rank, depth), bf16)] + [piece] * (2 * CHUNKS),
    )

    up_way, down_way = chunks[:CHUNKS], chunks[CHUNKS:]
    near_swapped = swap_cores(near_rows, n)
    own = len(near) * rows
    (mine,) = product(functools.partial(core_kernel, rows), [near_rows], weight, [], own, [own])
    (up,) = call(cast_kernel, [up], [mine], [(up.shape, bf16)])
    arrived = []
    for _ in range(2, last - 1):
        up_way, down_way = ring_hop(up_way, down_way, n)
        arrived += up_way + down_way
    (mid_rows,) = join(arrived, [mine, up])

    total, rounded = call(
        functools.partial(partial_kernel, n, window, [near, mid], come_from),
        [near_rows, mid_rows, *received, factor, near_swapped],
        [],
        sums,
        [
            pltpu.SMEM(adapters.shape, jnp.int32),
            pltpu.VMEM((n * rows, window.size), bf16),
            pltpu.VMEM((2 * held, n * rows, rank), jnp.float32),
            pltpu.VMEM((n, rows, rank), jnp.float32),
            pltpu.SemaphoreType.DMA,
        ],
        outside=[adapters],
    )
    near_base, mine = product(
        functools.partial(near_base_kernel, rows, len(near), len(mid)),
        [near_swapped, mine, mid_rows],
        weight,
        [rounded],
        own + len(mid) * rows,
        [2 * own, len(mid) * rows],
    )
    total, rounded = call(add_kernel, [total, lax.ppermute(rounded, AXES, y_perm(n))], [], sums)
    up_way, down_way = ring_hop(up_way, down_way, n)
    late_rows, turned = join([mid_rows, *up_way, *down_way], [rounded, near_base], 1)

    late_swapped = swap_cores(late_rows, n)
    late = len(mid) + len(far)
    mid_base, far_base = product(
        functools.partial(late_base_kernel, rows, len(mid), len(far)),
        [late_swapped, mine],
        weight,
        [],
        late * rows,
        [2 * len(mid) * rows, len(far) * rows],
    )
    total, rounded = call(
        add_kernel,
        [total] + [lax.ppermute(rounded, AXES, z_perm(n, shift)) for shift in range(1, n // 2)],
        [mid_base],
        sums,
    )
    (last_rows,) = join([lax.ppermute(turned, AXES, ring_perm(n, 1, -1))], [rounded])
    last_pair = (last_rows, swap_cores(last_rows, n))

    return finish(
        n,
        rows,
        [near, mid, far, [last]],
        [adapters, rows_per_block],
        [near_base, mid_base, far_base],
        [late_rows, *last_pair],
        weight,
        [total, swap_cores(rounded, n)],
        up,
    )


def solution(mesh):
    placed = (
        P(("groups", "seq", "adapter"), None),
        P(None, ("seq", "adapter")),
        P(("groups", "adapter"), "seq", None),
        P("groups", None, ("seq", "adapter")),
        P("groups", None),
        P("groups"),
    )
    return jax.shard_map(
        functools.partial(on_device, mesh.shape["seq"]),
        mesh=mesh,
        in_specs=placed,
        out_specs=P("groups", ("seq", "adapter")),
        check_vma=False,
    )
```

```python
import functools

import jax
import jax.numpy as jnp
from jax import lax
from jax.experimental import pallas as pl
from jax.experimental.pallas import tpu as pltpu
from jax.sharding import PartitionSpec as P

BLOCK = 128
AXES = ("seq", "adapter")
CHUNKS = 2


def ring_perm(n, way, other_way=None):
    order = [2 * z for z in range(n // 2)] + [2 * z + 1 for z in reversed(range(n // 2))]
    ways = (way, way if other_way is None else other_way)
    return [(2 * s + c, 2 * order[(pos + ways[c]) % n] + c) for pos, s in enumerate(order) for c in range(2)]


def swap_cores(x, n):
    return lax.ppermute(x, AXES, [(2 * s + c, 2 * s + 1 - c) for s in range(n) for c in range(2)])


def chip_at(distance, n):
    s = lax.axis_index("seq")
    z = s >> 1
    pos = jnp.where(s & 1 == 0, z, n - 1 - z) + distance
    pos = jnp.where(pos >= n, pos - n, pos)
    pos = jnp.where(pos < 0, pos + n, pos)
    return jnp.where(pos < n // 2, 2 * pos, 2 * (n - 1 - pos) + 1)


def y_perm(n):
    return [(2 * s + c, 2 * (s ^ 1) + c) for s in range(n) for c in range(2)]


def z_perm(n, shift):
    nz = n // 2
    return [
        (2 * (2 * z + y) + c, 2 * (2 * ((z - shift) % nz) + y) + c)
        for z in range(nz)
        for y in range(2)
        for c in range(2)
    ]


def hop_distances(hop, n):
    if hop == 0:
        return [0]
    return [-hop, hop] if hop < n // 2 else [hop]


def ring_hop(up, down, n):
    return [lax.ppermute(x, AXES, ring_perm(n, 1)) for x in up], [lax.ppermute(x, AXES, ring_perm(n, -1)) for x in down]


def join_kernel(ways, *refs):
    count = len(refs) - 1 - ways
    pieces, out, on = refs[:count], refs[count], refs[count + 1 :]
    first = 0
    for piece in pieces:
        out[first : first + piece.shape[0], :] = piece[...]
        first += piece.shape[0]
    arrived = pieces[len(pieces) - 2 * CHUNKS :]
    if ways == 1:
        c = lax.axis_index("adapter")
        rows = arrived[0].shape[0]
        for core in range(2):

            @pl.when(c == core)
            def _():
                for i, piece in enumerate(arrived[core * CHUNKS : (core + 1) * CHUNKS]):
                    on[0][i * rows : (i + 1) * rows, :] = piece[...]


def join(pieces, after, ways=0):
    (rows, depth), dtype = pieces[-1].shape, pieces[-1].dtype
    on = [CHUNKS * rows] * ways
    outs = [((count, depth), dtype) for count in [sum(x.shape[0] for x in pieces), *on]]
    return call(functools.partial(join_kernel, ways), pieces, after, outs)


def whole(count):
    return [pl.BlockSpec(memory_space=pltpu.VMEM)] * count


def in_vmem(arrays):
    return [pltpu.with_memory_space_constraint(x, pltpu.VMEM) for x in arrays]


def call(kernel, arrays, after, outs, scratch=(), limit=8, flops=0, outside=()):
    operands = len(arrays) + len(outside)

    def body(*refs):
        kernel(*refs[:operands], *refs[operands + len(after) :])

    return pl.pallas_call(
        body,
        out_shape=[pltpu.VMEM(shape, dtype) for shape, dtype in outs],
        in_specs=whole(len(arrays)) + [pl.BlockSpec(memory_space=pl.ANY)] * (len(outside) + len(after)),
        out_specs=whole(len(outs)),
        scratch_shapes=list(scratch),
        compiler_params=pltpu.CompilerParams(vmem_limit_bytes=limit << 20),
        cost_estimate=pl.CostEstimate(flops=flops, bytes_accessed=0, transcendentals=0),
    )(*in_vmem(arrays), *outside, *after)


class Window:
    def __init__(self, n, width, depth):
        self.width, self.depth = width, depth
        self.size = -(-(width + max(s * width % 128 for s in range(n))) // 128) * 128
        for s in range(n):
            start = s * width // 128 * 128
            assert start // depth == (start + self.size - 1) // depth

    def start(self, chip):
        return (chip * self.width) >> 7 << 7

    def shift(self, chip):
        return chip * self.width - self.start(chip)


def near_kernel(tokens, behind, ahead, factor, out, *chunks):
    held, rank, size = factor.shape
    rows, depth = chunks[0].shape
    for i, ref in enumerate((tokens, behind, ahead)):
        for k in range(CHUNKS):
            piece = ref[:, k * depth : (k + 1) * depth]
            at = (i * CHUNKS + k) * rows
            out[at : at + rows, :] = piece
            if i:
                chunks[(i - 1) * CHUNKS + k][...] = piece
    first = 3 * CHUNKS * rows
    out[first:, :] = jnp.zeros((rank, depth), out.dtype)
    for index in range(held):
        out[first:, index * size : (index + 1) * size] = factor[index]


def pack(parts, out):
    chips, rows, rank = parts.shape
    for t in range(chips):
        i, k = t % (chips // 2), t // (chips // 2)
        out[i * rows : (i + 1) * rows, k * rank : (k + 1) * rank] = parts[t].astype(out.dtype)


def partial_kernel(n, window, groups, far, *refs):
    *pieces, factor, other, adapters_ref, total, rounded, adapters, x, products, parts, sem = refs
    lookup = pltpu.make_async_copy(adapters_ref, adapters, sem)
    lookup.start()
    pieces, received = pieces[: len(groups)], pieces[len(groups) :]
    s, c = lax.axis_index("seq"), lax.axis_index("adapter")
    rows, size = received[0].shape
    held, rank, _ = factor.shape
    start = window.start(s)
    chunk = jnp.where(start >= window.depth, 1, 0)
    inside = pl.multiple_of(start - chunk * window.depth, 128)
    order = []
    for piece, distances in zip(pieces, groups):
        for i, distance in enumerate(distances):
            row = pl.multiple_of((i * CHUNKS + chunk) * rows, rows)
            x[len(order) * rows : (len(order) + 1) * rows, :] = piece[pl.ds(row, rows), pl.ds(inside, size)]
            order.append(distance)
    for piece, distance in zip(received, far):
        x[len(order) * rows : (len(order) + 1) * rows, :] = piece[...]
        order.append(distance)
    below = other.shape[0] - rank
    for index in range(held):
        theirs = other[below:, index * size : (index + 1) * size]
        for core, weights in ((c, factor[index]), (1 - c, theirs)):
            products[core * held + index] = lax.dot_general(
                x[...], weights, (((1,), (1,)), ((), ())), preferred_element_type=jnp.float32
            )
    lookup.wait()
    for i, distance in enumerate(order):
        chip = chip_at(distance, n)
        parts[chip] = products[adapters[chip * 2 * rows // BLOCK], i * rows : (i + 1) * rows, :]
    pack(parts, total)
    rounded[...] = total[...].astype(jnp.bfloat16)


def add_kernel(total, *refs):
    *received, out, rounded = refs
    value = total[...]
    for x in received:
        value += x[...].astype(jnp.float32)
    out[...] = value
    rounded[...] = value.astype(jnp.bfloat16)


def prepare_kernel(n, window, distances, tokens, down_ref, factor, *refs):
    *sends, down, sems = refs
    copies = [pltpu.make_async_copy(down_ref, down, sems.at[0])]
    for k, (distance, send) in enumerate(zip(distances, sends)):
        start = pl.multiple_of(window.start(chip_at(distance, n)), 128)
        copies.append(pltpu.make_async_copy(tokens.at[:, pl.ds(start, window.size)], send, sems.at[1 + k]))
    for copy in copies:
        copy.start()
    copies[0].wait()
    zeros = jnp.zeros((down.shape[1], window.size - window.width), jnp.float32)
    for index in range(down.shape[0]):
        wide = jnp.concatenate([down[index], zeros], 1)
        factor[index] = pltpu.roll(wide, window.shift(lax.axis_index("seq")), 1).astype(jnp.bfloat16)
    for copy in copies[1:]:
        copy.wait()


def full_rows(rows):
    return max(rows, 128)


def assemble_core(ref, chips, rows, held, skip=0, first=0):
    depth = ref.shape[1]
    for i in range(chips):
        for k in range(CHUNKS):
            at = ((skip + i) * CHUNKS + k) * rows
            held[first + i * rows : first + (i + 1) * rows, k * depth : (k + 1) * depth] = ref[at : at + rows, :]


def interleave(rows, chips, mine, others, base, at):
    c = lax.axis_index("adapter")
    for i in range(chips):
        here = slice(i * rows, (i + 1) * rows)
        for core, value in ((c, mine[here]), (1 - c, others[here])):
            base[pl.ds(pl.multiple_of((2 * i + core) * rows, rows), rows), at] = value


def core_kernel(rows, ref, *refs):
    *weights, base, held = refs
    assemble_core(ref, base.shape[0] // rows, rows, held)
    columns = tile_width(base.shape[1])
    for j in range(0, base.shape[1], columns):
        at = slice(j, j + columns)
        base[:, at] = multiply(held, weights, at)[: base.shape[0]]


def near_base_kernel(rows, near, mid, swapped, mine, mid_rows, weight, base, mid_base, held):
    assemble_core(swapped, near, rows, held)
    assemble_core(mid_rows, mid, rows, held, 0, near * rows)
    columns = tile_width(base.shape[1])
    for j in range(0, base.shape[1], columns):
        at = slice(j, j + columns)
        tile = multiply(held, [weight], at)
        interleave(rows, near, mine[: near * rows, at], tile, base, at)
        mid_base[:, at] = tile[near * rows : (near + mid) * rows]


def late_base_kernel(rows, mid, far, swapped, mine, weight, base, far_base, held):
    assemble_core(swapped, mid + far, rows, held)
    columns = tile_width(base.shape[1])
    for j in range(0, base.shape[1], columns):
        at = slice(j, j + columns)
        tile = multiply(held, [weight], at)
        interleave(rows, mid, mine[:, at], tile, base, at)
        far_base[:, at] = tile[mid * rows : (mid + far) * rows]


def product(kernel, arrays, weight, after, total, outs):
    (depth, width), total = weight.shape, full_rows(total)
    return call(
        kernel,
        [*arrays, weight],
        after,
        [((rows, width), jnp.float32) for rows in outs],
        [pltpu.VMEM((total, depth), jnp.bfloat16)],
        limit=8 + (2 * total * depth >> 20),
        flops=2 * total * depth * width,
    )


def cast_kernel(source, out):
    out[...] = source[...].astype(out.dtype)


def in_hbm(arrays):
    return [pltpu.with_memory_space_constraint(x, pltpu.HBM) for x in arrays]


def prepare(kernel, arrays, later, outs, scratch):
    operands = len(arrays)

    def body(*refs):
        kernel(*refs[:operands], *refs[operands + len(later) :])

    return pl.pallas_call(
        body,
        out_shape=[pltpu.VMEM(shape, dtype) for shape, dtype in outs],
        in_specs=[pl.BlockSpec(memory_space=pltpu.HBM)] * (operands + len(later)),
        out_specs=whole(len(outs)),
        scratch_shapes=scratch,
        compiler_params=pltpu.CompilerParams(vmem_limit_bytes=8 << 20),
        cost_estimate=pl.CostEstimate(flops=0, bytes_accessed=0, transcendentals=0),
    )(*in_hbm(arrays), *in_hbm(later))


def assemble(pairs, counts, rows, held):
    c = lax.axis_index("adapter")
    first = 0
    for pair, chips in zip(pairs, counts):
        depth = pair[0].shape[1]
        for chip in range(chips):
            for k in range(CHUNKS):
                at = (chip * CHUNKS + k) * rows
                for ref, core in zip(pair, (c, 1 - c)):
                    row = pl.multiple_of(first + core * rows, rows)
                    held[pl.ds(row, rows), k * depth : (k + 1) * depth] = ref[at : at + rows, :]
            first += 2 * rows


def tile_width(width):
    return 768 if width % 768 == 0 else width


def multiply(held, weights, at):
    total, first = 0.0, 0
    for w in weights:
        columns = held[:, first : first + w.shape[0]]
        total += jnp.dot(columns, w[:, at], preferred_element_type=jnp.float32)
        first += w.shape[0]
    return total


def finish_kernel(n, rows, groups, *refs):
    near_base, mid_base, far_base, late_rows, mine, others, weight, own, other, up_ref = refs[:10]
    adapters_ref, live_ref, out_ref, held, shrink, far_rows, block, adapters, live, sems, small_sems = refs[10:]
    lookups = [
        pltpu.make_async_copy(source, to, small_sems.at[k])
        for k, (source, to) in enumerate(((adapters_ref, adapters), (live_ref, live)))
    ]
    for lookup in lookups:
        lookup.start()
    c = lax.axis_index("adapter")
    chip_rows, rank = 2 * rows, up_ref.shape[1]
    tiles, _, columns = block.shape
    _, mid, far, _ = (len(group) for group in groups)
    assemble([(mine, others)], [1], rows, held)
    assemble_core(late_rows, far, rows, held, mid, chip_rows)
    for t in range(n):
        i, k = t % (n // 2), t // (n // 2)
        for ref, core in ((own, c), (other, 1 - c)):
            part = ref[i * rows : (i + 1) * rows, k * rank : (k + 1) * rank]
            shrink[t, pl.ds(pl.multiple_of(core * rows, rows), rows), :] = part.astype(jnp.bfloat16)
    for lookup in lookups:
        lookup.wait()
    early = [(base, i) for base, group in ((near_base, groups[0]), (mid_base, groups[1])) for i in range(len(group))]
    sources = [distance for group in groups for distance in group]
    copies = []

    def put(j, which, value_of):
        at = slice(j * columns, (j + 1) * columns)
        for i in which:
            first = chip_at(sources[i], n) * chip_rows
            of_block = first // BLOCK
            delta = jnp.dot(
                shrink[chip_at(sources[i], n)],
                up_ref[adapters[of_block], :, at],
                preferred_element_type=jnp.float32,
            )
            index = lax.broadcasted_iota(jnp.int32, delta.shape, 0) + (first - of_block * BLOCK)
            value = jnp.where(index < live[of_block], value_of(i, at) + delta, 0.0)
            block[j, i * chip_rows : (i + 1) * chip_rows, :] = value.astype(out_ref.dtype)

    def send(j, which):
        for i in which:
            first = pl.multiple_of(chip_at(sources[i], n) * chip_rows, chip_rows)
            copies.append(
                pltpu.make_async_copy(
                    block.at[j, pl.ds(i * chip_rows, chip_rows), :],
                    out_ref.at[pl.ds(first, chip_rows), pl.ds(j * columns, columns)],
                    sems.at[j, i],
                )
            )
            copies[-1].start()

    def early_value(i, at):
        base, k = early[i]
        return base[k * chip_rows : (k + 1) * chip_rows, at]

    for j in range(tiles):
        at = slice(j * columns, (j + 1) * columns)
        tile = multiply(held, [weight], at)
        interleave(rows, far, tile[chip_rows : chip_rows + far * rows], far_base[:, at], far_rows, slice(0, columns))

        def value_of(i, at, tile=tile):
            if i < len(early):
                return early_value(i, at)
            k = i - len(early)
            return far_rows[k * chip_rows : (k + 1) * chip_rows, :] if k < far else tile[:chip_rows]

        for i in range(n):
            put(j, [i], value_of)
            send(j, [i])
    for copy in copies:
        copy.wait()


def finish(n, rows, groups, lookups, bases, late, weight, sums, up):
    (rank, width), depth = up.shape[1:], weight.shape[0]
    total, columns = 2 * n * rows, 256 if width % 256 == 0 else width
    arrays = [*bases, *late, weight, *sums, up]
    far = len(groups[2])
    held = full_rows((2 + far) * rows)
    return pl.pallas_call(
        functools.partial(finish_kernel, n, rows, groups),
        out_shape=jax.ShapeDtypeStruct((total, width), jnp.bfloat16),
        in_specs=whole(len(arrays)) + [pl.BlockSpec(memory_space=pl.ANY)] * len(lookups),
        out_specs=pl.BlockSpec(memory_space=pl.ANY),
        scratch_shapes=[
            pltpu.VMEM((held, depth), jnp.bfloat16),
            pltpu.VMEM((n, 2 * rows, rank), jnp.bfloat16),
            pltpu.VMEM((2 * far * rows, columns), jnp.float32),
            pltpu.VMEM((width // columns, total, columns), jnp.bfloat16),
            *(pltpu.SMEM(x.shape, x.dtype) for x in lookups),
            pltpu.SemaphoreType.DMA((width // columns, n)),
            pltpu.SemaphoreType.DMA((len(lookups),)),
        ],
        compiler_params=pltpu.CompilerParams(vmem_limit_bytes=10 << 20),
        cost_estimate=pl.CostEstimate(
            flops=2 * held * depth * width, bytes_accessed=2 * total * width, transcendentals=0
        ),
    )(*in_vmem(arrays), *lookups)


def on_device(n, tokens, weight, down, up, adapter_per_block, rows_per_block):
    rows, features = tokens.shape
    depth = features // CHUNKS
    held, width, rank = down.shape
    last = n // 2
    adapters = adapter_per_block[:, 0]
    window = Window(n, width, depth)
    near, mid, far = ([d for hop in hops for d in hop_distances(hop, n)] for hops in ((0, 1), range(2, last - 1), [last - 1]))
    half = (n // 2 * rows, 2 * rank)
    sums = [(half, jnp.float32), (half, jnp.bfloat16)]

    (behind,), (ahead,) = ring_hop([tokens], [tokens], n)
    ends = far + [last]
    bf16 = jnp.bfloat16
    factor, *sends = prepare(
        functools.partial(prepare_kernel, n, window, ends),
        [tokens, jnp.swapaxes(down, 1, 2)],
        [weight, up],
        [((held, rank, window.size), bf16)] + [((rows, window.size), bf16)] * len(ends),
        [
            pltpu.VMEM((held, rank, width), down.dtype),
            pltpu.SemaphoreType.DMA((1 + len(ends),)),
        ],
    )
    received = [lax.ppermute(x, AXES, ring_perm(n, d)) for d, x in zip(ends, sends)]
    come_from = [-d for d in far] + [last]
    piece = ((rows, depth), bf16)
    near_rows, *chunks = call(
        near_kernel,
        [tokens, behind, ahead, factor],
        received,
        [((len(near) * CHUNKS * rows + rank, depth), bf16)] + [piece] * (2 * CHUNKS),
    )

    up_way, down_way = chunks[:CHUNKS], chunks[CHUNKS:]
    near_swapped = swap_cores(near_rows, n)
    own = len(near) * rows
    (mine,) = product(functools.partial(core_kernel, rows), [near_rows], weight, [], own, [own])
    (up,) = call(cast_kernel, [up], [mine], [(up.shape, bf16)])
    arrived = []
    for _ in range(2, last - 1):
        up_way, down_way = ring_hop(up_way, down_way, n)
        arrived += up_way + down_way
    (mid_rows,) = join(arrived, [mine, up])

    total, rounded = call(
        functools.partial(partial_kernel, n, window, [near, mid], come_from),
        [near_rows, mid_rows, *received, factor, near_swapped],
        [],
        sums,
        [
            pltpu.SMEM(adapters.shape, jnp.int32),
            pltpu.VMEM((n * rows, window.size), bf16),
            pltpu.VMEM((2 * held, n * rows, rank), jnp.float32),
            pltpu.VMEM((n, rows, rank), jnp.float32),
            pltpu.SemaphoreType.DMA,
        ],
        outside=[adapters],
    )
    near_base, mine = product(
        functools.partial(near_base_kernel, rows, len(near), len(mid)),
        [near_swapped, mine, mid_rows],
        weight,
        [rounded],
        own + len(mid) * rows,
        [2 * own, len(mid) * rows],
    )
    total, rounded = call(add_kernel, [total, lax.ppermute(rounded, AXES, y_perm(n))], [], sums)
    up_way, down_way = ring_hop(up_way, down_way, n)
    late_rows, turned = join([mid_rows, *up_way, *down_way], [rounded, near_base], 1)

    late_swapped = swap_cores(late_rows, n)
    late = len(mid) + len(far)
    mid_base, far_base = product(
        functools.partial(late_base_kernel, rows, len(mid), len(far)),
        [late_swapped, mine],
        weight,
        [],
        late * rows,
        [2 * len(mid) * rows, len(far) * rows],
    )
    total, rounded = call(
        add_kernel,
        [total] + [lax.ppermute(rounded, AXES, z_perm(n, shift)) for shift in range(1, n // 2)],
        [mid_base],
        sums,
    )
    (last_rows,) = join([lax.ppermute(turned, AXES, ring_perm(n, 1, -1))], [rounded])
    last_pair = (last_rows, swap_cores(last_rows, n))

    return finish(
        n,
        rows,
        [near, mid, far, [last]],
        [adapters, rows_per_block],
        [near_base, mid_base, far_base],
        [late_rows, *last_pair],
        weight,
        [total, swap_cores(rounded, n)],
        up,
    )


def solution(mesh):
    placed = (
        P(("groups", "seq", "adapter"), None),
        P(None, ("seq", "adapter")),
        P(("groups", "adapter"), "seq", None),
        P("groups", None, ("seq", "adapter")),
        P("groups", None),
        P("groups"),
    )
    return jax.shard_map(
        functools.partial(on_device, mesh.shape["seq"]),
        mesh=mesh,
        in_specs=placed,
        out_specs=P("groups", ("seq", "adapter")),
        check_vma=False,
    )
```
